128 devices in a mesh: chan: 4 (over z), pix: 32 (over x, y, core).
Axes of the slice: x: 4, y: 4, z: 4, core: 2. Of those that a mesh axis runs over, the one named last changes fastest.
Arguments:
- feat_one: bfloat16 [196, 768, 256], P('chan', 'pix'), may hold values from -6 to 6
- feat_two: bfloat16 [196, 768, 256], P('chan', 'pix'), may hold values from -6 to 6
- up_flow: bfloat16 [2, 768, 256], P(None, 'pix'), may hold values from 0.049804688 to 0.94921875
- up_feat: bfloat16 [2, 768, 256], P(None, 'pix', 'chan'), may hold values from -6 to 6
- target_flow: float32 [2, 768, 256], P(None, 'pix', 'chan'), may hold values from -6 to 6
- valid_mask: int32 [768, 256], P('pix', 'chan'), may hold values from 0 to 1, as said below
- conv_one: bfloat16 [9, 128, 281], replicated, may hold values from -0.125 to 0.125
- conv_two: bfloat16 [9, 128, 409], replicated, may hold values from -0.09375 to 0.09375
- conv_three: bfloat16 [9, 96, 537], replicated, may hold values from -0.078125 to 0.078125
- conv_four: bfloat16 [9, 64, 633], replicated, may hold values from -0.078125 to 0.078125
- conv_five: bfloat16 [9, 32, 697], replicated, may hold values from -0.078125 to 0.078125
- flow_head: bfloat16 [9, 2, 729], replicated, may hold values from -0.15625 to 0.15625
- bias_one: float32 [128], replicated, may hold values from -3 to 3
- bias_two: float32 [128], replicated, may hold values from -3 to 3
- bias_three: float32 [96], replicated, may hold values from -3 to 3
- bias_four: float32 [64], replicated, may hold values from -3 to 3
- bias_five: float32 [32], replicated, may hold values from -3 to 3
- bias_head: float32 [2], replicated, may hold values from -3 to 3
Outputs:
- flow_out: float32 [2, 768, 256], P(None, 'pix', 'chan')
- metrics: float32 [3], replicated
- grad_feat_one: float32 [196, 768, 256], P('chan', 'pix')
- grad_feat_two: float32 [196, 768, 256], P('chan', 'pix')
- grad_up_flow: float32 [2, 768, 256], P(None, 'pix', 'chan')
- grad_up_feat: float32 [2, 768, 256], P(None, 'pix', 'chan')
- grad_conv_one: float32 [9, 128, 281], replicated
- grad_conv_two: float32 [9, 128, 409], replicated
- grad_conv_three: float32 [9, 96, 537], replicated
- grad_conv_four: float32 [9, 64, 633], replicated
- grad_conv_five: float32 [9, 32, 697], replicated
- grad_flow_head: float32 [9, 2, 729], replicated
- grad_bias_one: float32 [128], replicated
- grad_bias_two: float32 [128], replicated
- grad_bias_three: float32 [96], replicated
- grad_bias_four: float32 [64], replicated
- grad_bias_five: float32 [32], replicated
- grad_bias_head: float32 [2], replicated
The draws below stay inside these ranges and needn't reach their ends.
Inputs may be any that keep to these rules, and one draw needn't show every extreme that they name: In each aligned group of 8 rows valid_mask is 1 on the columns below a width of 64 to 256 and 0 beyond; the first group is valid on all 256 columns.
All inputs are finite; a program needn't handle non-finite values.
Results may differ from the reference program's by a relative error of at most 0.015.
Values may be sent and summed in bfloat16 or wider, within the bound.
No kernel may reach another device: no remote copies, remote signals or barrier semaphores. Data moves between devices by JAX's collectives and lax.ppermute only.
A program may use at most 320 MiB of HBM per device.

```python
import jax
import jax.numpy as jnp
from jax import lax

W = 256
CH = 196
MD = 4
C1 = 128
C2 = 128
C3 = 96
C4 = 64
C5 = 32
CIN0 = 281
H = 768


def draw_valid_mask(key, part):
    key = jax.random.fold_in(key, 11)
    groups = H // 8
    widths = jax.random.randint(key, (groups,), W // 4, W + 1)
    widths = jnp.where(jnp.arange(groups) == 0, W, widths)
    columns = jnp.arange(W)
    grid = (columns[None, :] < widths[:, None]).astype(jnp.int32)
    return jnp.repeat(grid, 8, axis=0)


def shard_levels(own_key, extent, cuts, least, largest):
    factor_of, own = 1.0, jax.random.fold_in(own_key, 6)
    for dim, shards_of in cuts:
        draws = jnp.exp(jax.random.uniform(jax.random.fold_in(own, dim), (shards_of,), jnp.float32, least / len(cuts), largest / len(cuts)))
        factor_of = factor_of * jnp.repeat(draws, extent[dim] // shards_of).reshape([-1 if axis == dim else 1 for axis in range(len(extent))])
    return factor_of


def normal_values(rng, dims, scale, limit, cuts=(), kind=jnp.bfloat16):
    array = jax.random.normal(rng, dims, jnp.float32) * scale
    if len(cuts) > 0:
        array = shard_levels(rng, dims, cuts, -0.22, 0.18) * array
    return jnp.clip(array, min=-limit, max=limit).astype(kind)


def setup_inputs(seed: int = 0) -> dict:
    key_list = jax.random.split(jax.random.key(seed), 19)
    return {
        "feat_one": normal_values(key_list[0], (CH, H, W), 1.0, 6.0, ((0, 4), (1, 32))),
        "feat_two": normal_values(key_list[1], (CH, H, W), 1.0, 6.0, ((0, 4), (1, 32))),
        "up_flow": jnp.clip(0.049804688 + 0.89941406 * jax.random.uniform(key_list[2], (2, H, W), jnp.float32) ** shard_levels(key_list[2], (2, H, W), ((1, 32),), -0.2, 0.2), 0.049804688, 0.94921875).astype(jnp.bfloat16),
        "up_feat": normal_values(key_list[3], (2, H, W), 1.0, 6.0, ((1, 32), (2, 4))),
        "target_flow": normal_values(key_list[4], (2, H, W), 1.0, 6.0, ((1, 32), (2, 4)), jnp.float32),
        "valid_mask": draw_valid_mask(jax.random.fold_in(key_list[18], 71), 0),
        "conv_one": normal_values(key_list[6], (9, C1, CIN0), (9 * CIN0) ** -0.5, 0.125),
        "conv_two": normal_values(key_list[7], (9, C2, CIN0 + C1), (9 * (CIN0 + C1)) ** -0.5, 0.09375),
        "conv_three": normal_values(key_list[8], (9, C3, CIN0 + C1 + C2), (9 * (CIN0 + C1 + C2)) ** -0.5, 0.078125),
        "conv_four": normal_values(key_list[9], (9, C4, CIN0 + C1 + C2 + C3), (9 * (CIN0 + C1 + C2 + C3)) ** -0.5, 0.078125),
        "conv_five": normal_values(key_list[10], (9, C5, CIN0 + C1 + C2 + C3 + C4), (9 * (CIN0 + C1 + C2 + C3 + C4)) ** -0.5, 0.078125),
        "flow_head": normal_values(key_list[11], (9, 2, CIN0 + C1 + C2 + C3 + C4 + C5), (9 * (CIN0 + C1 + C2 + C3 + C4 + C5) // 4) ** -0.5, 0.15625),
        "bias_one": normal_values(key_list[12], (C1,), 0.5, 3.0, (), jnp.float32),
        "bias_two": normal_values(key_list[13], (C2,), 0.5, 3.0, (), jnp.float32),
        "bias_three": normal_values(key_list[14], (C3,), 0.5, 3.0, (), jnp.float32),
        "bias_four": normal_values(key_list[15], (C4,), 0.5, 3.0, (), jnp.float32),
        "bias_five": normal_values(key_list[16], (C5,), 0.5, 3.0, (), jnp.float32),
        "bias_head": normal_values(key_list[17], (2,), 1.0, 3.0, (), jnp.float32),
    }


@jax.custom_vjp
def low(v):
    return lax.optimization_barrier(v.astype(jnp.bfloat16)).astype(jnp.float32)

@jax.custom_vjp
def low_back(v):
    return v

def low_keep(v):
    return (low(v), None)

def low_pass(kept, grad):
    return (grad,)

def back_keep(v):
    return (v, None)

def back_low(kept, grad):
    return (low(grad),)
low.defvjp(low_keep, low_pass)
low_back.defvjp(back_keep, back_low)

def warp(feature, flow):
    across = flow[0]
    downward = flow[1]
    padded = jnp.pad(feature, ((0, 0), (0, 1), (0, 1)))
    upper_row = (1.0 - across) * padded[:, :-1, :-1] + across * padded[:, :-1, 1:]
    lower_row = (1.0 - across) * padded[:, 1:, :-1] + across * padded[:, 1:, 1:]
    return (1.0 - downward) * upper_row + downward * lower_row

def correlate(first, warped):
    span = 2 * MD + 1
    padded = jnp.pad(warped, ((0, 0), (MD, MD), (MD, MD)))
    zero_index = jnp.zeros((), jnp.int32)

    def one_shift(index):
        row_off = (index // span).astype(jnp.int32)
        col_off = (index % span).astype(jnp.int32)
        window = lax.dynamic_slice(padded, (zero_index, row_off, col_off), first.shape)
        return lax.optimization_barrier(jnp.sum(first * window, axis=0)) / CH ** 0.5
    return lax.map(jax.checkpoint(one_shift), jnp.arange(span * span, dtype=jnp.int32))

def conv_sum(pieces, weight, bias):
    outputs = weight.shape[1]
    kernel = weight.reshape(3, 3, outputs, weight.shape[2]).transpose(2, 3, 0, 1)
    total = jnp.zeros((outputs,) + pieces[0].shape[1:], jnp.float32) + bias[:, None, None]
    start = 0
    for piece in pieces:
        depth = piece.shape[0]
        total = total + lax.conv_general_dilated(piece[None], kernel[:, start:start + depth], (1, 1), ((1, 1), (1, 1)), precision=lax.Precision.HIGHEST)[0]
        start += depth
    return total

def forward(first, second, flow_in, feat_in, weights, biases, target, mask):
    warped = low(warp(second, flow_in))
    cost = low(low_back(correlate(first, warped)))
    pieces = [jnp.concatenate([cost, low_back(first), flow_in, feat_in], axis=0)]
    for layer in range(5):
        pre = low_back(conv_sum(pieces[::-1], weights[layer], biases[layer]))
        pieces.append(low(jax.nn.silu(pre)))
    flow = low_back(conv_sum(pieces[::-1], weights[5], biases[5]))
    diff = flow - target
    error = jnp.sqrt(diff[0] * diff[0] + diff[1] * diff[1] + 1.0)
    loss = jnp.sum(mask * (error - 1.0))
    outliers = jnp.sum(mask * jax.nn.sigmoid(4.0 * (error - 2.0)))
    return (loss, (flow, outliers, jnp.sum(mask)))

def reference(feat_one, feat_two, up_flow, up_feat, target_flow, valid_mask, conv_one, conv_two, conv_three, conv_four, conv_five, flow_head, bias_one, bias_two, bias_three, bias_four, bias_five, bias_head):
    weights = [w.astype(jnp.float32) for w in (conv_one, conv_two, conv_three, conv_four, conv_five, flow_head)]
    biases = [b.astype(jnp.float32) for b in (bias_one, bias_two, bias_three, bias_four, bias_five, bias_head)]
    mask = valid_mask.astype(jnp.float32)
    target = target_flow.astype(jnp.float32)

    def loss_of(first, second, flow_in, feat_in, wts, bss):
        return forward(first, second, flow_in, feat_in, wts, bss, target, mask)
    primals = (feat_one.astype(jnp.float32), feat_two.astype(jnp.float32), up_flow.astype(jnp.float32), up_feat.astype(jnp.float32), weights, biases)
    loss, pullback, extras = jax.vjp(loss_of, *primals, has_aux=True)
    flow, outliers, count = extras
    grads = pullback(jnp.ones_like(loss))
    gfirst, gsecond, gflow, gfeat, gweights, gbiases = grads
    metrics = jnp.stack([loss, outliers, count])
    return (flow, metrics, gfirst, gsecond, gflow, gfeat, gweights[0], gweights[1], gweights[2], gweights[3], gweights[4], gweights[5], gbiases[0], gbiases[1], gbiases[2], gbiases[3], gbiases[4], gbiases[5])
```

```python
import jax
import jax.numpy as jnp
import numpy as np
from jax import lax
from jax.experimental import pallas as pl
from jax.experimental.pallas import tpu as pltpu
from jax.sharding import PartitionSpec as P

CH = 196
MD = 4
CH_SLOT = 49
OUTS = (128, 128, 96, 64, 32, 2)
ROW0 = (0, 128, 256, 384, 448, 480)
DEPTH = (281, 409, 537, 633, 697, 729)


def start_lane(channel):
    if channel < 81:
        dy, dx = divmod(channel, 9)
        if dy < 4:
            return 0, 64 * dy + 49 + dx
        if dy < 8:
            if dx < 6:
                return 0, 64 * (dy - 4) + 58 + dx
            return 1, 3 * (dy - 4) + dx - 6
        return 1, 12 + dx
    if channel < 277:
        slot, inner = divmod(channel - 81, CH_SLOT)
        return 0, 64 * slot + inner
    return 1, 21 + channel - 277


def lane_maps():
    wide = np.zeros((729, 768), np.float32)
    rest = np.zeros((3, 729, 128), np.float32)
    for c in range(729):
        if c < 32:
            wide[c, 704 + c] = 1
        elif c < 96:
            wide[c, 640 + c - 32] = 1
        elif c < 192:
            wide[c, 512 + c - 96] = 1
        elif c < 320:
            wide[c, 384 + c - 192] = 1
        elif c < 448:
            wide[c, 256 + c - 320] = 1
        else:
            block, lane = start_lane(c - 448)
            if block == 0:
                wide[c, lane] = 1
            else:
                for dx in range(3):
                    rest[dx, c, 32 * dx + lane] = 1
    return wide, rest


def gather_map():
    table = np.zeros((896, 768), np.float32)
    for c in range(281):
        block, lane = start_lane(c)
        table[256 * block + lane, 448 + c] = 1
    table[256 + 25, 729] = 1
    for i in range(128):
        table[384 + i, 320 + i] = 1
        table[512 + i, 192 + i] = 1
    for i in range(96):
        table[640 + i, 96 + i] = 1
        table[768 + i, (32 + i) if i < 64 else i - 64] = 1
    return table


def start_map():
    table = np.zeros((281, 384), np.float32)
    for c in range(281):
        block, lane = start_lane(c)
        table[c, 256 * block + lane] = 1
    return table

BF = jnp.bfloat16
F32 = jnp.float32
HALO = 12
PITCH = 96
ROWS = 24
COLS = 64
LEFT = 16
WROWS = ROWS + 2 * HALO
NPX = WROWS * PITCH
GUARD = 16
VMEM_MB = 62


def nt(a, b):
    return lax.dot_general(a, b, (((1,), (1,)), ((), ())), preferred_element_type=F32)


def nn(a, b):
    return lax.dot_general(a, b, (((1,), (0,)), ((), ())), preferred_element_type=F32)


def decode_kernel(
    xm_ref, xr_ref, w_ref, wr_ref,
    a_ref, g_ref, dm_ref, dr_ref, flow_ref, met_ref,
    xs, xq, sh, pre, sc, mk, sem,
):
    lane = lax.broadcasted_iota(jnp.int32, (PITCH, 128), 1)

    def rows(lo, hi, body):
        def step(i, carry):
            body(pl.multiple_of(i * PITCH, PITCH))
            return carry
        lax.fori_loop(lo, hi, step, 0)

    def shifted_store(dst, lanes, lo, hi):
        def body(p):
            for d in range(3):
                dst[d, pl.ds(p, PITCH), lanes] = sc[pl.ds(p + GUARD + d - 1, PITCH), :].astype(BF)
        rows(lo, hi, body)

    def chunked(lo, hi, count, body):
        size = (hi - lo) * PITCH // count

        def step(i, carry):
            body(pl.multiple_of(lo * PITCH + i * size, 16), size)
            return carry
        lax.fori_loop(0, count, step, 0)

    sc[pl.ds(0, GUARD), :] = jnp.zeros((GUARD, 128), F32)
    sc[pl.ds(GUARD + NPX, GUARD), :] = jnp.zeros((GUARD, 128), F32)

    def rest_in(p):
        value = xr_ref[pl.ds(p, PITCH), :].astype(F32)
        sc[pl.ds(p + GUARD, PITCH), :] = value
        mk[pl.ds(p, PITCH), :] = jnp.broadcast_to(value[:, 25:26], (PITCH, 128))
    rows(0, WROWS, rest_in)

    def rest_cat(p):
        low = sc[pl.ds(p + GUARD - 1, PITCH), :]
        mid = pltpu.roll(sc[pl.ds(p + GUARD, PITCH), :], 32, 1)
        high = pltpu.roll(sc[pl.ds(p + GUARD + 1, PITCH), :], 64, 1)
        xq[pl.ds(p, PITCH), :] = jnp.where(
            lane < 32, low, jnp.where(lane < 64, mid, jnp.where(lane < 96, high, 0.0))
        ).astype(BF)
    rows(0, WROWS, rest_cat)

    for half in range(2):
        lanes = slice(128 * half, 128 * half + 128)

        def main_in(p):
            sc[pl.ds(p + GUARD, PITCH), :] = xm_ref[pl.ds(p, PITCH), lanes].astype(F32)
        rows(0, WROWS, main_in)
        shifted_store(xs, lanes, 0, WROWS)

    def start_sums(p, size):
        total = None
        for dy in range(3):
            at = p + PITCH * (dy - 1)
            term = nt(xq[pl.ds(at, size), :], wr_ref[dy])
            total = term if total is None else total + term
            for dx in range(3):
                total = total + nt(xs[dx, pl.ds(at, size), :], w_ref[3 * dy + dx, :, 0:256])
        pre[pl.ds(p, size), :] = total
    chunked(1, WROWS - 1, 6, start_sums)

    first_lane = [0, 128, 256, 384, 384]
    part = [(0, 128), (0, 128), (0, 96), (0, 64), (64, 96)]
    for layer in range(5):
        block = slice(first_lane[layer], first_lane[layer] + 128)
        from_lane, to_lane = part[layer]
        inside = (lane >= from_lane) & (lane < to_lane)
        lo, hi = layer + 1, WROWS - layer - 1

        def activate(p, block=block, inside=inside):
            value = pre[pl.ds(p, PITCH), block]
            sig = 1.0 / (1.0 + jnp.exp(-value))
            keep = inside & (mk[pl.ds(p, PITCH), :] > 0.0)
            sc[pl.ds(p + GUARD, PITCH), :] = jnp.where(keep, value * sig, 0.0)
            slope = jnp.where(keep, sig * (1.0 + value * (1.0 - sig)), 0.0)
            pre[pl.ds(p, PITCH), block] = jnp.where(inside, slope, value)
        rows(lo, hi, activate)
        piece = min(layer, 3)

        def keep_core(p, layer=layer, piece=piece):
            value = sc[pl.ds(p + GUARD, PITCH), :].astype(BF)
            q = pl.multiple_of(p - HALO * PITCH, PITCH)
            lanes = slice(128 * piece, 128 * piece + 128)
            if layer == 4:
                a_ref[pl.ds(q, PITCH), lanes] = a_ref[pl.ds(q, PITCH), lanes] + value
            else:
                a_ref[pl.ds(q, PITCH), lanes] = value
        rows(HALO, HALO + ROWS, keep_core)
        shifted_store(sh, slice(128 * piece, 128 * piece + 128), lo, hi)
        out0 = min(128 * (layer + 1), 384)

        def add_sums(p, size, piece=piece, out0=out0):
            total = pre[pl.ds(p, size), out0:512]
            for dy in range(3):
                at = p + PITCH * (dy - 1)
                left = jnp.concatenate(
                    [sh[dx, pl.ds(at, size), 128 * piece : 128 * piece + 128] for dx in range(3)], axis=1
                )
                right = jnp.concatenate(
                    [w_ref[3 * dy + dx, out0:512, 256 + 128 * piece : 384 + 128 * piece] for dx in range(3)],
                    axis=1,
                )
                total = total + nt(left, right)
            pre[pl.ds(p, size), out0:512] = total
        chunked(lo + 1, hi - 1, 6, add_sums)

    is_flow = (lane >= 96) & (lane < 98)
    column = lax.broadcasted_iota(jnp.int32, (PITCH, 128), 0)
    core_column = (column >= LEFT) & (column < LEFT + COLS)
    met_ref[...] = jnp.zeros((3, PITCH, 128), F32)

    def loss(p):
        flow = pre[pl.ds(p, PITCH), 384:512]
        rest = xr_ref[pl.ds(p, PITCH), :].astype(F32)
        target = pltpu.roll(rest, 96 - 28, 1) + pltpu.roll(rest, 96 - 30, 1)
        diff = jnp.where(is_flow, flow - target, 0.0)
        square = diff * diff
        other = jnp.where(lane == 96, pltpu.roll(square, 127, 1), pltpu.roll(square, 1, 1))
        error = jnp.sqrt(square + other + 1.0)
        mask = jnp.broadcast_to(rest[:, 27:28], (PITCH, 128))
        sc[pl.ds(p + GUARD, PITCH), :] = jnp.where(is_flow, mask * diff / error, 0.0)
        return flow, mask, error

    def loss_rim(p):
        loss(p)

    def loss_core(p):
        flow, mask, error = loss(p)
        q = pl.multiple_of(p - HALO * PITCH, PITCH)
        flow_ref[pl.ds(q, PITCH), :] = flow
        mask = jnp.where(core_column, mask, 0.0)
        met_ref[0] += mask * (error - 1.0)
        met_ref[1] += mask / (1.0 + jnp.exp(-4.0 * (error - 2.0)))
        met_ref[2] += mask

    rows(6, HALO, loss_rim)
    rows(HALO, HALO + ROWS, loss_core)
    rows(HALO + ROWS, WROWS - 6, loss_rim)
    shifted_store(sh, slice(384, 512), 6, WROWS - 6)

    for layer in range(4, -1, -1):
        lo, hi = HALO - layer - 1, HALO + ROWS + layer + 1
        piece = min(layer, 3)
        out0 = min(128 * (layer + 1), 384)
        block = slice(first_lane[layer], first_lane[layer] + 128)
        from_lane, to_lane = part[layer]
        inside = (lane >= from_lane) & (lane < to_lane)
        c0 = 256 + 128 * piece

        def back(p, size, out0=out0, c0=c0):
            total = None
            for dy in range(3):
                at = p - PITCH * (dy - 1)
                left = jnp.concatenate([sh[2 - dx, pl.ds(at, size), out0:512] for dx in range(3)], axis=1)
                right = jnp.concatenate([w_ref[3 * dy + dx, out0:512, c0 : c0 + 128] for dx in range(3)], axis=0)
                term = nn(left, right)
                total = term if total is None else total + term
            dm_ref_f[pl.ds(p, size), :] = total
        dm_ref_f = mk
        chunked(lo, hi, 6, back)

        def slope(p, layer=layer, block=block, inside=inside):
            value = mk[pl.ds(p, PITCH), :] * pre[pl.ds(p, PITCH), block]
            if layer >= 3:
                old = sc[pl.ds(p + GUARD, PITCH), :]
                sc[pl.ds(p + GUARD, PITCH), :] = jnp.where(inside, value, old)
            else:
                sc[pl.ds(p + GUARD, PITCH), :] = value
        rows(lo, hi, slope)
        shifted_store(sh, slice(128 * piece, 128 * piece + 128), lo, hi)

    copy = pltpu.make_async_copy(sh.at[:, pl.ds((HALO - 1) * PITCH, (ROWS + 2) * PITCH), :], g_ref, sem)
    copy.start()

    def back_rest(p, size):
        total = None
        for dy in range(3):
            term = nn(sh[1, pl.ds(p - PITCH * (dy - 1), size), :], wr_ref[dy])
            total = term if total is None else total + term
        sc[pl.ds(p + GUARD, size), :] = total
    chunked(HALO, HALO + ROWS, 6, back_rest)

    def rest_out(p):
        q = pl.multiple_of(p - HALO * PITCH, PITCH)
        dr_ref[pl.ds(q, PITCH), :] = (
            sc[pl.ds(p + GUARD + 1, PITCH), :]
            + pltpu.roll(sc[pl.ds(p + GUARD, PITCH), :], 96, 1)
            + pltpu.roll(sc[pl.ds(p + GUARD - 1, PITCH), :], 64, 1)
        )
    rows(HALO, HALO + ROWS, rest_out)

    def back_main(p, size):
        total = None
        for dy in range(3):
            at = p - PITCH * (dy - 1)
            for dx in range(3):
                term = nn(sh[2 - dx, pl.ds(at, size), :], w_ref[3 * dy + dx, :, 0:256])
                total = term if total is None else total + term
        q = pl.multiple_of(p - HALO * PITCH, 16)
        dm_ref[pl.ds(q, size), :] = total.astype(BF)
    chunked(HALO, HALO + ROWS, 6, back_main)
    copy.wait()


def decode(xm, xr, w, wr):
    core = ROWS * PITCH
    vm = pl.BlockSpec(memory_space=pltpu.VMEM)
    return pl.pallas_call(
        decode_kernel,
        out_shape=(
            jax.ShapeDtypeStruct((core, 512), BF),
            jax.ShapeDtypeStruct((3, (ROWS + 2) * PITCH, 512), BF),
            jax.ShapeDtypeStruct((core, 256), BF),
            jax.ShapeDtypeStruct((core, 128), F32),
            jax.ShapeDtypeStruct((core, 128), F32),
            jax.ShapeDtypeStruct((3, PITCH, 128), F32),
        ),
        in_specs=[vm] * 4,
        out_specs=(vm, pl.BlockSpec(memory_space=pl.ANY), vm, vm, vm, vm),
        scratch_shapes=[
            pltpu.VMEM((3, NPX, 256), BF),
            pltpu.VMEM((NPX, 128), BF),
            pltpu.VMEM((3, NPX, 512), BF),
            pltpu.VMEM((NPX, 512), F32),
            pltpu.VMEM((NPX + 2 * GUARD, 128), F32),
            pltpu.VMEM((NPX, 128), F32),
            pltpu.SemaphoreType.DMA,
        ],
        compiler_params=pltpu.CompilerParams(vmem_limit_bytes=VMEM_MB * 2**20),
        name="decode",
    )(xm, xr, w, wr)

TILE_ROWS = 2048


def tn(a, b):
    return lax.dot_general(a, b, (((0,), (0,)), ((), ())), preferred_element_type=F32)


def wgrad_kernel(g_ref, xm_ref, xr_ref, a_ref, qp_ref, o_ref, b_ref, xp):
    column = lax.broadcasted_iota(jnp.int32, (PITCH, 768), 0)
    core = (column >= LEFT) & (column < LEFT + COLS)
    core = jnp.concatenate([core] * 4, axis=0)
    size = 4 * PITCH

    def gather(i, carry):
        at = pl.ds(pl.multiple_of(i * size, size), size)
        left = jnp.concatenate([xm_ref[at, :], xr_ref[at, :], a_ref[at, :]], axis=1)
        xp[at, :] = jnp.where(core, nn(left, qp_ref[...]), 0.0).astype(BF)
        return carry
    lax.fori_loop(0, ROWS // 4, gather, 0)

    for k in range(9):
        dy, dx = divmod(k, 3)
        at = pl.ds(PITCH * (2 - dy), ROWS * PITCH)
        base = TILE_ROWS * k
        value = tn(g_ref[2 - dx, at, 0:256], xp[:, 256:768])
        if k == 4:
            b_ref[0:256, :] = value[:, 384:512]
        low = value.astype(BF)
        for t in range(3):
            o_ref[base + 128 * t : base + 128 * t + 128, :] = low[0:128, 128 * t + 128 : 128 * t + 256]
        for t in range(4):
            o_ref[base + 384 + 128 * t : base + 512 + 128 * t, :] = low[128:256, 128 * t : 128 * t + 128]
        value = tn(g_ref[2 - dx, at, 256:512], xp[...])
        if k == 4:
            b_ref[256:512, :] = value[:, 640:768]
        low = value.astype(BF)
        for t in range(5):
            o_ref[base + 896 + 96 * t : base + 992 + 96 * t, :] = low[0:96, 128 * t + 128 : 128 * t + 256]
        for t in range(6):
            o_ref[base + 1376 + 112 * t : base + 1488 + 112 * t, :] = low[128:240, 128 * t : 128 * t + 128]


def wgrad(g, xm, xr, a, qp):
    vm = pl.BlockSpec(memory_space=pltpu.VMEM)
    return pl.pallas_call(
        wgrad_kernel,
        out_shape=(
            jax.ShapeDtypeStruct((9 * TILE_ROWS, 128), BF),
            jax.ShapeDtypeStruct((512, 128), F32),
        ),
        in_specs=[vm] * 5,
        out_specs=(vm, vm),
        scratch_shapes=[pltpu.VMEM((ROWS * PITCH, 768), BF)],
        compiler_params=pltpu.CompilerParams(vmem_limit_bytes=VMEM_MB * 2**20),
        name="wgrad",
    )(g, xm, xr, a, qp)


def unpack_kernel(s_ref, o1, o2, o3, o4, o5, o6):
    def tiles(base, height, count):
        return jnp.concatenate(
            [s_ref[base + height * t : base + height * (t + 1), :].astype(F32) for t in range(count)], axis=1
        )
    o1[0] = tiles(0, 128, 3)[:, 64 : 64 + 281]
    o2[0] = tiles(384, 128, 4)[:, 64 : 64 + 409]
    o3[0] = tiles(896, 96, 5)[:, 64 : 64 + 537]
    last = tiles(1376, 112, 6)
    o4[0] = last[0:64, 96:729]
    o5[0] = last[64:96, 32:729]
    o6[0] = last[96:98, 0:729]


def unpack(summed):
    shapes = ((128, 281), (128, 409), (96, 537), (64, 633), (32, 697), (2, 729))
    return pl.pallas_call(
        unpack_kernel,
        grid=(9,),
        out_shape=tuple(jax.ShapeDtypeStruct((9,) + s, F32) for s in shapes),
        in_specs=[pl.BlockSpec((TILE_ROWS, 128), lambda k: (k, 0))],
        out_specs=tuple(pl.BlockSpec((1,) + s, lambda k: (k, 0, 0)) for s in shapes),
        compiler_params=pltpu.CompilerParams(vmem_limit_bytes=32 * 2**20),
        name="unpack",
    )(summed)
WIDE, REST = lane_maps()
GATHER = gather_map()
START = start_map()


def arrange(convs, biases):
    wide = jnp.asarray(WIDE, BF)
    rest = jnp.asarray(REST, BF)
    blocks = []
    rest_blocks = []
    lanes = lax.broadcasted_iota(jnp.int32, (1, 128), 1)
    for n in range(6):
        outs, depth = OUTS[n], DEPTH[n]
        extra = (128, 128, 128, 64, 32, 32)[n] - outs
        weight = convs[n]
        term = lax.dot_general(
            weight, wide[729 - depth :], (((2,), (0,)), ((), ())), preferred_element_type=F32
        ).astype(BF)
        blocks.append(jnp.pad(term, ((0, 0), (0, extra), (0, 0))))
        split = weight.reshape(3, 3, outs, depth)
        total = sum(
            lax.dot_general(
                split[:, dx], rest[dx, 729 - depth :], (((2,), (0,)), ((), ())), preferred_element_type=F32
            )
            for dx in range(3)
        )
        high = biases[n].astype(BF).astype(F32)
        low = biases[n] - high
        bias = jnp.where(lanes == 57, high[:, None], 0.0) + jnp.where(lanes == 58, low[:, None], 0.0)
        total = jnp.concatenate([total[:1], total[1:2] + bias[None], total[2:]], axis=0)
        rest_blocks.append(jnp.pad(total.astype(BF), ((0, 0), (0, extra), (0, 0))))
    return jnp.concatenate(blocks, axis=1), jnp.concatenate(rest_blocks, axis=1)


def padded_2(block, sides, width):
    for axis, dim in sides:
        count = lax.axis_size(axis)
        forward = [(i, i + 1) for i in range(count - 1)]
        backward = [(target, source) for source, target in forward]
        low = lax.ppermute(
            lax.slice_in_dim(block, block.shape[dim] - width, None, axis=dim), axis, forward
        )
        high = lax.ppermute(lax.slice_in_dim(block, 0, width, axis=dim), axis, backward)
        block = jnp.concatenate([low, block, high], axis=dim)
    return block


def passed_along(value, axis, steps):
    count = lax.axis_size(axis)
    initial, last = (max(0, -steps), min(count, count - steps))
    return lax.ppermute(value, axis, [(source, source + steps) for source in range(initial, last)])


def warp_band(feature, flow):
    out_rows = feature.shape[1] - 2
    padded = jnp.pad(feature, ((0, 0), (0, 0), (0, 1)))
    across = flow[0, 1 : out_rows + 1]
    downward = flow[1, 1 : out_rows + 1]
    upper_row = (1.0 - across) * padded[:, 1 : out_rows + 1, :-1] + across * padded[
        :, 1 : out_rows + 1, 1:
    ]
    lower_row = (1.0 - across) * padded[:, 2 : out_rows + 2, :-1] + across * padded[
        :, 2 : out_rows + 2, 1:
    ]
    return (1.0 - downward) * upper_row + downward * lower_row


def correlate_band(first, warped):
    span = 2 * MD + 1
    rows = first.shape[1]
    width = first.shape[2]
    padded = jnp.pad(warped, ((0, 0), (0, 0), (MD, MD)))
    planes = []
    for row_off in range(span):
        for col_off in range(span):
            planes.append(
                jnp.sum(
                    first * padded[:, row_off : row_off + rows, col_off : col_off + width], axis=0
                )
            )
    return jnp.stack(planes) / CH**0.5


def all_sum(value):
    axes = ("chan", "pix")
    count = lax.axis_size(axes)
    height = value.shape[0] // count
    parts = value.reshape(count, height, 128)
    parts = lax.all_to_all(parts, axes, split_axis=0, concat_axis=0, tiled=True)
    block = jnp.sum(parts.astype(F32), axis=0).astype(BF)
    spread = jnp.broadcast_to(block[None], (count, height, 128))
    spread = lax.all_to_all(spread, axes, split_axis=0, concat_axis=0, tiled=True)
    return spread.reshape(value.shape)


def local(
    feat_one, feat_two, up_flow, up_feat, target_flow, valid_mask,
    conv_one, conv_two, conv_three, conv_four, conv_five, flow_head,
    bias_one, bias_two, bias_three, bias_four, bias_five, bias_head,
):
    convs = [conv_one, conv_two, conv_three, conv_four, conv_five, flow_head]
    biases = [bias_one, bias_two, bias_three, bias_four, bias_five, bias_head]
    weight, weight_rest = arrange(convs, biases)
    rows = feat_one.shape[1]
    width = feat_one.shape[2]
    cols = width // lax.axis_size("chan")
    local_ch = feat_two.shape[0]
    halo_rows = MD + 1
    joined = jnp.concatenate([feat_two, up_flow], axis=0)
    banded = padded_2(joined, (("pix", 1),), halo_rows).astype(jnp.float32)
    warped, warp_back = jax.vjp(jax.checkpoint(warp_band), banded[:local_ch], banded[local_ch:])
    warped_low = lax.optimization_barrier(warped.astype(jnp.bfloat16)).astype(jnp.float32)
    partial_cost, cost_back = jax.vjp(
        jax.checkpoint(correlate_band), feat_one.astype(jnp.float32), warped_low
    )
    cost = lax.psum_scatter(
        partial_cost.astype(jnp.bfloat16), "chan", scatter_dimension=2, tiled=True
    )
    first_cols = lax.all_to_all(feat_one, "chan", split_axis=2, concat_axis=0, tiled=True)
    col_start = lax.axis_index("chan") * cols
    flow_cols = lax.dynamic_slice_in_dim(up_flow, col_start, cols, 2)
    start_piece = jnp.concatenate([cost, first_cols, flow_cols, up_feat], axis=0)

    start = lax.dot_general(
        start_piece.reshape(281, rows * cols), jnp.asarray(START, BF),
        (((0,), (0,)), ((), ())), preferred_element_type=F32,
    ).astype(BF)
    high = target_flow.astype(BF)
    low = (target_flow - high.astype(F32)).astype(BF)
    one = jnp.ones((1, rows, cols), BF)
    extra = jnp.concatenate([one, one, valid_mask.astype(BF)[None], high, low], axis=0)
    extra = jnp.transpose(extra.reshape(7, rows * cols))
    window = jnp.concatenate([start[:, :281], extra], axis=1).reshape(rows, cols, 288)
    window = padded_2(window, (("pix", 0), ("chan", 1)), HALO)
    window = jnp.pad(window, ((0, 0), (LEFT - HALO, PITCH - COLS - LEFT - HALO), (0, 0)))
    main = window[:, :, :256].reshape(NPX, 256)
    rest = jnp.pad(window[:, :, 256:], ((0, 0), (0, 0), (0, 96))).reshape(NPX, 128)
    acts, slopes, grad_main, grad_rest, flow, sums = decode(main, rest, weight, weight_rest)
    core_px = slice(HALO * PITCH, (HALO + ROWS) * PITCH)
    grads, bias_sums = wgrad(slopes, main[core_px], rest[core_px], acts, jnp.asarray(GATHER, BF))

    def core(value):
        return value.reshape(ROWS, PITCH, -1)[:, LEFT : LEFT + COLS]

    flow_out = jnp.transpose(core(flow)[:, :, 96:98], (2, 0, 1))
    table = jnp.asarray(START, BF)
    grad_start = lax.dot_general(
        table[:277, :256], core(grad_main).reshape(rows * cols, 256),
        (((1,), (1,)), ((), ())), preferred_element_type=F32,
    ) + lax.dot_general(
        table[:277, 256:], core(grad_rest).reshape(rows * cols, 128).astype(BF),
        (((1,), (1,)), ((), ())), preferred_element_type=F32,
    )
    grad_start = grad_start.reshape(277, rows, cols)
    small = jnp.transpose(core(grad_rest)[:, :, 21:25], (2, 0, 1))
    grad_cost = grad_start[:81].astype(BF)
    grad_first_dec = grad_start[81:].astype(BF)
    grad_flow_dec = small[:2]
    grad_up_feat = small[2:]
    cost_full = lax.all_gather(grad_cost, "chan", axis=2, tiled=True).astype(jnp.float32)
    first_back = lax.all_to_all(
        grad_first_dec, "chan", split_axis=0, concat_axis=2, tiled=True
    ).astype(jnp.float32)
    grad_first_corr, grad_warped = cost_back(cost_full)
    grad_feat_one = grad_first_corr + first_back
    grad_band, grad_flow_band = warp_back(grad_warped)
    joined_grad = jnp.concatenate([grad_band, grad_flow_band], axis=0)
    upper_rim = joined_grad[:, :halo_rows]
    lower_rim = joined_grad[:, halo_rows + rows :]
    middle = joined_grad[:, halo_rows : halo_rows + rows]
    from_below = passed_along(upper_rim.astype(jnp.bfloat16), "pix", -1).astype(upper_rim.dtype)
    from_above = passed_along(lower_rim.astype(jnp.bfloat16), "pix", 1).astype(lower_rim.dtype)
    middle = middle + jnp.pad(from_below, ((0, 0), (rows - halo_rows, 0), (0, 0)))
    middle = middle + jnp.pad(from_above, ((0, 0), (0, rows - halo_rows), (0, 0)))
    grad_feat_two = middle[:local_ch]
    flow_part = lax.psum_scatter(
        middle[local_ch:].astype(jnp.bfloat16), "chan", scatter_dimension=2, tiled=True
    ).astype(jnp.float32)
    grad_up_flow = flow_part + grad_flow_dec
    scalars = jnp.sum(sums[:, :, 96], axis=1)
    small = jnp.concatenate([bias_sums[:, 89], scalars, jnp.zeros((509,), F32)]).reshape(8, 128)
    small = jnp.sum(lax.all_gather(small, ("chan", "pix"), axis=0), axis=0).reshape(1024)
    bias_sums, scalars = small[:512], small[512:515]
    summed = all_sum(grads)
    weight_grads = unpack(summed)
    bias_grads = [bias_sums[ROW0[n] : ROW0[n] + OUTS[n]] for n in range(6)]
    return (flow_out, scalars, grad_feat_one, grad_feat_two, grad_up_flow, grad_up_feat, *weight_grads, *bias_grads)


def solution(mesh):
    return jax.shard_map(
        local,
        mesh=mesh,
        in_specs=(
            P("chan", "pix", None),
            P("chan", "pix", None),
            P(None, "pix", None),
            P(None, "pix", "chan"),
            P(None, "pix", "chan"),
            P("pix", "chan"),
        )
        + (P(),) * 12,
        out_specs=(
            P(None, "pix", "chan"),
            P(),
            P("chan", "pix", None),
            P("chan", "pix", None),
            P(None, "pix", "chan"),
            P(None, "pix", "chan"),
        )
        + (P(),) * 12,
        check_vma=False,
    )
```

```python
import jax
import jax.numpy as jnp
import numpy as np
from jax import lax
from jax.experimental import pallas as pl
from jax.experimental.pallas import tpu as pltpu
from jax.sharding import PartitionSpec as P

CH = 196
MD = 4
CH_SLOT = 49
OUTS = (128, 128, 96, 64, 32, 2)
ROW0 = (0, 128, 256, 384, 448, 480)
DEPTH = (281, 409, 537, 633, 697, 729)


def start_lane(channel):
    if channel < 81:
        dy, dx = divmod(channel, 9)
        if dy < 4:
            return 0, 64 * dy + 49 + dx
        if dy < 8:
            if dx < 6:
                return 0, 64 * (dy - 4) + 58 + dx
            return 1, 3 * (dy - 4) + dx - 6
        return 1, 12 + dx
    if channel < 277:
        slot, inner = divmod(channel - 81, CH_SLOT)
        return 0, 64 * slot + inner
    return 1, 21 + channel - 277


def lane_maps():
    wide = np.zeros((729, 768), np.float32)
    rest = np.zeros((3, 729, 128), np.float32)
    for c in range(729):
        if c < 32:
            wide[c, 704 + c] = 1
        elif c < 96:
            wide[c, 640 + c - 32] = 1
        elif c < 192:
            wide[c, 512 + c - 96] = 1
        elif c < 320:
            wide[c, 384 + c - 192] = 1
        elif c < 448:
            wide[c, 256 + c - 320] = 1
        else:
            block, lane = start_lane(c - 448)
            if block == 0:
                wide[c, lane] = 1
            else:
                for dx in range(3):
                    rest[dx, c, 32 * dx + lane] = 1
    return wide, rest


def gather_map():
    table = np.zeros((896, 768), np.float32)
    for c in range(281):
        block, lane = start_lane(c)
        table[288 * block + lane, 448 + c] = 1
    table[288 + 25, 729] = 1
    for i in range(128):
        table[384 + i, 320 + i] = 1
        table[512 + i, 192 + i] = 1
    for i in range(96):
        table[640 + i, 96 + i] = 1
        table[768 + i, (32 + i) if i < 64 else i - 64] = 1
    return table


def start_map():
    table = np.zeros((281, 384), np.float32)
    for c in range(281):
        block, lane = start_lane(c)
        table[c, 256 * block + lane] = 1
    return table

BF = jnp.bfloat16
F32 = jnp.float32
HALO = 12
PITCH = 96
ROWS = 24
COLS = 64
LEFT = 16
WROWS = ROWS + 2 * HALO
NPX = WROWS * PITCH
GUARD = 16
VMEM_MB = 62


def nt(a, b):
    return lax.dot_general(a, b, (((1,), (1,)), ((), ())), preferred_element_type=F32)


def nn(a, b):
    return lax.dot_general(a, b, (((1,), (0,)), ((), ())), preferred_element_type=F32)


def decode_kernel(
    top_ref, h0_ref, h1_ref, bottom_ref, left_ref, right_ref, w_ref, wr_ref,
    a_ref, g_ref, xm_ref, xr_ref, dm_ref, dr_ref, flow_ref, met_ref,
    xs, xq, sh, pre, sc, mk, sems,
):
    lane = lax.broadcasted_iota(jnp.int32, (PITCH, 128), 1)

    def rows(lo, hi, body):
        def step(i, carry):
            body(pl.multiple_of(i * PITCH, PITCH))
            return carry
        lax.fori_loop(lo, hi, step, 0)

    def shifted_store(dst, lanes, lo, hi):
        def body(p):
            for d in range(3):
                dst[d, pl.ds(p, PITCH), lanes] = sc[pl.ds(p + GUARD + d - 1, PITCH), :].astype(BF)
        rows(lo, hi, body)

    def chunked(lo, hi, count, body):
        size = (hi - lo) * PITCH // count

        def step(i, carry):
            body(pl.multiple_of(lo * PITCH + i * size, 16), size)
            return carry
        lax.fori_loop(0, count, step, 0)

    sc[pl.ds(0, GUARD), :] = jnp.zeros((GUARD, 128), F32)
    sc[pl.ds(GUARD + NPX, GUARD), :] = jnp.zeros((GUARD, 128), F32)

    for h, tile in enumerate((top_ref, h0_ref, h1_ref, bottom_ref)):
        def main_rows(i, carry, h=h, tile=tile):
            p = pl.multiple_of((12 * h + i) * PITCH, PITCH)
            for half in range(2):
                lanes = slice(128 * half, 128 * half + 128)
                at = pl.multiple_of((12 * half + i) * COLS, COLS)
                xs[1, pl.ds(p, LEFT), lanes] = left_ref[27 * h + 12 * half + i]
                xs[1, pl.ds(p + LEFT, COLS), lanes] = tile[pl.ds(at, COLS), :]
                xs[1, pl.ds(p + LEFT + COLS, LEFT), lanes] = right_ref[27 * h + 12 * half + i]
            return carry
        lax.fori_loop(0, 12, main_rows, 0)
        for a in range(4):
            def rest_rows(b, carry, h=h, tile=tile, a=a):
                p = pl.multiple_of((12 * h + 3 * a + b) * PITCH, PITCH)
                value = jnp.concatenate(
                    [
                        left_ref[27 * h + 24 + b].astype(F32),
                        tile[pl.ds(pl.multiple_of(1536 + b * COLS, COLS), COLS), :].astype(F32),
                        right_ref[27 * h + 24 + b].astype(F32),
                    ],
                    axis=0,
                )
                value = jnp.where(lane < 32, pltpu.roll(value, (128 - 32 * a) % 128, 1), 0.0)
                sc[pl.ds(p + GUARD, PITCH), :] = value
                mk[pl.ds(p, PITCH), :] = jnp.broadcast_to(value[:, 25:26], (PITCH, 128))
                return carry
            lax.fori_loop(0, 3, rest_rows, 0)

    def rest_cat(p):
        low = sc[pl.ds(p + GUARD - 1, PITCH), :]
        mid = pltpu.roll(sc[pl.ds(p + GUARD, PITCH), :], 32, 1)
        high = pltpu.roll(sc[pl.ds(p + GUARD + 1, PITCH), :], 64, 1)
        xq[pl.ds(p, PITCH), :] = jnp.where(
            lane < 32, low, jnp.where(lane < 64, mid, jnp.where(lane < 96, high, 0.0))
        ).astype(BF)
    rows(0, WROWS, rest_cat)

    for half in range(2):
        lanes = slice(128 * half, 128 * half + 128)

        def main_in(p):
            sc[pl.ds(p + GUARD, PITCH), :] = xs[1, pl.ds(p, PITCH), lanes].astype(F32)
        rows(0, WROWS, main_in)
        shifted_store(xs, lanes, 0, WROWS)

    core = pl.ds(HALO * PITCH, ROWS * PITCH)
    keep = [
        pltpu.make_async_copy(xs.at[1, core, :], xm_ref, sems.at[1]),
        pltpu.make_async_copy(xq.at[core, :], xr_ref, sems.at[2]),
    ]
    for copy in keep:
        copy.start()

    def start_sums(p, size):
        total = None
        for dy in range(3):
            at = p + PITCH * (dy - 1)
            term = nt(xq[pl.ds(at, size), :], wr_ref[dy])
            total = term if total is None else total + term
            for dx in range(3):
                total = total + nt(xs[dx, pl.ds(at, size), :], w_ref[3 * dy + dx, :, 0:256])
        pre[pl.ds(p, size), :] = total
    chunked(1, WROWS - 1, 6, start_sums)

    first_lane = [0, 128, 256, 384, 384]
    part = [(0, 128), (0, 128), (0, 96), (0, 64), (64, 96)]
    for layer in range(5):
        block = slice(first_lane[layer], first_lane[layer] + 128)
        from_lane, to_lane = part[layer]
        inside = (lane >= from_lane) & (lane < to_lane)
        lo, hi = layer + 1, WROWS - layer - 1

        def activate(p, block=block, inside=inside):
            value = pre[pl.ds(p, PITCH), block]
            sig = 1.0 / (1.0 + jnp.exp(-value))
            keep = inside & (mk[pl.ds(p, PITCH), :] > 0.0)
            sc[pl.ds(p + GUARD, PITCH), :] = jnp.where(keep, value * sig, 0.0)
            slope = jnp.where(keep, sig * (1.0 + value * (1.0 - sig)), 0.0)
            pre[pl.ds(p, PITCH), block] = jnp.where(inside, slope, value)
        rows(lo, hi, activate)
        piece = min(layer, 3)

        def keep_core(p, layer=layer, piece=piece):
            value = sc[pl.ds(p + GUARD, PITCH), :].astype(BF)
            q = pl.multiple_of(p - HALO * PITCH, PITCH)
            lanes = slice(128 * piece, 128 * piece + 128)
            if layer == 4:
                a_ref[pl.ds(q, PITCH), lanes] = a_ref[pl.ds(q, PITCH), lanes] + value
            else:
                a_ref[pl.ds(q, PITCH), lanes] = value
        rows(HALO, HALO + ROWS, keep_core)
        shifted_store(sh, slice(128 * piece, 128 * piece + 128), lo, hi)
        out0 = min(128 * (layer + 1), 384)

        def add_sums(p, size, piece=piece, out0=out0):
            total = pre[pl.ds(p, size), out0:512]
            for dy in range(3):
                at = p + PITCH * (dy - 1)
                left = jnp.concatenate(
                    [sh[dx, pl.ds(at, size), 128 * piece : 128 * piece + 128] for dx in range(3)], axis=1
                )
                right = jnp.concatenate(
                    [w_ref[3 * dy + dx, out0:512, 256 + 128 * piece : 384 + 128 * piece] for dx in range(3)],
                    axis=1,
                )
                total = total + nt(left, right)
            pre[pl.ds(p, size), out0:512] = total
        chunked(lo + 1, hi - 1, 6, add_sums)

    is_flow = (lane >= 96) & (lane < 98)
    column = lax.broadcasted_iota(jnp.int32, (PITCH, 128), 0)
    core_column = (column >= LEFT) & (column < LEFT + COLS)
    met_ref[...] = jnp.zeros((3, PITCH, 128), F32)

    def loss(p):
        flow = pre[pl.ds(p, PITCH), 384:512]
        rest = xq[pl.ds(p, PITCH), :].astype(F32)
        target = pltpu.roll(rest, 96 - 60, 1) + pltpu.roll(rest, 96 - 62, 1)
        diff = jnp.where(is_flow, flow - target, 0.0)
        square = diff * diff
        other = jnp.where(lane == 96, pltpu.roll(square, 127, 1), pltpu.roll(square, 1, 1))
        error = jnp.sqrt(square + other + 1.0)
        mask = jnp.broadcast_to(rest[:, 59:60], (PITCH, 128))
        sc[pl.ds(p + GUARD, PITCH), :] = jnp.where(is_flow, mask * diff / error, 0.0)
        return flow, mask, error

    def loss_rim(p):
        loss(p)

    def loss_core(p):
        flow, mask, error = loss(p)
        q = pl.multiple_of(p - HALO * PITCH, PITCH)
        flow_ref[pl.ds(q, PITCH), :] = flow
        mask = jnp.where(core_column, mask, 0.0)
        met_ref[0] += mask * (error - 1.0)
        met_ref[1] += mask / (1.0 + jnp.exp(-4.0 * (error - 2.0)))
        met_ref[2] += mask

    rows(6, HALO, loss_rim)
    rows(HALO, HALO + ROWS, loss_core)
    rows(HALO + ROWS, WROWS - 6, loss_rim)
    shifted_store(sh, slice(384, 512), 6, WROWS - 6)

    for layer in range(4, -1, -1):
        lo, hi = HALO - layer - 1, HALO + ROWS + layer + 1
        piece = min(layer, 3)
        out0 = min(128 * (layer + 1), 384)
        block = slice(first_lane[layer], first_lane[layer] + 128)
        from_lane, to_lane = part[layer]
        inside = (lane >= from_lane) & (lane < to_lane)
        c0 = 256 + 128 * piece

        def back(p, size, out0=out0, c0=c0):
            total = None
            for dy in range(3):
                at = p - PITCH * (dy - 1)
                left = jnp.concatenate([sh[2 - dx, pl.ds(at, size), out0:512] for dx in range(3)], axis=1)
                right = jnp.concatenate([w_ref[3 * dy + dx, out0:512, c0 : c0 + 128] for dx in range(3)], axis=0)
                term = nn(left, right)
                total = term if total is None else total + term
            mk[pl.ds(p, size), :] = total
        chunked(lo, hi, 6, back)

        def slope(p, layer=layer, block=block, inside=inside):
            value = mk[pl.ds(p, PITCH), :] * pre[pl.ds(p, PITCH), block]
            if layer >= 3:
                old = sc[pl.ds(p + GUARD, PITCH), :]
                sc[pl.ds(p + GUARD, PITCH), :] = jnp.where(inside, value, old)
            else:
                sc[pl.ds(p + GUARD, PITCH), :] = value
        rows(lo, hi, slope)
        shifted_store(sh, slice(128 * piece, 128 * piece + 128), lo, hi)

    copy = pltpu.make_async_copy(sh.at[:, pl.ds((HALO - 1) * PITCH, (ROWS + 2) * PITCH), :], g_ref, sems.at[0])
    keep.append(copy)
    copy.start()

    def back_rest(p, size):
        total = None
        for dy in range(3):
            term = nn(sh[1, pl.ds(p - PITCH * (dy - 1), size), :], wr_ref[dy])
            total = term if total is None else total + term
        sc[pl.ds(p + GUARD, size), :] = total
    chunked(HALO, HALO + ROWS, 6, back_rest)

    def rest_out(p):
        q = pl.multiple_of(p - HALO * PITCH, PITCH)
        dr_ref[pl.ds(q, PITCH), :] = (
            sc[pl.ds(p + GUARD + 1, PITCH), :]
            + pltpu.roll(sc[pl.ds(p + GUARD, PITCH), :], 96, 1)
            + pltpu.roll(sc[pl.ds(p + GUARD - 1, PITCH), :], 64, 1)
        )
    rows(HALO, HALO + ROWS, rest_out)

    def back_main(p, size):
        total = None
        for dy in range(3):
            at = p - PITCH * (dy - 1)
            for dx in range(3):
                term = nn(sh[2 - dx, pl.ds(at, size), :], w_ref[3 * dy + dx, :, 0:256])
                total = term if total is None else total + term
        q = pl.multiple_of(p - HALO * PITCH, 16)
        dm_ref[pl.ds(q, size), :] = total.astype(BF)
    chunked(HALO, HALO + ROWS, 6, back_main)
    for copy in keep:
        copy.wait()


def decode(top, h0, h1, bottom, left, right, w, wr):
    core = ROWS * PITCH
    vm = pl.BlockSpec(memory_space=pltpu.VMEM)
    hbm = pl.BlockSpec(memory_space=pl.ANY)
    return pl.pallas_call(
        decode_kernel,
        out_shape=(
            jax.ShapeDtypeStruct((core, 512), BF),
            jax.ShapeDtypeStruct((3, (ROWS + 2) * PITCH, 512), BF),
            jax.ShapeDtypeStruct((core, 256), BF),
            jax.ShapeDtypeStruct((core, 128), BF),
            jax.ShapeDtypeStruct((core, 256), BF),
            jax.ShapeDtypeStruct((core, 128), F32),
            jax.ShapeDtypeStruct((core, 128), F32),
            jax.ShapeDtypeStruct((3, PITCH, 128), F32),
        ),
        in_specs=[vm] * 8,
        out_specs=(vm, hbm, hbm, hbm, vm, vm, vm, vm),
        scratch_shapes=[
            pltpu.VMEM((3, NPX, 256), BF),
            pltpu.VMEM((NPX, 128), BF),
            pltpu.VMEM((3, NPX, 512), BF),
            pltpu.VMEM((NPX, 512), F32),
            pltpu.VMEM((NPX + 2 * GUARD, 128), F32),
            pltpu.VMEM((NPX, 128), F32),
            pltpu.SemaphoreType.DMA((3,)),
        ],
        compiler_params=pltpu.CompilerParams(vmem_limit_bytes=VMEM_MB * 2**20),
        name="decode",
    )(top, h0, h1, bottom, left, right, w, wr)

TILE_ROWS = 2048


def tn(a, b):
    return lax.dot_general(a, b, (((0,), (0,)), ((), ())), preferred_element_type=F32)


def wgrad_kernel(g_ref, xm_ref, xr_ref, a_ref, qp_ref, o_ref, xp):
    column = lax.broadcasted_iota(jnp.int32, (PITCH, 768), 0)
    core = (column >= LEFT) & (column < LEFT + COLS)
    core = jnp.concatenate([core] * 4, axis=0)
    size = 4 * PITCH

    def gather(i, carry):
        at = pl.ds(pl.multiple_of(i * size, size), size)
        left = jnp.concatenate([xm_ref[at, :], xr_ref[at, :], a_ref[at, :]], axis=1)
        xp[at, :] = jnp.where(core, nn(left, qp_ref[...]), 0.0).astype(BF)
        return carry
    lax.fori_loop(0, ROWS // 4, gather, 0)

    for k in range(9):
        dy, dx = divmod(k, 3)
        at = pl.ds(PITCH * (2 - dy), ROWS * PITCH)
        base = TILE_ROWS * k
        value = tn(g_ref[2 - dx, at, 0:256], xp[:, 256:768])
        low = value.astype(BF)
        for t in range(3):
            o_ref[base + 128 * t : base + 128 * t + 128, :] = low[0:128, 128 * t + 128 : 128 * t + 256]
        for t in range(4):
            o_ref[base + 384 + 128 * t : base + 512 + 128 * t, :] = low[128:256, 128 * t : 128 * t + 128]
        value = tn(g_ref[2 - dx, at, 256:512], xp[...])
        low = value.astype(BF)
        for t in range(5):
            o_ref[base + 896 + 96 * t : base + 992 + 96 * t, :] = low[0:96, 128 * t + 128 : 128 * t + 256]
        for t in range(6):
            o_ref[base + 1376 + 112 * t : base + 1488 + 112 * t, :] = low[128:240, 128 * t : 128 * t + 128]


def wgrad(g, xm, xr, a, qp):
    vm = pl.BlockSpec(memory_space=pltpu.VMEM)
    return pl.pallas_call(
        wgrad_kernel,
        out_shape=jax.ShapeDtypeStruct((9 * TILE_ROWS, 128), BF),
        in_specs=[vm] * 5,
        out_specs=vm,
        scratch_shapes=[pltpu.VMEM((ROWS * PITCH, 768), BF)],
        compiler_params=pltpu.CompilerParams(vmem_limit_bytes=VMEM_MB * 2**20),
        name="wgrad",
    )(g, xm, xr, a, qp)


def unpack_kernel(s_ref, o1, o2, o3, o4, o5, o6, b_ref):
    def tiles(base, height, count):
        return jnp.concatenate(
            [s_ref[base + height * t : base + height * (t + 1), :].astype(F32) for t in range(count)], axis=1
        )
    o1[0] = tiles(0, 128, 3)[:, 64 : 64 + 281]
    o2[0] = tiles(384, 128, 4)[:, 64 : 64 + 409]
    o3[0] = tiles(896, 96, 5)[:, 64 : 64 + 537]
    last = tiles(1376, 112, 6)
    o4[0] = last[0:64, 96:729]
    o5[0] = last[64:96, 32:729]
    o6[0] = last[96:98, 0:729]

    @pl.when(pl.program_id(0) == 4)
    def _():
        b_ref[0:128, :] = tiles(256, 128, 1)
        b_ref[128:256, :] = tiles(768, 128, 1)
        b_ref[256:352, :] = tiles(1280, 96, 1)
        b_ref[352:384, :] = jnp.zeros((32, 128), F32)
        b_ref[384:496, :] = last[:, 640:768]
        b_ref[496:512, :] = jnp.zeros((16, 128), F32)


def unpack(summed):
    shapes = ((128, 281), (128, 409), (96, 537), (64, 633), (32, 697), (2, 729))
    results = pl.pallas_call(
        unpack_kernel,
        grid=(9,),
        out_shape=tuple(jax.ShapeDtypeStruct((9,) + s, F32) for s in shapes)
        + (jax.ShapeDtypeStruct((512, 128), F32),),
        in_specs=[pl.BlockSpec((TILE_ROWS, 128), lambda k: (k, 0))],
        out_specs=tuple(pl.BlockSpec((1,) + s, lambda k: (k, 0, 0)) for s in shapes)
        + (pl.BlockSpec((512, 128), lambda k: (0, 0)),),
        compiler_params=pltpu.CompilerParams(vmem_limit_bytes=32 * 2**20),
        name="unpack",
    )(summed)
    return results[:6], results[6]

SLOT = 64
WIN = 80
PAY = 12 * COLS + 16 * WIN
HALF = 27 * COLS


def slanted(x, shift):
    shift = shift % 128
    if shift % 8:
        x = pltpu.roll(x, shift % 8, 1)
    return pltpu.roll(x, shift - shift % 8, 1, stride=1, stride_axis=0)


def two_rows(lane, parts):
    swap = [pltpu.roll(part, 64, 1) for part in parts]
    first = [jnp.where(lane < 64, parts[2 * h], swap[2 * h + 1]) for h in range(2)]
    second = [jnp.where(lane < 64, swap[2 * h], parts[2 * h + 1]) for h in range(2)]
    return jnp.concatenate(first, axis=1), jnp.concatenate(second, axis=1)


def pack_kernel(f1_ref, f2_ref, above_ref, below_ref, o_ref, band, turn):
    eye = jnp.where(
        lax.broadcasted_iota(jnp.int32, (256, 256), 0) == lax.broadcasted_iota(jnp.int32, (256, 256), 1), 1.0, 0.0
    ).astype(BF)
    back = jnp.where(
        lax.broadcasted_iota(jnp.int32, (256, 256), 0) + lax.broadcasted_iota(jnp.int32, (256, 256), 1) == 255, 1.0, 0.0
    ).astype(BF)
    last = lax.broadcasted_iota(jnp.int32, (SLOT, 256), 1) == 255
    channel = lax.broadcasted_iota(jnp.int32, (SLOT, 256), 0) < CH // 4
    band[0:MD] = above_ref[...]
    band[MD : MD + ROWS] = f2_ref[...]
    band[MD + ROWS :] = below_ref[...]
    turn[...] = jnp.zeros(turn.shape, F32)

    def first(i, carry):
        both = jnp.concatenate([f1_ref[i], f1_ref[i + 12]], axis=0)
        value = nt(back, both).astype(BF)
        for z in range(4):
            o_ref[z, pl.ds(pl.multiple_of(i * COLS, COLS), COLS), :] = value[192 - COLS * z : 256 - COLS * z]
        return carry
    lax.fori_loop(0, 12, first, 0)

    def warped(t):
        upper = band[t].astype(F32)
        lower = band[t + 1].astype(F32)
        u = upper[49:50]
        v = upper[50:51]

        def across(x):
            return (1.0 - u) * x + u * jnp.where(last, 0.0, pltpu.roll(x, 255, 1))
        value = (1.0 - v) * across(upper) + v * across(lower)
        return jnp.where(channel, value, 0.0).astype(BF)

    def second(i, carry):
        both = jnp.concatenate([warped(i), warped(i + 16)], axis=0)
        turn[8:264, :] = nt(eye, both)
        for z in range(4):
            start = pl.multiple_of(12 * COLS + i * WIN, 16)
            o_ref[z, pl.ds(start, WIN), :] = turn[COLS * z + 4 : COLS * z + 4 + WIN, :].astype(BF)
        return carry
    lax.fori_loop(0, 16, second, 0)


def pack(f1, f2, above, below):
    vm = pl.BlockSpec(memory_space=pltpu.VMEM)
    return pl.pallas_call(
        pack_kernel,
        out_shape=jax.ShapeDtypeStruct((4, PAY, 128), BF),
        in_specs=[vm] * 4,
        out_specs=vm,
        scratch_shapes=[pltpu.VMEM((33, SLOT, 256), BF), pltpu.VMEM((288, 128), F32)],
        compiler_params=pltpu.CompilerParams(vmem_limit_bytes=32 * 2**20),
        name="pack",
    )(f1, f2, above, below)


def flip_matrix():
    total = lax.broadcasted_iota(jnp.int32, (COLS, COLS), 0) + lax.broadcasted_iota(jnp.int32, (COLS, COLS), 1)
    return jnp.where(total == COLS - 1, 1.0, 0.0).astype(BF)


def read_features(rx_ref, lane, first_rows, warped_rows):
    def first(i, carry):
        at = pl.ds(pl.multiple_of(i * COLS, COLS), COLS)
        one, two = two_rows(lane[:COLS], [rx_ref[q, at, :].astype(F32) for q in range(4)])
        first_rows(i, one.astype(BF))
        first_rows(i + 12, two.astype(BF))
        return carry
    lax.fori_loop(0, 12, first, 0)

    def second(i, carry):
        at = pl.ds(pl.multiple_of(12 * COLS + i * WIN, 16), WIN)
        one, two = two_rows(lane[:WIN], [rx_ref[q, at, :].astype(F32) for q in range(4)])
        warped_rows(i, one.astype(BF))
        warped_rows(i + 16, two.astype(BF))
        return carry
    lax.fori_loop(0, 16, second, 0)


def cost_kernel(rx_ref, ex_ref, h0_ref, h1_ref, fs, ws, rs):
    lane = lax.broadcasted_iota(jnp.int32, (128, 128), 1)

    def put_first(i, value):
        fs[i] = value

    def put_warped(i, value):
        ws[i, 0:WIN] = value
    read_features(rx_ref, lane, put_first, put_warped)
    lane = lane[:COLS]
    flip = flip_matrix()

    def row(ii, carry):
        for half, out in ((0, h0_ref), (1, h1_ref)):
            i = ii + 12 * half
            left = fs[i]
            sums = nt(left, ws[pl.ds(i, 9)].reshape(9 * 128, 256)) * (1.0 / CH**0.5)

            def band(dy, t, lo, hi, value):
                block = slanted(sums[:, 128 * dy : 128 * dy + 128], t - 63)
                return jnp.where((lane >= lo) & (lane < hi), block, value)
            for h in range(2):
                value = left[:, 128 * h : 128 * h + 128].astype(F32)
                for s in range(2):
                    at = 64 * s + 49
                    value = band(2 * h + s, at, at, at + 9, value)
                    value = band(4 + 2 * h + s, at + 9, at + 9, at + 15, value)
                value = nn(flip, value.astype(BF)).astype(BF)
                out[pl.ds(pl.multiple_of(768 * h + ii * COLS, COLS), COLS), :] = value
            value = jnp.zeros((COLS, 128), F32)
            for a in range(4):
                value = band(4 + a, 3 * a - 6, 3 * a, 3 * a + 3, value)
            value = band(8, 12, 12, 21, value)
            rs[i] = nn(flip, value.astype(BF)) + ex_ref[i].astype(F32)
        return carry
    lax.fori_loop(0, 12, row, 0)
    for half, out in ((0, h0_ref), (1, h1_ref)):
        for b in range(3):
            total = rs[12 * half + b]
            for a in range(1, 4):
                total = total + pltpu.roll(rs[12 * half + 3 * a + b], 32 * a, 1)
            out[1536 + COLS * b : 1536 + COLS * b + COLS, :] = total.astype(BF)


def cost_volume(rx, extra):
    vm = pl.BlockSpec(memory_space=pltpu.VMEM)
    return pl.pallas_call(
        cost_kernel,
        out_shape=(jax.ShapeDtypeStruct((HALF, 128), BF),) * 2,
        in_specs=[vm] * 2,
        out_specs=(vm, vm),
        scratch_shapes=[
            pltpu.VMEM((ROWS, COLS, 256), BF),
            pltpu.VMEM((ROWS + 8, 128, 256), BF),
            pltpu.VMEM((ROWS, COLS, 128), F32),
        ],
        compiler_params=pltpu.CompilerParams(vmem_limit_bytes=32 * 2**20),
        name="cost_volume",
    )(rx, extra)


def cost_back_kernel(rx_ref, dm_ref, dr_ref, o_ref, fs, ws, bs, gs):
    lane = lax.broadcasted_iota(jnp.int32, (128, 128), 1)
    fs[0:8] = jnp.zeros((8, COLS, 256), BF)
    fs[32:40] = jnp.zeros((8, COLS, 256), BF)

    flip = flip_matrix()

    def put_first(i, value):
        fs[i + 8] = nn(flip, value).astype(BF)

    def put_warped(i, value):
        ws[i, 0:WIN] = value
        ws[i, WIN:] = jnp.zeros((128 - WIN, 256), BF)
    read_features(rx_ref, lane, put_first, put_warped)

    def clear(t, carry):
        bs[t] = jnp.zeros((9 * COLS, 128), BF)
        bs[t + 24] = jnp.zeros((9 * COLS, 128), BF)
        return carry
    lax.fori_loop(0, 8, clear, 0)
    lane = lane[:COLS]
    ahead = lane - lax.broadcasted_iota(jnp.int32, (COLS, 128), 0)

    def row(i, carry):
        at = pl.ds(pl.multiple_of(i * PITCH + LEFT, 16), COLS)
        main = dm_ref[at, :].astype(F32)
        halves = [main[:, 0:128], main[:, 128:256]]
        rest = dr_ref[at, :].astype(BF).astype(F32)

        def band(source, t, lo, hi):
            shift = (-t) % 128
            extra = shift % 8
            block = pltpu.roll(source, shift - extra, 1, stride=1, stride_axis=0)
            block = jnp.where(((ahead + (extra - lo)) & 127) < hi - lo, block, 0.0)
            return pltpu.roll(block, extra, 1) if extra else block
        bands = []
        for dy in range(4):
            bands.append(band(halves[dy // 2], 64 * (dy % 2) + 49, 0, 9))
        for a in range(4):
            bands.append(band(halves[a // 2], 64 * (a % 2) + 58, 0, 6) + band(rest, 3 * a - 6, 6, 9))
        bands.append(band(rest, 12, 0, 9))
        bands = [b.astype(BF) for b in bands]
        for dy in range(9):
            bs[i + dy, (8 - dy) * COLS : (9 - dy) * COLS, :] = bands[dy]
        total = nn(jnp.concatenate(bands, axis=1), ws[pl.ds(i, 9)].reshape(9 * 128, 256))
        gs[i] = total * (1.0 / CH**0.5) + main
        return carry
    lax.fori_loop(0, ROWS, row, 0)

    def put(start, size, one, two):
        for z in range(4):
            h, odd = divmod(z, 2)
            a = one[:, 128 * h : 128 * h + 128]
            b = two[:, 128 * h : 128 * h + 128]
            if odd:
                a = pltpu.roll(a, 64, 1)
            else:
                b = pltpu.roll(b, 64, 1)
            low = lax.broadcasted_iota(jnp.int32, (size, 128), 1) < 64
            o_ref[z, pl.ds(start, size), :] = jnp.where(low, a, b).astype(BF)

    def send_first(i, carry):
        put(pl.multiple_of(i * COLS, COLS), COLS, gs[i], gs[i + 12])
        return carry
    lax.fori_loop(0, 12, send_first, 0)

    def send_warped(i, carry):
        both = []
        for t in (i, i + 16):
            right = fs[pl.ds(t, 9)].reshape(9 * COLS, 256)
            value = lax.dot_general(bs[t], right, (((0,), (0,)), ((), ())), preferred_element_type=F32)
            both.append(value[0:WIN] * (1.0 / CH**0.5))
        put(pl.multiple_of(12 * COLS + i * WIN, 16), WIN, both[0], both[1])
        return carry
    lax.fori_loop(0, 16, send_warped, 0)


def cost_back(rx, grad_main, grad_rest):
    vm = pl.BlockSpec(memory_space=pltpu.VMEM)
    return pl.pallas_call(
        cost_back_kernel,
        out_shape=jax.ShapeDtypeStruct((4, PAY, 128), BF),
        in_specs=[vm] * 3,
        out_specs=vm,
        scratch_shapes=[
            pltpu.VMEM((ROWS + 16, COLS, 256), BF),
            pltpu.VMEM((ROWS + 8, 128, 256), BF),
            pltpu.VMEM((ROWS + 8, 9 * COLS, 128), BF),
            pltpu.VMEM((ROWS, COLS, 256), F32),
        ],
        compiler_params=pltpu.CompilerParams(vmem_limit_bytes=40 * 2**20),
        name="cost_back",
    )(rx, grad_main, grad_rest)


def turn_kernel(rp_ref, g1_ref, gw_ref, up_ref, down_ref, turn):
    eye = jnp.where(
        lax.broadcasted_iota(jnp.int32, (128, 128), 0) == lax.broadcasted_iota(jnp.int32, (128, 128), 1), 1.0, 0.0
    ).astype(BF)

    def first(i, carry):
        at = pl.ds(pl.multiple_of(i * COLS, COLS), COLS)
        value = nt(eye, jnp.concatenate([rp_ref[z, at, :] for z in range(4)], axis=0))
        g1_ref[i] = value[0:SLOT]
        g1_ref[i + 12] = value[SLOT:]
        return carry
    lax.fori_loop(0, 12, first, 0)

    def second(i, carry):
        at = pl.ds(pl.multiple_of(12 * COLS + i * WIN, 16), WIN)
        turn[...] = jnp.zeros(turn.shape, F32)
        for z in range(4):
            rows = slice(COLS * z + 4, COLS * z + 4 + WIN)
            turn[rows, :] = turn[rows, :] + rp_ref[z, at, :].astype(F32)
        value = jnp.transpose(turn[8:264, :])
        gw_ref[i] = value[0:SLOT]
        gw_ref[i + 16] = value[SLOT:]
        return carry
    lax.fori_loop(0, 16, second, 0)
    up_ref[...] = gw_ref[0:4].astype(BF)
    down_ref[...] = gw_ref[27:32].astype(BF)


def turn(rp):
    vm = pl.BlockSpec(memory_space=pltpu.VMEM)
    return pl.pallas_call(
        turn_kernel,
        out_shape=(
            jax.ShapeDtypeStruct((ROWS, SLOT, 256), F32),
            jax.ShapeDtypeStruct((ROWS + 8, SLOT, 256), F32),
            jax.ShapeDtypeStruct((4, SLOT, 256), BF),
            jax.ShapeDtypeStruct((5, SLOT, 256), BF),
        ),
        in_specs=[vm],
        out_specs=(vm,) * 4,
        scratch_shapes=[pltpu.VMEM((288, 128), F32)],
        compiler_params=pltpu.CompilerParams(vmem_limit_bytes=32 * 2**20),
        name="turn",
    )(rp)


def warp_back_kernel(gw_ref, from_above, from_below, f2_ref, above_ref, below_ref, g2_ref, gf_ref, full, band):
    first = lax.broadcasted_iota(jnp.int32, (SLOT, 256), 1) == 0
    last = lax.broadcasted_iota(jnp.int32, (SLOT, 256), 1) == 255
    channel = lax.broadcasted_iota(jnp.int32, (SLOT, 256), 0) < CH // 4
    band[0] = above_ref[3]
    band[1 : ROWS + 1] = f2_ref[...]
    band[ROWS + 1] = below_ref[0]
    full[...] = gw_ref[3:28]
    full[0:5] = full[0:5] + from_above[...].astype(F32)
    full[21:25] = full[21:25] + from_below[...].astype(F32)

    def spread(u, x):
        part = u * x
        return (x - part) + jnp.where(first, 0.0, pltpu.roll(part, 1, 1))

    def row(r, carry):
        upper = band[r + 1].astype(F32)
        lower = band[r + 2].astype(F32)
        before = band[r].astype(F32)
        u, v = upper[49:50], upper[50:51]
        grad = full[r + 1]
        g2_ref[r] = spread(u, (1.0 - v) * grad) + spread(before[49:50], before[50:51] * full[r])
        upper_next = jnp.where(last, 0.0, pltpu.roll(upper, 255, 1))
        lower_next = jnp.where(last, 0.0, pltpu.roll(lower, 255, 1))
        to_u = (1.0 - v) * (upper_next - upper) + v * (lower_next - lower)
        to_v = ((1.0 - u) * lower + u * lower_next) - ((1.0 - u) * upper + u * upper_next)
        along = jnp.sum(jnp.where(channel, grad * to_u, 0.0), axis=0, keepdims=True)
        down = jnp.sum(jnp.where(channel, grad * to_v, 0.0), axis=0, keepdims=True)
        gf_ref[r] = jnp.concatenate([along, down, jnp.zeros((6, 256), F32)], axis=0)
        return carry
    lax.fori_loop(0, ROWS, row, 0)


def warp_back(gw, from_above, from_below, f2, above, below):
    vm = pl.BlockSpec(memory_space=pltpu.VMEM)
    return pl.pallas_call(
        warp_back_kernel,
        out_shape=(
            jax.ShapeDtypeStruct((ROWS, SLOT, 256), F32),
            jax.ShapeDtypeStruct((ROWS, 8, 256), F32),
        ),
        in_specs=[vm] * 6,
        out_specs=(vm, vm),
        scratch_shapes=[pltpu.VMEM((ROWS + 1, SLOT, 256), F32), pltpu.VMEM((ROWS + 2, SLOT, 256), BF)],
        compiler_params=pltpu.CompilerParams(vmem_limit_bytes=32 * 2**20),
        name="warp_back",
    )(gw, from_above, from_below, f2, above, below)
WIDE, REST = lane_maps()
GATHER = gather_map()
START = start_map()


def arrange(convs, biases):
    wide = jnp.asarray(WIDE, BF)
    rest = jnp.asarray(REST, BF)
    blocks = []
    rest_blocks = []
    lanes = lax.broadcasted_iota(jnp.int32, (1, 128), 1)
    for n in range(6):
        outs, depth = OUTS[n], DEPTH[n]
        extra = (128, 128, 128, 64, 32, 32)[n] - outs
        weight = convs[n]
        term = lax.dot_general(
            weight, wide[729 - depth :], (((2,), (0,)), ((), ())), preferred_element_type=F32
        ).astype(BF)
        blocks.append(jnp.pad(term, ((0, 0), (0, extra), (0, 0))))
        split = weight.reshape(3, 3, outs, depth)
        total = sum(
            lax.dot_general(
                split[:, dx], rest[dx, 729 - depth :], (((2,), (0,)), ((), ())), preferred_element_type=F32
            )
            for dx in range(3)
        )
        high = biases[n].astype(BF).astype(F32)
        low = biases[n] - high
        bias = jnp.where(lanes == 57, high[:, None], 0.0) + jnp.where(lanes == 58, low[:, None], 0.0)
        total = jnp.concatenate([total[:1], total[1:2] + bias[None], total[2:]], axis=0)
        rest_blocks.append(jnp.pad(total.astype(BF), ((0, 0), (0, extra), (0, 0))))
    return jnp.concatenate(blocks, axis=1), jnp.concatenate(rest_blocks, axis=1)


def ring(axis, steps):
    count = lax.axis_size(axis)
    return [(i, i + steps) for i in range(max(0, -steps), min(count, count - steps))]


def all_sum(value, scalars):
    axes = ("chan", "pix")
    count = lax.axis_size(axes)
    height = value.shape[0] // count
    parts = value.reshape(count, height, 128)
    parts = lax.all_to_all(parts, axes, split_axis=0, concat_axis=0, tiled=True)
    block = jnp.sum(parts.astype(F32), axis=0).astype(BF)
    high = lax.reduce_precision(scalars, 8, 7)
    middle = lax.reduce_precision(scalars - high, 8, 7)
    low = scalars - high - middle
    extra = jnp.stack([high, middle, low]).astype(BF)
    extra = jnp.pad(extra, ((0, 13), (0, 128 - scalars.shape[0])))
    spread = jnp.broadcast_to(jnp.concatenate([block, extra], axis=0)[None], (count, height + 16, 128))
    spread = lax.all_to_all(spread, axes, split_axis=0, concat_axis=0, tiled=True)
    sums = jnp.sum(spread[:, height : height + 3, : scalars.shape[0]].astype(F32), axis=(0, 1))
    return spread[:, :height].reshape(value.shape), sums


def local(
    feat_one, feat_two, up_flow, up_feat, target_flow, valid_mask,
    conv_one, conv_two, conv_three, conv_four, conv_five, flow_head,
    bias_one, bias_two, bias_three, bias_four, bias_five, bias_head,
):
    convs = [conv_one, conv_two, conv_three, conv_four, conv_five, flow_head]
    biases = [bias_one, bias_two, bias_three, bias_four, bias_five, bias_head]
    channels = feat_one.shape[0]
    f2 = jnp.concatenate([feat_two, up_flow, jnp.zeros((SLOT - channels - 2, ROWS, 256), BF)], axis=0)
    f2 = jnp.transpose(f2, (1, 0, 2))
    above = lax.ppermute(f2[ROWS - MD :], "pix", ring("pix", 1))
    below = lax.ppermute(f2[: MD + 1], "pix", ring("pix", -1))
    f1 = jnp.transpose(jnp.pad(feat_one, ((0, SLOT - channels), (0, 0), (0, 0))), (1, 0, 2))
    features = lax.all_to_all(pack(f1, f2, above, below), "chan", split_axis=0, concat_axis=0, tiled=True)
    weight, weight_rest = arrange(convs, biases)

    flow_cols = lax.dynamic_slice_in_dim(up_flow, lax.axis_index("chan") * COLS, COLS, 2)
    high = target_flow.astype(BF)
    low = (target_flow - high.astype(F32)).astype(BF)
    one = jnp.ones((2, ROWS, COLS), BF)
    planes = jnp.concatenate([flow_cols, up_feat, one, valid_mask.astype(BF)[None], high, low], axis=0)
    extra = jnp.pad(jnp.transpose(planes, (1, 2, 0)), ((0, 0), (0, 0), (21, 96)))
    upper, lower = cost_volume(features, extra)
    top = lax.ppermute(lower, "pix", ring("pix", 1))
    bottom = lax.ppermute(upper, "pix", ring("pix", -1))
    tiles = [tile.reshape(27, COLS, 128) for tile in (top, upper, lower, bottom)]
    left = lax.ppermute(
        jnp.concatenate([tile[:, COLS - LEFT :] for tile in tiles], axis=0), "chan", ring("chan", 1)
    )
    right = lax.ppermute(
        jnp.concatenate([tile[:, :LEFT] for tile in tiles], axis=0), "chan", ring("chan", -1)
    )
    acts, slopes, main, rest, grad_main, grad_rest, flow, sums = decode(
        top, upper, lower, bottom, left, right, weight, weight_rest
    )
    returned = lax.all_to_all(
        cost_back(features, grad_main, grad_rest), "chan", split_axis=0, concat_axis=0, tiled=True
    )
    grads = wgrad(slopes, main, rest, acts, jnp.asarray(GATHER, BF))
    scalars = jnp.sum(sums[:, :, 96], axis=1)
    grad_one, partial, to_above, to_below = turn(returned)
    from_above = lax.ppermute(to_below, "pix", ring("pix", 1))
    from_below = lax.ppermute(to_above, "pix", ring("pix", -1))
    grad_two, grad_flow = warp_back(partial, from_above, from_below, f2, above, below)
    grad_feat_one = jnp.transpose(grad_one[:, :channels], (1, 0, 2))
    grad_feat_two = jnp.transpose(grad_two[:, :channels], (1, 0, 2))
    flow_parts = jnp.transpose(grad_flow[:, :2].reshape(ROWS, 2, 4, COLS), (2, 1, 0, 3)).astype(BF)
    flow_parts = lax.all_to_all(flow_parts, "chan", split_axis=0, concat_axis=0, tiled=True)

    def core(value):
        return jnp.transpose(value.reshape(ROWS, PITCH, -1)[:, LEFT : LEFT + COLS], (2, 0, 1))

    flow_out = core(flow[:, 96:98])
    small = core(grad_rest[:, 21:25])
    grad_up_flow = jnp.sum(flow_parts.astype(F32), axis=0) + small[:2]
    summed, scalars = all_sum(grads, scalars)
    weight_grads, bias_grads = unpack(summed)
    bias_grads = [bias_grads[ROW0[n] : ROW0[n] + OUTS[n], 89] for n in range(6)]
    return (flow_out, scalars, grad_feat_one, grad_feat_two, grad_up_flow, small[2:], *weight_grads, *bias_grads)


def solution(mesh):
    return jax.shard_map(
        local,
        mesh=mesh,
        in_specs=(
            P("chan", "pix", None),
            P("chan", "pix", None),
            P(None, "pix", None),
            P(None, "pix", "chan"),
            P(None, "pix", "chan"),
            P("pix", "chan"),
        )
        + (P(),) * 12,
        out_specs=(
            P(None, "pix", "chan"),
            P(),
            P("chan", "pix", None),
            P("chan", "pix", None),
            P(None, "pix", "chan"),
            P(None, "pix", "chan"),
        )
        + (P(),) * 12,
        check_vma=False,
    )
```

```python
import jax
import jax.numpy as jnp
import numpy as np
from jax import lax
from jax.experimental import pallas as pl
from jax.experimental.pallas import tpu as pltpu
from jax.sharding import PartitionSpec as P

CH = 196
MD = 4
CH_SLOT = 49
OUTS = (128, 128, 96, 64, 32, 2)
ROW0 = (0, 128, 256, 384, 448, 480)
DEPTH = (281, 409, 537, 633, 697, 729)


def start_lane(channel):
    if channel < 81:
        dy, dx = divmod(channel, 9)
        if dy < 4:
            return 0, 64 * dy + 49 + dx
        if dy < 8:
            if dx < 6:
                return 0, 64 * (dy - 4) + 58 + dx
            return 1, 3 * (dy - 4) + dx - 6
        return 1, 12 + dx
    if channel < 277:
        slot, inner = divmod(channel - 81, CH_SLOT)
        return 0, 64 * slot + inner
    return 1, 21 + channel - 277


def lane_maps():
    wide = np.zeros((729, 768), np.float32)
    rest = np.zeros((729, 128), np.float32)
    for c in range(729):
        if c < 32:
            wide[c, 704 + c] = 1
        elif c < 96:
            wide[c, 640 + c - 32] = 1
        elif c < 192:
            wide[c, 512 + c - 96] = 1
        elif c < 320:
            wide[c, 384 + c - 192] = 1
        elif c < 448:
            wide[c, 256 + c - 320] = 1
        else:
            block, lane = start_lane(c - 448)
            if block == 0:
                wide[c, lane] = 1
            else:
                rest[c, lane] = 1
    return wide, rest


def gather_map():
    table = np.zeros((1024, 768), np.float32)
    for c in range(281):
        block, lane = start_lane(c)
        table[288 * block + lane, 448 + c] = 1
    table[288 + 25, 729] = 1
    for i in range(128):
        table[384 + i, 320 + i] = 1
        table[512 + i, 192 + i] = 1
    for i in range(96):
        table[640 + i, 96 + i] = 1
    for i in range(64):
        table[768 + i, 32 + i] = 1
    for i in range(32):
        table[896 + 64 + i, i] = 1
    return table

CH = 196
MD = 4
BF = jnp.bfloat16
F32 = jnp.float32
HALO = 12
PITCH = 96
ROWS = 24
COLS = 64
LEFT = 16
WROWS = ROWS + 2 * HALO
NPX = WROWS * PITCH
GUARD = 16
VMEM_MB = 62


def nt(a, b):
    return lax.dot_general(a, b, (((1,), (1,)), ((), ())), preferred_element_type=F32)


def nn(a, b):
    return lax.dot_general(a, b, (((1,), (0,)), ((), ())), preferred_element_type=F32)


def decode_kernel(
    top_ref, h0_ref, h1_ref, bottom_ref, left_ref, right_ref, w_ref, wr_ref,
    a_ref, g_ref, xm_ref, xr_ref, dm_ref, dr_ref, flow_ref, met_ref,
    xs, xq, sh, pre, part, mk, sems,
):
    lane = lax.broadcasted_iota(jnp.int32, (PITCH, 128), 1)
    core = pl.ds(HALO * PITCH, ROWS * PITCH)

    def rows(lo, hi, body, unroll=2):
        def step(i, carry):
            for u in range(unroll):
                body(pl.multiple_of(lo * PITCH + (i * unroll + u) * PITCH, PITCH))
            return carry
        lax.fori_loop(0, (hi - lo) // unroll, step, 0)

    def put_shifted(dst, p, lanes, value):
        height = value.shape[0]
        dst[0, pl.ds(p, PITCH), lanes] = pltpu.roll(value, 1, 0).astype(BF)
        dst[1, pl.ds(p, PITCH), lanes] = value.astype(BF)
        dst[2, pl.ds(p, PITCH), lanes] = pltpu.roll(value, height - 1, 0).astype(BF)

    def chunked(lo, hi, count, body):
        size = (hi - lo) * PITCH // count

        def step(i, carry):
            body(pl.multiple_of(lo * PITCH + i * size, 16), size)
            return carry
        lax.fori_loop(0, count, step, 0)

    for h, tile in enumerate((top_ref, h0_ref, h1_ref, bottom_ref)):
        def main_rows(i, carry, h=h, tile=tile):
            p = pl.multiple_of((12 * h + i) * PITCH, PITCH)
            for half in range(2):
                at = pl.multiple_of((12 * half + i) * COLS, COLS)
                value = jnp.concatenate(
                    [
                        left_ref[27 * h + 12 * half + i].astype(F32),
                        tile[pl.ds(at, COLS), :].astype(F32),
                        right_ref[27 * h + 12 * half + i].astype(F32),
                    ],
                    axis=0,
                )
                put_shifted(xs, p, slice(128 * half, 128 * half + 128), value)
            return carry
        lax.fori_loop(0, 12, main_rows, 0)

        def rest_rows(b, carry, h=h, tile=tile):
            packed = jnp.concatenate(
                [
                    left_ref[27 * h + 24 + b].astype(F32),
                    tile[pl.ds(pl.multiple_of(1536 + b * COLS, COLS), COLS), :].astype(F32),
                    right_ref[27 * h + 24 + b].astype(F32),
                ],
                axis=0,
            )
            for a in range(4):
                p = pl.multiple_of((12 * h + 3 * a + b) * PITCH, PITCH)
                value = jnp.where(lane < 32, pltpu.roll(packed, (128 - 32 * a) % 128, 1), 0.0)
                mk[pl.ds(p, PITCH), :] = jnp.broadcast_to(value[:, 25:26], (PITCH, 128))
                low = pltpu.roll(value, 1, 0)
                mid = pltpu.roll(value, 32, 1)
                high = pltpu.roll(pltpu.roll(value, PITCH - 1, 0), 64, 1)
                xq[pl.ds(p, PITCH), :] = (low + mid + high).astype(BF)
            return carry
        lax.fori_loop(0, 3, rest_rows, 0)

    keep = [
        pltpu.make_async_copy(xs.at[1, core, :], xm_ref, sems.at[1]),
        pltpu.make_async_copy(xq.at[core, :], xr_ref, sems.at[2]),
    ]
    for copy in keep:
        copy.start()

    def start_sums(p, size):
        left = jnp.concatenate([xq[pl.ds(p + PITCH * (dy - 1), size), :] for dy in range(3)], axis=1)
        total = nt(left, jnp.concatenate([wr_ref[dy] for dy in range(3)], axis=1))
        for dy in range(3):
            at = p + PITCH * (dy - 1)
            for dx in range(3):
                total = total + nt(xs[dx, pl.ds(at, size), :], w_ref[3 * dy + dx, :, 0:256])
        pre[pl.ds(p, size), :] = total
    chunked(1, WROWS - 1, 3, start_sums)

    first_lane = [0, 128, 256, 384, 384]
    lanes_of = [(0, 128), (0, 128), (0, 96), (0, 64), (64, 96)]
    kept = []
    for layer in range(5):
        block = slice(first_lane[layer], first_lane[layer] + 128)
        from_lane, to_lane = lanes_of[layer]
        inside = (lane >= from_lane) & (lane < to_lane)
        lo, hi = layer + 1, WROWS - layer - 1
        piece = min(layer, 3)
        lanes = slice(128 * piece, 128 * piece + 128)
        if layer == 4:
            kept[3].wait()

        def activate(p, block=block, inside=inside, lanes=lanes, layer=layer):
            value = pre[pl.ds(p, PITCH), block]
            sig = 0.5 * jnp.tanh(0.5 * value) + 0.5
            live = mk[pl.ds(p, PITCH), :] > 0.0
            if layer >= 3:
                live = live & inside
            act = value * sig
            slope = jnp.where(live, sig + act * (1.0 - sig), 0.0)
            if layer >= 3:
                slope = jnp.where(inside, slope, value)
            pre[pl.ds(p, PITCH), block] = slope
            put_shifted(sh, p, lanes, jnp.where(live, act, 0.0))
        rows(lo, hi, activate)
        copy = pltpu.make_async_copy(
            sh.at[1, core, lanes], a_ref.at[:, 128 * layer : 128 * layer + 128], sems.at[3 + layer]
        )
        copy.start()
        kept.append(copy)
        out0 = min(128 * (layer + 1), 384)

        def add_sums(p, size, piece=piece, out0=out0):
            lanes = slice(128 * piece, 128 * piece + 128)
            left = jnp.concatenate(
                [sh[dx, pl.ds(p + PITCH * (dy - 1), size), lanes] for dy in range(3) for dx in range(3)], axis=1
            )
            right = jnp.concatenate(
                [w_ref[k, out0:512, 256 + 128 * piece : 384 + 128 * piece] for k in range(9)], axis=1
            )
            pre[pl.ds(p, size), out0:512] = pre[pl.ds(p, size), out0:512] + nt(left, right)
        chunked(lo + 1, hi - 1, 3, add_sums)

    is_flow = (lane >= 96) & (lane < 98)
    column = lax.broadcasted_iota(jnp.int32, (PITCH, 128), 0)
    core_column = (column >= LEFT) & (column < LEFT + COLS)
    met_ref[...] = jnp.zeros((3, PITCH, 128), F32)
    kept[0].wait()
    kept[1].wait()
    kept[2].wait()
    kept[4].wait()

    def loss(p):
        flow = pre[pl.ds(p, PITCH), 384:512]
        rest = xq[pl.ds(p, PITCH), :].astype(F32)
        target = pltpu.roll(rest, 96 - 60, 1) + pltpu.roll(rest, 96 - 62, 1)
        diff = jnp.where(is_flow, flow - target, 0.0)
        square = diff * diff
        other = jnp.where(lane == 96, pltpu.roll(square, 127, 1), pltpu.roll(square, 1, 1))
        error = jnp.sqrt(square + other + 1.0)
        mask = jnp.broadcast_to(rest[:, 59:60], (PITCH, 128))
        put_shifted(sh, p, slice(384, 512), jnp.where(is_flow, mask * diff / error, 0.0))
        return flow, mask, error

    def loss_rim(p):
        loss(p)

    def loss_core(p):
        flow, mask, error = loss(p)
        q = pl.multiple_of(p - HALO * PITCH, PITCH)
        flow_ref[pl.ds(q, PITCH), :] = flow
        mask = jnp.where(core_column, mask, 0.0)
        met_ref[0] += mask * (error - 1.0)
        met_ref[1] += mask / (1.0 + jnp.exp(-4.0 * (error - 2.0)))
        met_ref[2] += mask

    rows(6, HALO, loss_rim)
    rows(HALO, HALO + ROWS, loss_core)
    rows(HALO + ROWS, WROWS - 6, loss_rim)

    for layer in range(4, -1, -1):
        lo, hi = HALO - layer - 1, HALO + ROWS + layer + 1
        piece = min(layer, 3)
        lanes = slice(128 * piece, 128 * piece + 128)
        out0 = min(128 * (layer + 1), 384)
        block = slice(first_lane[layer], first_lane[layer] + 128)
        from_lane, to_lane = lanes_of[layer]
        inside = (lane >= from_lane) & (lane < to_lane)
        c0 = 256 + 128 * piece

        def back(p, size, out0=out0, c0=c0):
            left = jnp.concatenate(
                [sh[2 - dx, pl.ds(p - PITCH * (dy - 1), size), out0:512] for dy in range(3) for dx in range(3)], axis=1
            )
            right = jnp.concatenate([w_ref[k, out0:512, c0 : c0 + 128] for k in range(9)], axis=0)
            part[pl.ds(p, size), :] = nn(left, right)
        chunked(lo, hi, 3, back)

        def slope(p, layer=layer, block=block, inside=inside, lanes=lanes):
            value = part[pl.ds(p, PITCH), :] * pre[pl.ds(p, PITCH), block]
            if layer >= 3:
                value = jnp.where(inside, value, sh[1, pl.ds(p, PITCH), lanes].astype(F32))
            put_shifted(sh, p, lanes, value)
        rows(lo, hi, slope)

    copy = pltpu.make_async_copy(sh.at[:, pl.ds((HALO - 1) * PITCH, (ROWS + 2) * PITCH), :], g_ref, sems.at[0])
    keep.append(copy)
    copy.start()

    def back_rest(p, size):
        total = None
        for dy in range(3):
            term = nn(sh[1, pl.ds(p - PITCH * (dy - 1), size), :], wr_ref[dy])
            total = term if total is None else total + term
        part[pl.ds(p, size), :] = total
    chunked(HALO, HALO + ROWS, 6, back_rest)

    def rest_out(p):
        q = pl.multiple_of(p - HALO * PITCH, PITCH)
        value = part[pl.ds(p, PITCH), :]
        dr_ref[pl.ds(q, PITCH), :] = (
            pltpu.roll(value, PITCH - 1, 0)
            + pltpu.roll(value, 96, 1)
            + pltpu.roll(pltpu.roll(value, 1, 0), 64, 1)
        )
    rows(HALO, HALO + ROWS, rest_out)

    def back_main(p, size):
        total = None
        for dy in range(3):
            at = p - PITCH * (dy - 1)
            for dx in range(3):
                term = nn(sh[2 - dx, pl.ds(at, size), :], w_ref[3 * dy + dx, :, 0:256])
                total = term if total is None else total + term
        q = pl.multiple_of(p - HALO * PITCH, 16)
        dm_ref[pl.ds(q, size), :] = total.astype(BF)
    chunked(HALO, HALO + ROWS, 6, back_main)
    for copy in keep:
        copy.wait()


def decode(top, h0, h1, bottom, left, right, w, wr):
    size = ROWS * PITCH
    vm = pl.BlockSpec(memory_space=pltpu.VMEM)
    hbm = pl.BlockSpec(memory_space=pl.ANY)
    return pl.pallas_call(
        decode_kernel,
        out_shape=(
            jax.ShapeDtypeStruct((size, 640), BF),
            jax.ShapeDtypeStruct((3, (ROWS + 2) * PITCH, 512), BF),
            jax.ShapeDtypeStruct((size, 256), BF),
            jax.ShapeDtypeStruct((size, 128), BF),
            jax.ShapeDtypeStruct((size, 256), BF),
            jax.ShapeDtypeStruct((size, 128), F32),
            jax.ShapeDtypeStruct((size, 128), F32),
            jax.ShapeDtypeStruct((3, PITCH, 128), F32),
        ),
        in_specs=[vm] * 8,
        out_specs=(hbm, hbm, hbm, hbm, vm, vm, vm, vm),
        scratch_shapes=[
            pltpu.VMEM((3, NPX, 256), BF),
            pltpu.VMEM((NPX, 128), BF),
            pltpu.VMEM((3, NPX, 512), BF),
            pltpu.VMEM((NPX, 512), F32),
            pltpu.VMEM((NPX, 128), F32),
            pltpu.VMEM((NPX, 128), F32),
            pltpu.SemaphoreType.DMA((8,)),
        ],
        compiler_params=pltpu.CompilerParams(vmem_limit_bytes=VMEM_MB * 2**20),
        name="decode",
    )(top, h0, h1, bottom, left, right, w, wr)


def arrange_kernel(c1, c2, c3, c4, c5, c6, wide_ref, rest_ref, bias_ref, w_ref, wr_ref):
    w_ref[:, 352:384, :] = jnp.zeros((9, 32, 768), BF)
    w_ref[:, 480:512, :] = jnp.zeros((9, 32, 768), BF)
    wr_ref[:, 352:384, :] = jnp.zeros((3, 32, 128), BF)
    wr_ref[:, 480:512, :] = jnp.zeros((3, 32, 128), BF)
    lane = lax.broadcasted_iota(jnp.int32, (512, 128), 1)
    bias = bias_ref[...]
    high = bias.astype(BF).astype(F32)
    bias = jnp.where(lane == 57, high, jnp.where(lane == 58, bias - high, 0.0))

    for n, ref in enumerate((c1, c2, c3, c4, c5, c6)):
        outs, depth = OUTS[n], DEPTH[n]
        rows = slice(ROW0[n], ROW0[n] + outs)
        wide = wide_ref[729 - depth :, :]
        rest = rest_ref[729 - depth :, :]
        dims = (((0,), (0,)), ((), ())) if n < 2 else (((1,), (0,)), ((), ()))
        for dy in range(3):
            total = bias[rows] if dy == 1 else jnp.zeros((outs, 128), F32)
            for dx in range(3):
                weight = ref[3 * dy + dx]
                w_ref[3 * dy + dx, rows, :] = lax.dot_general(
                    weight, wide, dims, preferred_element_type=F32
                ).astype(BF)
                part = lax.dot_general(weight, rest, dims, preferred_element_type=F32)
                total = total + (pltpu.roll(part, 32 * dx, 1) if dx else part)
            wr_ref[dy, rows, :] = total.astype(BF)


def arrange(convs, biases):
    vm = pl.BlockSpec(memory_space=pltpu.VMEM)
    bias = jnp.concatenate(
        [biases[0], biases[1], biases[2], jnp.zeros((32,), F32), biases[3], biases[4], biases[5], jnp.zeros((30,), F32)]
    ).reshape(512, 1)
    turned = [jnp.transpose(convs[0], (0, 2, 1)), jnp.transpose(convs[1], (0, 2, 1))]
    return pl.pallas_call(
        arrange_kernel,
        out_shape=(jax.ShapeDtypeStruct((9, 512, 768), BF), jax.ShapeDtypeStruct((3, 512, 128), BF)),
        in_specs=[vm] * 9,
        out_specs=(vm, vm),
        compiler_params=pltpu.CompilerParams(vmem_limit_bytes=40 * 2**20),
        cost_estimate=pl.CostEstimate(flops=4 * 10**9, bytes_accessed=16 * 10**6, transcendentals=0),
        name="arrange",
    )(*turned, *convs[2:], jnp.asarray(WIDE, BF), jnp.asarray(REST, BF), bias)

TILE_ROWS = 2048
TOTAL_ROWS = 9 * TILE_ROWS
HALF_ROWS = TOTAL_ROWS // 2


def tn(a, b):
    return lax.dot_general(a, b, (((0,), (0,)), ((), ())), preferred_element_type=F32)


def wgrad_kernel(core_ref, g_ref, xm_ref, xr_ref, a_ref, qp_ref, own_ref, sent_ref, xp, o_ref, sems):
    column = lax.broadcasted_iota(jnp.int32, (PITCH, 768), 0)
    core = (column >= LEFT) & (column < LEFT + COLS)
    core = jnp.concatenate([core] * 4, axis=0)
    size = 4 * PITCH

    def gather(i, carry):
        at = pl.ds(pl.multiple_of(i * size, size), size)
        left = jnp.concatenate([xm_ref[at, :], xr_ref[at, :], a_ref[at, :]], axis=1)
        xp[at, :] = jnp.where(core, nn(left, qp_ref[...]), 0.0).astype(BF)
        return carry
    lax.fori_loop(0, ROWS // 4, gather, 0)

    for k in range(9):
        dy, dx = divmod(k, 3)
        at = pl.ds(PITCH * (2 - dy), ROWS * PITCH)
        base = TILE_ROWS * k
        value = tn(g_ref[2 - dx, at, 0:256], xp[:, 256:768])
        low = value.astype(BF)
        for t in range(3):
            o_ref[base + 128 * t : base + 128 * t + 128, :] = low[0:128, 128 * t + 128 : 128 * t + 256]
        for t in range(4):
            o_ref[base + 384 + 128 * t : base + 512 + 128 * t, :] = low[128:256, 128 * t : 128 * t + 128]
        value = tn(g_ref[2 - dx, at, 256:512], xp[...])
        low = value.astype(BF)
        for t in range(5):
            o_ref[base + 896 + 96 * t : base + 992 + 96 * t, :] = low[0:96, 128 * t + 128 : 128 * t + 256]
        for t in range(6):
            o_ref[base + 1376 + 112 * t : base + 1488 + 112 * t, :] = low[128:240, 128 * t : 128 * t + 128]
    core = core_ref[0]
    copies = [
        pltpu.make_async_copy(
            o_ref.at[pl.ds(pl.multiple_of(at * HALF_ROWS, HALF_ROWS), HALF_ROWS), :], target, sems.at[n]
        )
        for n, (target, at) in enumerate(((own_ref, core), (sent_ref, 1 - core)))
    ]
    for copy in copies:
        copy.start()
    for copy in copies:
        copy.wait()


def wgrad(core, g, xm, xr, a, qp):
    vm = pl.BlockSpec(memory_space=pltpu.VMEM)
    hbm = pl.BlockSpec(memory_space=pl.ANY)
    return pl.pallas_call(
        wgrad_kernel,
        out_shape=(jax.ShapeDtypeStruct((HALF_ROWS, 128), BF),) * 2,
        in_specs=[pl.BlockSpec(memory_space=pltpu.SMEM)] + [vm] * 5,
        out_specs=(hbm, hbm),
        scratch_shapes=[
            pltpu.VMEM((ROWS * PITCH, 768), BF),
            pltpu.VMEM((TOTAL_ROWS, 128), BF),
            pltpu.SemaphoreType.DMA((2,)),
        ],
        compiler_params=pltpu.CompilerParams(vmem_limit_bytes=VMEM_MB * 2**20),
        name="wgrad",
    )(core, g, xm, xr, a, qp)

NOTE = 16


def half_sum_kernel(own_ref, got_ref, note_ref, got_note_ref, o_ref):
    count, height = o_ref.shape[0], o_ref.shape[1] - NOTE
    notes = jnp.concatenate([note_ref[0:8].astype(F32), got_note_ref[0:8].astype(F32)], axis=0).astype(BF)
    for b in range(count):
        rows = slice(height * b, height * (b + 1))
        o_ref[b, 0:height] = (own_ref[rows, :].astype(F32) + got_ref[rows, :].astype(F32)).astype(BF)
        o_ref[b, height:] = notes


def half_sum(own, got, note, got_note, count):
    height = HALF_ROWS // count
    steps = 4
    block = HALF_ROWS // steps
    return pl.pallas_call(
        half_sum_kernel,
        grid=(steps,),
        in_specs=[
            pl.BlockSpec((block, 128), lambda i: (i, 0)),
            pl.BlockSpec((block, 128), lambda i: (i, 0)),
            pl.BlockSpec((NOTE, 128), lambda i: (0, 0)),
            pl.BlockSpec((NOTE, 128), lambda i: (0, 0)),
        ],
        out_specs=pl.BlockSpec((count // steps, height + NOTE, 128), lambda i: (i, 0, 0)),
        out_shape=jax.ShapeDtypeStruct((count, height + NOTE, 128), BF),
        name="half_sum",
    )(own, got, note, got_note)


def spread_kernel(parts_ref, o_ref, note_ref):
    count, height = o_ref.shape[0], o_ref.shape[1]

    def add(b, carry):
        total, notes = carry
        return total + parts_ref[b, 0:height].astype(F32), notes + parts_ref[b, height:].astype(F32)
    zero = (jnp.zeros((height, 128), F32), jnp.zeros((NOTE, 128), F32))
    total, notes = lax.fori_loop(0, count, add, zero)
    note_ref[...] = notes
    total = total.astype(BF)

    def put(b, carry):
        o_ref[b] = total
        return carry
    lax.fori_loop(0, count, put, 0)


def spread_total(parts):
    count, height, _ = parts.shape
    vm = pl.BlockSpec(memory_space=pltpu.VMEM)
    return pl.pallas_call(
        spread_kernel,
        out_shape=(
            jax.ShapeDtypeStruct((count, height - NOTE, 128), BF),
            jax.ShapeDtypeStruct((NOTE, 128), F32),
        ),
        in_specs=[vm],
        out_specs=(vm, vm),
        compiler_params=pltpu.CompilerParams(vmem_limit_bytes=32 * 2**20),
        name="spread_total",
    )(parts)


def unpack_kernel(core_ref, mine_ref, other_ref, o1, o2, o3, o4, o5, o6, b_ref, all_ref, sems):
    k = pl.program_id(0)

    @pl.when(k == 0)
    def _():
        core = core_ref[0]
        copies = [
            pltpu.make_async_copy(
                source, all_ref.at[pl.ds(pl.multiple_of(at * HALF_ROWS, HALF_ROWS), HALF_ROWS), :], sems.at[n]
            )
            for n, (source, at) in enumerate(((mine_ref, core), (other_ref, 1 - core)))
        ]
        for copy in copies:
            copy.start()
        for copy in copies:
            copy.wait()
    first = pl.multiple_of(k * TILE_ROWS, TILE_ROWS)

    def tiles(base, height, count):
        return jnp.concatenate(
            [all_ref[pl.ds(first + base + height * t, height), :].astype(F32) for t in range(count)], axis=1
        )
    o1[0] = jnp.transpose(tiles(0, 128, 3))[64 : 64 + 281]
    o2[0] = jnp.transpose(tiles(384, 128, 4))[64 : 64 + 409]
    o3[0] = tiles(896, 96, 5)[:, 64 : 64 + 537]
    last = tiles(1376, 112, 6)
    o4[0] = last[0:64, 96:729]
    o5[0] = last[64:96, 32:729]
    o6[0] = last[96:98, 0:729]

    @pl.when(k == 4)
    def _():
        b_ref[0:128, :] = tiles(256, 128, 1)
        b_ref[128:256, :] = tiles(768, 128, 1)
        b_ref[256:352, :] = tiles(1280, 96, 1)
        b_ref[352:384, :] = jnp.zeros((32, 128), F32)
        b_ref[384:496, :] = last[:, 640:768]
        b_ref[496:512, :] = jnp.zeros((16, 128), F32)


def unpack(core, mine, other):
    shapes = ((281, 128), (409, 128), (96, 537), (64, 633), (32, 697), (2, 729))
    hbm = pl.BlockSpec(memory_space=pl.ANY)
    results = pl.pallas_call(
        unpack_kernel,
        grid_spec=pltpu.PrefetchScalarGridSpec(
            num_scalar_prefetch=1,
            grid=(9,),
            in_specs=[hbm, hbm],
            out_specs=tuple(pl.BlockSpec((1,) + s, lambda k, core: (k, 0, 0)) for s in shapes)
            + (pl.BlockSpec((512, 128), lambda k, core: (0, 0)),),
            scratch_shapes=[pltpu.VMEM((TOTAL_ROWS, 128), BF), pltpu.SemaphoreType.DMA((2,))],
        ),
        out_shape=tuple(jax.ShapeDtypeStruct((9,) + s, F32) for s in shapes)
        + (jax.ShapeDtypeStruct((512, 128), F32),),
        compiler_params=pltpu.CompilerParams(vmem_limit_bytes=32 * 2**20),
        name="unpack",
    )(core, mine, other)
    grads = list(results[:6])
    grads[0] = jnp.transpose(grads[0], (0, 2, 1))
    grads[1] = jnp.transpose(grads[1], (0, 2, 1))
    return grads, results[6]


SWAP = [(0, 1), (1, 0)]
CHIPS = ("chan", "xy")


def chip_parts(own, sent, scalars):
    high = lax.reduce_precision(scalars, 8, 7)
    middle = lax.reduce_precision(scalars - high, 8, 7)
    low = scalars - high - middle
    note = jnp.stack([high, middle, low]).astype(BF)
    note = jnp.pad(note, ((0, NOTE - 3), (0, 128 - scalars.shape[0])))
    got_note = lax.ppermute(note, "core", SWAP)
    got = lax.ppermute(sent, "core", SWAP)
    return half_sum(own, got, note, got_note, lax.axis_size(CHIPS))


def sum_parts(core, parts):
    spread, notes = spread_total(parts)
    mine = lax.all_to_all(spread, CHIPS, split_axis=0, concat_axis=0, tiled=True).reshape(HALF_ROWS, 128)
    other = lax.ppermute(mine, "core", SWAP)
    grads, biases = unpack(core, mine, other)
    return grads, biases, jnp.sum(notes[:, :3], axis=0)

SLOT = 64
WIN = 80
PAY = 12 * COLS + 16 * WIN
HALF = 27 * COLS


def slanted(x, shift):
    shift = shift % 128
    if shift % 8:
        x = pltpu.roll(x, shift % 8, 1)
    return pltpu.roll(x, shift - shift % 8, 1, stride=1, stride_axis=0)


def two_rows(lane, parts):
    swap = [pltpu.roll(part, 64, 1) for part in parts]
    first = [jnp.where(lane < 64, parts[2 * h], swap[2 * h + 1]) for h in range(2)]
    second = [jnp.where(lane < 64, swap[2 * h], parts[2 * h + 1]) for h in range(2)]
    return jnp.concatenate(first, axis=1), jnp.concatenate(second, axis=1)


def pack_kernel(f1_ref, f2_ref, above_ref, below_ref, o_ref, band, turn):
    eye = jnp.where(
        lax.broadcasted_iota(jnp.int32, (256, 256), 0) == lax.broadcasted_iota(jnp.int32, (256, 256), 1), 1.0, 0.0
    ).astype(BF)
    back = jnp.where(
        lax.broadcasted_iota(jnp.int32, (256, 256), 0) + lax.broadcasted_iota(jnp.int32, (256, 256), 1) == 255, 1.0, 0.0
    ).astype(BF)
    last = lax.broadcasted_iota(jnp.int32, (SLOT, 256), 1) == 255
    channel = lax.broadcasted_iota(jnp.int32, (SLOT, 256), 0) < CH // 4
    band[0:MD] = above_ref[...]
    band[MD : MD + ROWS] = f2_ref[...]
    band[MD + ROWS :] = below_ref[...]
    turn[...] = jnp.zeros(turn.shape, F32)

    def first(i, carry):
        both = jnp.concatenate([f1_ref[i], f1_ref[i + 12]], axis=0)
        value = nt(back, both).astype(BF)
        for z in range(4):
            o_ref[z, pl.ds(pl.multiple_of(i * COLS, COLS), COLS), :] = value[192 - COLS * z : 256 - COLS * z]
        return carry
    lax.fori_loop(0, 12, first, 0)

    def warped(t):
        upper = band[t].astype(F32)
        lower = band[t + 1].astype(F32)
        u = upper[49:50]
        v = upper[50:51]

        def across(x):
            return (1.0 - u) * x + u * jnp.where(last, 0.0, pltpu.roll(x, 255, 1))
        value = (1.0 - v) * across(upper) + v * across(lower)
        return jnp.where(channel, value, 0.0).astype(BF)

    def second(i, carry):
        both = jnp.concatenate([warped(i), warped(i + 16)], axis=0)
        turn[8:264, :] = nt(eye, both)
        for z in range(4):
            start = pl.multiple_of(12 * COLS + i * WIN, 16)
            o_ref[z, pl.ds(start, WIN), :] = turn[COLS * z + 4 : COLS * z + 4 + WIN, :].astype(BF)
        return carry
    lax.fori_loop(0, 16, second, 0)


def pack(f1, f2, above, below):
    vm = pl.BlockSpec(memory_space=pltpu.VMEM)
    return pl.pallas_call(
        pack_kernel,
        out_shape=jax.ShapeDtypeStruct((4, PAY, 128), BF),
        in_specs=[vm] * 4,
        out_specs=vm,
        scratch_shapes=[pltpu.VMEM((33, SLOT, 256), BF), pltpu.VMEM((288, 128), F32)],
        compiler_params=pltpu.CompilerParams(vmem_limit_bytes=32 * 2**20),
        name="pack",
    )(f1, f2, above, below)


def flip_matrix():
    total = lax.broadcasted_iota(jnp.int32, (COLS, COLS), 0) + lax.broadcasted_iota(jnp.int32, (COLS, COLS), 1)
    return jnp.where(total == COLS - 1, 1.0, 0.0).astype(BF)


def read_features(rx_ref, lane, first_rows, warped_rows):
    def first(i, carry):
        at = pl.ds(pl.multiple_of(i * COLS, COLS), COLS)
        one, two = two_rows(lane[:COLS], [rx_ref[q, at, :].astype(F32) for q in range(4)])
        first_rows(i, one.astype(BF))
        first_rows(i + 12, two.astype(BF))
        return carry
    lax.fori_loop(0, 12, first, 0)

    def second(i, carry):
        at = pl.ds(pl.multiple_of(12 * COLS + i * WIN, 16), WIN)
        one, two = two_rows(lane[:WIN], [rx_ref[q, at, :].astype(F32) for q in range(4)])
        warped_rows(i, one.astype(BF))
        warped_rows(i + 16, two.astype(BF))
        return carry
    lax.fori_loop(0, 16, second, 0)


def flip_four():
    i = lax.broadcasted_iota(jnp.int32, (4 * COLS, 4 * COLS), 0)
    j = lax.broadcasted_iota(jnp.int32, (4 * COLS, 4 * COLS), 1)
    here = ((i & (COLS - 1)) + (j & (COLS - 1)) == COLS - 1) & ((i & -COLS) == (j & -COLS))
    return jnp.where(here, 1.0, 0.0).astype(BF)


def cost_kernel(rx_ref, ex_ref, h0_ref, h1_ref, fs, ws, ms, vs, rs):
    lane = lax.broadcasted_iota(jnp.int32, (128, 128), 1)

    def put_first(i, value):
        fs[i] = value

    def put_warped(i, value):
        ws[i, 0:WIN] = value
    read_features(rx_ref, lane, put_first, put_warped)
    lane = lane[:COLS]
    flip = flip_four()

    for half, out in ((0, h0_ref), (1, h1_ref)):
        def group(g, carry, half=half, out=out):
            i = 12 * half + 4 * g
            ms[...] = nt(fs[pl.ds(i, 4)].reshape(4 * COLS, 256), ws[pl.ds(i, 12)].reshape(12 * 128, 256))
            for r in range(4):
                rows = slice(COLS * r, COLS * r + COLS)

                def band(dy, t, lo, hi, value, r=r, rows=rows):
                    block = slanted(ms[rows, 128 * (r + dy) : 128 * (r + dy) + 128], t - 63)
                    return jnp.where((lane >= lo) & (lane < hi), block * (1.0 / CH**0.5), value)
                for h in range(2):
                    value = fs[i + r, :, 128 * h : 128 * h + 128].astype(F32)
                    for s in range(2):
                        at = 64 * s + 49
                        value = band(2 * h + s, at, at, at + 9, value)
                        value = band(4 + 2 * h + s, at + 9, at + 9, at + 15, value)
                    vs[rows, 128 * h : 128 * h + 128] = value.astype(BF)
                value = jnp.zeros((COLS, 128), F32)
                for a in range(4):
                    value = band(4 + a, 3 * a - 6, 3 * a, 3 * a + 3, value)
                vs[rows, 256:384] = band(8, 12, 12, 21, value).astype(BF)
            turned = nn(flip, vs[...])
            for h in range(2):
                at = pl.multiple_of(768 * h + 4 * g * COLS, 4 * COLS)
                out[pl.ds(at, 4 * COLS), :] = turned[:, 128 * h : 128 * h + 128].astype(BF)
            rs[pl.ds(i, 4)] = turned[:, 256:384].reshape(4, COLS, 128) + ex_ref[pl.ds(i, 4)].astype(F32)
            return carry
        lax.fori_loop(0, 3, group, 0)
    for half, out in ((0, h0_ref), (1, h1_ref)):
        for b in range(3):
            total = rs[12 * half + b]
            for a in range(1, 4):
                total = total + pltpu.roll(rs[12 * half + 3 * a + b], 32 * a, 1)
            out[1536 + COLS * b : 1536 + COLS * b + COLS, :] = total.astype(BF)


def cost_volume(rx, extra):
    vm = pl.BlockSpec(memory_space=pltpu.VMEM)
    return pl.pallas_call(
        cost_kernel,
        out_shape=(jax.ShapeDtypeStruct((HALF, 128), BF),) * 2,
        in_specs=[vm] * 2,
        out_specs=(vm, vm),
        scratch_shapes=[
            pltpu.VMEM((ROWS, COLS, 256), BF),
            pltpu.VMEM((ROWS + 8, 128, 256), BF),
            pltpu.VMEM((4 * COLS, 12 * 128), F32),
            pltpu.VMEM((4 * COLS, 384), BF),
            pltpu.VMEM((ROWS, COLS, 128), F32),
        ],
        compiler_params=pltpu.CompilerParams(vmem_limit_bytes=32 * 2**20),
        name="cost_volume",
    )(rx, extra)


def cost_back_kernel(rx_ref, dm_ref, dr_ref, o_ref, fs, ws, bs, gs, gw):
    lane = lax.broadcasted_iota(jnp.int32, (128, 128), 1)
    zero = jnp.zeros((8, COLS, 256), BF)
    fs[0:8] = zero
    fs[32:40] = zero
    flip = flip_matrix()

    def put_first(i, value):
        fs[i + 8] = nn(flip, value).astype(BF)

    def put_warped(i, value):
        ws[i, 0:WIN] = value
        ws[i, WIN:] = jnp.zeros((128 - WIN, 256), BF)
    read_features(rx_ref, lane, put_first, put_warped)

    def clear(i, carry):
        bs[i] = jnp.zeros((15, COLS, 128), BF)
        bs[i + 32] = jnp.zeros((15, COLS, 128), BF)
        return carry
    lax.fori_loop(0, 8, clear, 0)
    lane = lane[:COLS]
    ahead = lane - lax.broadcasted_iota(jnp.int32, (COLS, 128), 0)

    def row(i, carry):
        at = pl.ds(pl.multiple_of(i * PITCH + LEFT, 16), COLS)
        halves = [dm_ref[at, 128 * h : 128 * h + 128].astype(F32) for h in range(2)]
        rest = dr_ref[at, :].astype(BF).astype(F32)

        def band(source, t, lo, hi):
            shift = (-t) % 128
            extra = shift % 8
            block = pltpu.roll(source, shift - extra, 1, stride=1, stride_axis=0)
            block = jnp.where(((ahead + (extra - lo)) & 127) < hi - lo, block, 0.0)
            return pltpu.roll(block, extra, 1) if extra else block
        bs[i + 8, 0:3] = jnp.zeros((3, COLS, 128), BF)
        bs[i + 8, 12:15] = jnp.zeros((3, COLS, 128), BF)
        for dy in range(4):
            bs[i + 8, dy + 3] = band(halves[dy // 2], 64 * (dy % 2) + 49, 0, 9).astype(BF)
        for a in range(4):
            value = band(halves[a // 2], 64 * (a % 2) + 58, 0, 6) + band(rest, 3 * a - 6, 6, 9)
            bs[i + 8, a + 7] = value.astype(BF)
        bs[i + 8, 11] = band(rest, 12, 0, 9).astype(BF)
        return carry
    lax.fori_loop(0, ROWS, row, 0)

    def to_first(g, carry):
        i = 4 * g
        left = jnp.concatenate(
            [jnp.concatenate([bs[i + 8 + r, t - r + 3] for t in range(12)], axis=1) for r in range(4)], axis=0
        )
        total = nn(left, ws[pl.ds(i, 12)].reshape(12 * 128, 256)) * (1.0 / CH**0.5)
        for r in range(4):
            at = pl.ds(pl.multiple_of((i + r) * PITCH + LEFT, 16), COLS)
            gs[i + r] = total[COLS * r : COLS * r + COLS] + dm_ref[at, :].astype(F32)
        return carry
    lax.fori_loop(0, ROWS // 4, to_first, 0)

    def to_warped(g, carry):
        t = 4 * g
        left = jnp.concatenate(
            [jnp.concatenate([bs[t + m, 11 - m + n] for n in range(4)], axis=1) for m in range(12)], axis=0
        )
        right = fs[pl.ds(t, 12)].reshape(12 * COLS, 256)
        total = lax.dot_general(left, right, (((0,), (0,)), ((), ())), preferred_element_type=F32)
        gw[pl.ds(t, 4)] = (total * (1.0 / CH**0.5)).reshape(4, 128, 256)
        return carry
    lax.fori_loop(0, 8, to_warped, 0)

    def put(start, size, one, two):
        for z in range(4):
            h, odd = divmod(z, 2)
            a = one[:, 128 * h : 128 * h + 128]
            b = two[:, 128 * h : 128 * h + 128]
            if odd:
                a = pltpu.roll(a, 64, 1)
            else:
                b = pltpu.roll(b, 64, 1)
            low = lax.broadcasted_iota(jnp.int32, (size, 128), 1) < 64
            o_ref[z, pl.ds(start, size), :] = jnp.where(low, a, b).astype(BF)

    def send_first(i, carry):
        put(pl.multiple_of(i * COLS, COLS), COLS, gs[i], gs[i + 12])
        return carry
    lax.fori_loop(0, 12, send_first, 0)

    def send_warped(i, carry):
        put(pl.multiple_of(12 * COLS + i * WIN, 16), WIN, gw[i, 0:WIN], gw[i + 16, 0:WIN])
        return carry
    lax.fori_loop(0, 16, send_warped, 0)


def cost_back(rx, grad_main, grad_rest):
    vm = pl.BlockSpec(memory_space=pltpu.VMEM)
    return pl.pallas_call(
        cost_back_kernel,
        out_shape=jax.ShapeDtypeStruct((4, PAY, 128), BF),
        in_specs=[vm] * 3,
        out_specs=vm,
        scratch_shapes=[
            pltpu.VMEM((ROWS + 16, COLS, 256), BF),
            pltpu.VMEM((ROWS + 8, 128, 256), BF),
            pltpu.VMEM((ROWS + 16, 15, COLS, 128), BF),
            pltpu.VMEM((ROWS, COLS, 256), F32),
            pltpu.VMEM((ROWS + 8, 128, 256), F32),
        ],
        compiler_params=pltpu.CompilerParams(vmem_limit_bytes=40 * 2**20),
        name="cost_back",
    )(rx, grad_main, grad_rest)


def turn_kernel(rp_ref, g1_ref, gw_ref, up_ref, down_ref, turn):
    eye = jnp.where(
        lax.broadcasted_iota(jnp.int32, (128, 128), 0) == lax.broadcasted_iota(jnp.int32, (128, 128), 1), 1.0, 0.0
    ).astype(BF)

    def first(i, carry):
        at = pl.ds(pl.multiple_of(i * COLS, COLS), COLS)
        value = nt(eye, jnp.concatenate([rp_ref[z, at, :] for z in range(4)], axis=0))
        g1_ref[i] = value[0:SLOT]
        g1_ref[i + 12] = value[SLOT:]
        return carry
    lax.fori_loop(0, 12, first, 0)

    def second(i, carry):
        at = pl.ds(pl.multiple_of(12 * COLS + i * WIN, 16), WIN)
        turn[...] = jnp.zeros(turn.shape, F32)
        for z in range(4):
            rows = slice(COLS * z + 4, COLS * z + 4 + WIN)
            turn[rows, :] = turn[rows, :] + rp_ref[z, at, :].astype(F32)
        value = jnp.transpose(turn[8:264, :])
        gw_ref[i] = value[0:SLOT]
        gw_ref[i + 16] = value[SLOT:]
        return carry
    lax.fori_loop(0, 16, second, 0)
    up_ref[...] = gw_ref[0:4].astype(BF)
    down_ref[...] = gw_ref[27:32].astype(BF)


def turn(rp):
    vm = pl.BlockSpec(memory_space=pltpu.VMEM)
    return pl.pallas_call(
        turn_kernel,
        out_shape=(
            jax.ShapeDtypeStruct((ROWS, SLOT, 256), F32),
            jax.ShapeDtypeStruct((ROWS + 8, SLOT, 256), F32),
            jax.ShapeDtypeStruct((4, SLOT, 256), BF),
            jax.ShapeDtypeStruct((5, SLOT, 256), BF),
        ),
        in_specs=[vm],
        out_specs=(vm,) * 4,
        scratch_shapes=[pltpu.VMEM((288, 128), F32)],
        compiler_params=pltpu.CompilerParams(vmem_limit_bytes=32 * 2**20),
        cost_estimate=pl.CostEstimate(flops=0, bytes_accessed=0, transcendentals=0),
        name="turn",
    )(rp)


def warp_back_kernel(gw_ref, from_above, from_below, f2_ref, above_ref, below_ref, g2_ref, gf_ref, full, band):
    first = lax.broadcasted_iota(jnp.int32, (SLOT, 256), 1) == 0
    last = lax.broadcasted_iota(jnp.int32, (SLOT, 256), 1) == 255
    channel = lax.broadcasted_iota(jnp.int32, (SLOT, 256), 0) < CH // 4
    band[0] = above_ref[3]
    band[1 : ROWS + 1] = f2_ref[...]
    band[ROWS + 1] = below_ref[0]
    full[...] = gw_ref[3:28]
    full[0:5] = full[0:5] + from_above[...].astype(F32)
    full[21:25] = full[21:25] + from_below[...].astype(F32)

    def spread(u, x):
        part = u * x
        return (x - part) + jnp.where(first, 0.0, pltpu.roll(part, 1, 1))

    def row(r, carry):
        upper = band[r + 1].astype(F32)
        lower = band[r + 2].astype(F32)
        before = band[r].astype(F32)
        u, v = upper[49:50], upper[50:51]
        grad = full[r + 1]
        g2_ref[r] = spread(u, (1.0 - v) * grad) + spread(before[49:50], before[50:51] * full[r])
        upper_next = jnp.where(last, 0.0, pltpu.roll(upper, 255, 1))
        lower_next = jnp.where(last, 0.0, pltpu.roll(lower, 255, 1))
        to_u = (1.0 - v) * (upper_next - upper) + v * (lower_next - lower)
        to_v = ((1.0 - u) * lower + u * lower_next) - ((1.0 - u) * upper + u * upper_next)
        along = jnp.sum(jnp.where(channel, grad * to_u, 0.0), axis=0, keepdims=True)
        down = jnp.sum(jnp.where(channel, grad * to_v, 0.0), axis=0, keepdims=True)
        gf_ref[r] = jnp.concatenate([along, down, jnp.zeros((6, 256), F32)], axis=0)
        return carry
    lax.fori_loop(0, ROWS, row, 0)


def warp_back(gw, from_above, from_below, f2, above, below):
    vm = pl.BlockSpec(memory_space=pltpu.VMEM)
    return pl.pallas_call(
        warp_back_kernel,
        out_shape=(
            jax.ShapeDtypeStruct((ROWS, SLOT, 256), F32),
            jax.ShapeDtypeStruct((ROWS, 8, 256), F32),
        ),
        in_specs=[vm] * 6,
        out_specs=(vm, vm),
        scratch_shapes=[pltpu.VMEM((ROWS + 1, SLOT, 256), F32), pltpu.VMEM((ROWS + 2, SLOT, 256), BF)],
        compiler_params=pltpu.CompilerParams(vmem_limit_bytes=32 * 2**20),
        cost_estimate=pl.CostEstimate(flops=0, bytes_accessed=0, transcendentals=0),
        name="warp_back",
    )(gw, from_above, from_below, f2, above, below)
WIDE, REST = lane_maps()
GATHER = gather_map()

PIX = ("xy", "core")


def ring(axis, steps):
    count = lax.axis_size(axis)
    return [(i, i + steps) for i in range(max(0, -steps), min(count, count - steps))]


def local(
    feat_one, feat_two, up_flow, up_feat, target_flow, valid_mask,
    conv_one, conv_two, conv_three, conv_four, conv_five, flow_head,
    bias_one, bias_two, bias_three, bias_four, bias_five, bias_head,
):
    convs = [conv_one, conv_two, conv_three, conv_four, conv_five, flow_head]
    biases = [bias_one, bias_two, bias_three, bias_four, bias_five, bias_head]
    channels = feat_one.shape[0]
    place = lax.axis_index("chan")
    f2 = jnp.concatenate([feat_two, up_flow, jnp.zeros((SLOT - channels - 2, ROWS, 256), BF)], axis=0)
    f2 = jnp.transpose(f2, (1, 0, 2))
    above = lax.ppermute(f2[ROWS - MD :], PIX, ring(PIX, 1))
    below = lax.ppermute(f2[: MD + 1], PIX, ring(PIX, -1))
    f1 = jnp.transpose(jnp.pad(feat_one, ((0, SLOT - channels), (0, 0), (0, 0))), (1, 0, 2))
    packed = pack(f1, f2, above, below)
    packed, convs, biases = lax.optimization_barrier((packed, convs, biases))
    features = lax.all_to_all(packed, "chan", split_axis=0, concat_axis=0, tiled=True)
    weight, weight_rest = arrange(convs, biases)

    flow_cols = lax.dynamic_slice_in_dim(up_flow, place * COLS, COLS, 2)
    high = target_flow.astype(BF)
    low = (target_flow - high.astype(F32)).astype(BF)
    one = jnp.ones((2, ROWS, COLS), BF)
    planes = jnp.concatenate([flow_cols, up_feat, one, valid_mask.astype(BF)[None], high, low], axis=0)
    extra = jnp.pad(jnp.transpose(planes, (1, 2, 0)), ((0, 0), (0, 0), (21, 96)))
    upper, lower = cost_volume(features, extra)
    top = lax.ppermute(lower, PIX, ring(PIX, 1))
    bottom = lax.ppermute(upper, PIX, ring(PIX, -1))
    tiles = [tile.reshape(27, COLS, 128) for tile in (top, upper, lower, bottom)]
    left = lax.ppermute(
        jnp.concatenate([tile[:, COLS - LEFT :] for tile in tiles], axis=0), "chan", ring("chan", 1)
    )
    right = lax.ppermute(
        jnp.concatenate([tile[:, :LEFT] for tile in tiles], axis=0), "chan", ring("chan", -1)
    )
    acts, slopes, main, rest, grad_main, grad_rest, flow, sums = decode(
        top, upper, lower, bottom, left, right, weight, weight_rest
    )
    payload = cost_back(features, grad_main, grad_rest)
    payload, slopes = lax.optimization_barrier((payload, slopes))
    returned = lax.all_to_all(payload, "chan", split_axis=0, concat_axis=0, tiled=True)
    core = lax.axis_index("core").astype(jnp.int32)[None]
    own, sent = wgrad(core, slopes, main, rest, acts, jnp.asarray(GATHER, BF))
    returned, own, sent = lax.optimization_barrier((returned, own, sent))
    parts = chip_parts(own, sent, jnp.sum(sums[:, :, 96], axis=1))
    returned, parts = lax.optimization_barrier((returned, parts))
    parts = lax.all_to_all(parts, CHIPS, split_axis=0, concat_axis=0, tiled=True)
    grad_one, partial, to_above, to_below = turn(returned)
    from_above = lax.ppermute(to_below, PIX, ring(PIX, 1))
    from_below = lax.ppermute(to_above, PIX, ring(PIX, -1))
    grad_two, grad_flow = warp_back(partial, from_above, from_below, f2, above, below)
    grad_feat_one = jnp.transpose(grad_one[:, :channels], (1, 0, 2))
    grad_feat_two = jnp.transpose(grad_two[:, :channels], (1, 0, 2))
    flow_parts = jnp.transpose(grad_flow[:, :2], (1, 0, 2))
    total = lax.dynamic_slice_in_dim(flow_parts, place * COLS, COLS, 2)
    flow_parts = flow_parts.astype(BF)
    for step in range(1, 4):
        sent = lax.dynamic_slice_in_dim(flow_parts, lax.rem(place + step, 4) * COLS, COLS, 2)
        total = total + lax.ppermute(sent, "chan", [(i, (i + step) % 4) for i in range(4)]).astype(F32)

    def pixels(value):
        return jnp.transpose(value.reshape(ROWS, PITCH, -1)[:, LEFT : LEFT + COLS], (2, 0, 1))

    flow_out = pixels(flow[:, 96:98])
    small = pixels(grad_rest[:, 21:25])
    grad_up_flow = total + small[:2]
    parts, *outputs = lax.optimization_barrier(
        (parts, flow_out, grad_feat_one, grad_feat_two, grad_up_flow, small[2:])
    )
    flow_out, grad_feat_one, grad_feat_two, grad_up_flow, grad_up_feat = outputs
    weight_grads, bias_grads, scalars = sum_parts(core, parts)
    bias_grads = [bias_grads[ROW0[n] : ROW0[n] + OUTS[n], 89] for n in range(6)]
    return (flow_out, scalars, grad_feat_one, grad_feat_two, grad_up_flow, grad_up_feat, *weight_grads, *bias_grads)


def solution(mesh):
    chan, pix = mesh.devices.shape
    cores = jax.sharding.Mesh(mesh.devices.reshape(chan, pix // 2, 2), ("chan", "xy", "core"))
    return jax.shard_map(
        local,
        mesh=cores,
        in_specs=(
            P("chan", PIX, None),
            P("chan", PIX, None),
            P(None, PIX, None),
            P(None, PIX, "chan"),
            P(None, PIX, "chan"),
            P(PIX, "chan"),
        )
        + (P(),) * 12,
        out_specs=(
            P(None, PIX, "chan"),
            P(),
            P("chan", PIX, None),
            P("chan", PIX, None),
            P(None, PIX, "chan"),
            P(None, PIX, "chan"),
        )
        + (P(),) * 12,
        check_vma=False,
    )
```

```python
import jax
import jax.numpy as jnp
import numpy as np
from jax import lax
from jax.experimental import pallas as pl
from jax.experimental.pallas import tpu as pltpu
from jax.sharding import PartitionSpec as P

CH = 196
MD = 4
CH_SLOT = 49
OUTS = (128, 128, 96, 64, 32, 2)
ROW0 = (0, 128, 256, 384, 448, 480)
DEPTH = (281, 409, 537, 633, 697, 729)


def start_lane(channel):
    if channel < 81:
        dy, dx = divmod(channel, 9)
        if dy < 4:
            return 0, 64 * dy + 49 + dx
        if dy < 8:
            if dx < 6:
                return 0, 64 * (dy - 4) + 58 + dx
            return 1, 3 * (dy - 4) + dx - 6
        return 1, 12 + dx
    if channel < 277:
        slot, inner = divmod(channel - 81, CH_SLOT)
        return 0, 64 * slot + inner
    return 1, 21 + channel - 277


def lane_maps():
    wide = np.zeros((729, 768), np.float32)
    rest = np.zeros((729, 128), np.float32)
    for c in range(729):
        if c < 32:
            wide[c, 704 + c] = 1
        elif c < 96:
            wide[c, 640 + c - 32] = 1
        elif c < 192:
            wide[c, 512 + c - 96] = 1
        elif c < 320:
            wide[c, 384 + c - 192] = 1
        elif c < 448:
            wide[c, 256 + c - 320] = 1
        else:
            block, lane = start_lane(c - 448)
            if block == 0:
                wide[c, lane] = 1
            else:
                rest[c, lane] = 1
    return wide, rest


def gather_map():
    table = np.zeros((1024, 768), np.float32)
    for c in range(281):
        block, lane = start_lane(c)
        table[288 * block + lane, 448 + c] = 1
    table[288 + 25, 729] = 1
    for i in range(128):
        table[384 + i, 320 + i] = 1
        table[512 + i, 192 + i] = 1
    for i in range(96):
        table[640 + i, 96 + i] = 1
    for i in range(64):
        table[768 + i, 32 + i] = 1
    for i in range(32):
        table[896 + 64 + i, i] = 1
    return table

CH = 196
MD = 4
BF = jnp.bfloat16
F32 = jnp.float32
HALO = 12
PITCH = 96
ROWS = 24
COLS = 64
LEFT = 16
WROWS = ROWS + 2 * HALO
NPX = WROWS * PITCH
GUARD = 16
VMEM_MB = 62


def nt(a, b):
    return lax.dot_general(a, b, (((1,), (1,)), ((), ())), preferred_element_type=F32)


def nn(a, b):
    return lax.dot_general(a, b, (((1,), (0,)), ((), ())), preferred_element_type=F32)


def decode_kernel(
    top_ref, h0_ref, h1_ref, bottom_ref, left_ref, right_ref, wm_ref, w_ref, wr_ref,
    a_ref, g_ref, xm_ref, xr_ref, flow_ref, met_ref,
    xs, xq, sh, pre, part, mk, sems,
):
    lane = lax.broadcasted_iota(jnp.int32, (PITCH, 128), 1)
    core = pl.ds(HALO * PITCH, ROWS * PITCH)

    def rows(lo, hi, body, unroll=2):
        def step(i, carry):
            for u in range(unroll):
                body(pl.multiple_of(lo * PITCH + (i * unroll + u) * PITCH, PITCH))
            return carry
        lax.fori_loop(0, (hi - lo) // unroll, step, 0)

    def put_shifted(dst, p, lanes, value):
        height = value.shape[0]
        dst[0, pl.ds(p, PITCH), lanes] = pltpu.roll(value, 1, 0).astype(BF)
        dst[1, pl.ds(p, PITCH), lanes] = value.astype(BF)
        dst[2, pl.ds(p, PITCH), lanes] = pltpu.roll(value, height - 1, 0).astype(BF)

    def chunked(lo, hi, count, body):
        size = (hi - lo) * PITCH // count

        def step(i, carry):
            body(pl.multiple_of(lo * PITCH + i * size, 16), size)
            return carry
        lax.fori_loop(0, count, step, 0)

    for h, tile in enumerate((top_ref, h0_ref, h1_ref, bottom_ref)):
        def main_rows(i, carry, h=h, tile=tile):
            p = pl.multiple_of((12 * h + i) * PITCH, PITCH)
            for half in range(2):
                at = pl.multiple_of((12 * half + i) * COLS, COLS)
                value = jnp.concatenate(
                    [
                        left_ref[27 * h + 12 * half + i].astype(F32),
                        tile[pl.ds(at, COLS), :].astype(F32),
                        right_ref[27 * h + 12 * half + i].astype(F32),
                    ],
                    axis=0,
                )
                put_shifted(xs, p, slice(128 * half, 128 * half + 128), value)
            return carry
        lax.fori_loop(0, 12, main_rows, 0)

        def rest_rows(b, carry, h=h, tile=tile):
            packed = jnp.concatenate(
                [
                    left_ref[27 * h + 24 + b].astype(F32),
                    tile[pl.ds(pl.multiple_of(1536 + b * COLS, COLS), COLS), :].astype(F32),
                    right_ref[27 * h + 24 + b].astype(F32),
                ],
                axis=0,
            )
            for a in range(4):
                p = pl.multiple_of((12 * h + 3 * a + b) * PITCH, PITCH)
                value = jnp.where(lane < 32, pltpu.roll(packed, (128 - 32 * a) % 128, 1), 0.0)
                mk[pl.ds(p, PITCH), :] = jnp.broadcast_to(value[:, 25:26], (PITCH, 128))
                low = pltpu.roll(value, 1, 0)
                mid = pltpu.roll(value, 32, 1)
                high = pltpu.roll(pltpu.roll(value, PITCH - 1, 0), 64, 1)
                xq[pl.ds(p, PITCH), :] = (low + mid + high).astype(BF)
            return carry
        lax.fori_loop(0, 3, rest_rows, 0)

    keep = [
        pltpu.make_async_copy(xs.at[1, core, :], xm_ref, sems.at[1]),
        pltpu.make_async_copy(xq.at[core, :], xr_ref, sems.at[2]),
    ]
    for copy in keep:
        copy.start()

    def start_sums(p, size):
        left = jnp.concatenate([xq[pl.ds(p + PITCH * (dy - 1), size), :] for dy in range(3)], axis=1)
        total = nt(left, jnp.concatenate([wr_ref[dy] for dy in range(3)], axis=1))
        for dy in range(3):
            at = p + PITCH * (dy - 1)
            for dx in range(3):
                total = total + nt(xs[dx, pl.ds(at, size), :], wm_ref[3 * dy + dx])
        pre[pl.ds(p, size), :] = total
    chunked(1, WROWS - 1, 3, start_sums)

    first_lane = [0, 128, 256, 384, 384]
    lanes_of = [(0, 128), (0, 128), (0, 96), (0, 64), (64, 96)]
    kept = []
    for layer in range(5):
        block = slice(first_lane[layer], first_lane[layer] + 128)
        from_lane, to_lane = lanes_of[layer]
        inside = (lane >= from_lane) & (lane < to_lane)
        lo, hi = layer + 1, WROWS - layer - 1
        piece = min(layer, 3)
        lanes = slice(128 * piece, 128 * piece + 128)
        if layer == 4:
            kept[3].wait()

        def activate(p, block=block, inside=inside, lanes=lanes, layer=layer):
            value = pre[pl.ds(p, PITCH), block]
            sig = 0.5 * jnp.tanh(0.5 * value) + 0.5
            live = mk[pl.ds(p, PITCH), :] > 0.0
            if layer >= 3:
                live = live & inside
            act = value * sig
            slope = jnp.where(live, sig + act * (1.0 - sig), 0.0)
            if layer >= 3:
                slope = jnp.where(inside, slope, value)
            pre[pl.ds(p, PITCH), block] = slope
            put_shifted(sh, p, lanes, jnp.where(live, act, 0.0))
        rows(lo, hi, activate)
        copy = pltpu.make_async_copy(
            sh.at[1, core, lanes], a_ref.at[:, 128 * layer : 128 * layer + 128], sems.at[3 + layer]
        )
        copy.start()
        kept.append(copy)
        out0 = min(128 * (layer + 1), 384)

        def add_sums(p, size, piece=piece, out0=out0):
            lanes = slice(128 * piece, 128 * piece + 128)
            left = jnp.concatenate(
                [sh[dx, pl.ds(p + PITCH * (dy - 1), size), lanes] for dy in range(3) for dx in range(3)], axis=1
            )
            right = jnp.concatenate(
                [w_ref[k, out0:512, 128 * piece : 128 * piece + 128] for k in range(9)], axis=1
            )
            pre[pl.ds(p, size), out0:512] = pre[pl.ds(p, size), out0:512] + nt(left, right)
        chunked(lo + 1, hi - 1, 3, add_sums)

    is_flow = (lane >= 96) & (lane < 98)
    column = lax.broadcasted_iota(jnp.int32, (PITCH, 128), 0)
    core_column = (column >= LEFT) & (column < LEFT + COLS)
    met_ref[...] = jnp.zeros((3, PITCH, 128), F32)
    kept[0].wait()
    kept[1].wait()
    kept[2].wait()
    kept[4].wait()

    def loss(p):
        flow = pre[pl.ds(p, PITCH), 384:512]
        rest = xq[pl.ds(p, PITCH), :].astype(F32)
        target = pltpu.roll(rest, 96 - 60, 1) + pltpu.roll(rest, 96 - 62, 1)
        diff = jnp.where(is_flow, flow - target, 0.0)
        square = diff * diff
        other = jnp.where(lane == 96, pltpu.roll(square, 127, 1), pltpu.roll(square, 1, 1))
        error = jnp.sqrt(square + other + 1.0)
        mask = jnp.broadcast_to(rest[:, 59:60], (PITCH, 128))
        put_shifted(sh, p, slice(384, 512), jnp.where(is_flow, mask * diff / error, 0.0))
        return flow, mask, error

    def loss_rim(p):
        loss(p)

    def loss_core(p):
        flow, mask, error = loss(p)
        q = pl.multiple_of(p - HALO * PITCH, PITCH)
        flow_ref[pl.ds(q, PITCH), :] = flow
        mask = jnp.where(core_column, mask, 0.0)
        met_ref[0] += mask * (error - 1.0)
        met_ref[1] += mask / (1.0 + jnp.exp(-4.0 * (error - 2.0)))
        met_ref[2] += mask

    rows(6, HALO, loss_rim)
    rows(HALO, HALO + ROWS, loss_core)
    rows(HALO + ROWS, WROWS - 6, loss_rim)

    for layer in range(4, -1, -1):
        lo, hi = HALO - layer - 1, HALO + ROWS + layer + 1
        piece = min(layer, 3)
        lanes = slice(128 * piece, 128 * piece + 128)
        out0 = min(128 * (layer + 1), 384)
        block = slice(first_lane[layer], first_lane[layer] + 128)
        from_lane, to_lane = lanes_of[layer]
        inside = (lane >= from_lane) & (lane < to_lane)
        c0 = 128 * piece

        def back(p, size, out0=out0, c0=c0):
            left = jnp.concatenate(
                [sh[2 - dx, pl.ds(p - PITCH * (dy - 1), size), out0:512] for dy in range(3) for dx in range(3)], axis=1
            )
            right = jnp.concatenate([w_ref[k, out0:512, c0 : c0 + 128] for k in range(9)], axis=0)
            part[pl.ds(p, size), :] = nn(left, right)
        chunked(lo, hi, 3, back)

        def slope(p, layer=layer, block=block, inside=inside, lanes=lanes):
            value = part[pl.ds(p, PITCH), :] * pre[pl.ds(p, PITCH), block]
            if layer >= 3:
                value = jnp.where(inside, value, sh[1, pl.ds(p, PITCH), lanes].astype(F32))
            put_shifted(sh, p, lanes, value)
        rows(lo, hi, slope)

    copy = pltpu.make_async_copy(sh.at[:, pl.ds((HALO - 1) * PITCH, (ROWS + 2) * PITCH), :], g_ref, sems.at[0])
    keep.append(copy)
    copy.start()

    for copy in keep:
        copy.wait()


def decode(*operands):
    size = ROWS * PITCH
    vm = pl.BlockSpec(memory_space=pltpu.VMEM)
    hbm = pl.BlockSpec(memory_space=pl.ANY)
    return pl.pallas_call(
        decode_kernel,
        out_shape=(
            jax.ShapeDtypeStruct((size, 640), BF),
            jax.ShapeDtypeStruct((3, (ROWS + 2) * PITCH, 512), BF),
            jax.ShapeDtypeStruct((size, 256), BF),
            jax.ShapeDtypeStruct((size, 128), BF),
            jax.ShapeDtypeStruct((size, 128), F32),
            jax.ShapeDtypeStruct((3, PITCH, 128), F32),
        ),
        in_specs=[vm] * 9,
        out_specs=(hbm, hbm, hbm, hbm, vm, vm),
        scratch_shapes=[
            pltpu.VMEM((3, NPX, 256), BF),
            pltpu.VMEM((NPX, 128), BF),
            pltpu.VMEM((3, NPX, 512), BF),
            pltpu.VMEM((NPX, 512), F32),
            pltpu.VMEM((NPX, 128), F32),
            pltpu.VMEM((NPX, 128), F32),
            pltpu.SemaphoreType.DMA((8,)),
        ],
        compiler_params=pltpu.CompilerParams(vmem_limit_bytes=VMEM_MB * 2**20),
        name="decode",
    )(*operands)


def arrange_kernel(c1, c2, c3, c4, c5, c6, wide_ref, rest_ref, bias_ref, wm_ref, w_ref, wr_ref):
    for rows in (slice(352, 384), slice(480, 512)):
        wm_ref[:, rows, :] = jnp.zeros((9, 32, 256), BF)
        w_ref[:, rows, :] = jnp.zeros((9, 32, 512), BF)
    wr_ref[:, 352:384, :] = jnp.zeros((3, 32, 128), BF)
    wr_ref[:, 480:512, :] = jnp.zeros((3, 32, 128), BF)
    lane = lax.broadcasted_iota(jnp.int32, (512, 128), 1)
    bias = bias_ref[...]
    high = bias.astype(BF).astype(F32)
    bias = jnp.where(lane == 57, high, jnp.where(lane == 58, bias - high, 0.0))

    for n, ref in enumerate((c1, c2, c3, c4, c5, c6)):
        outs, depth = OUTS[n], DEPTH[n]
        rows = slice(ROW0[n], ROW0[n] + outs)
        wide = wide_ref[729 - depth :, :]
        rest = rest_ref[729 - depth :, :]
        dims = (((0,), (0,)), ((), ())) if n < 2 else (((1,), (0,)), ((), ()))
        for dy in range(3):
            total = bias[rows] if dy == 1 else jnp.zeros((outs, 128), F32)
            for dx in range(3):
                weight = ref[3 * dy + dx]
                value = lax.dot_general(weight, wide, dims, preferred_element_type=F32).astype(BF)
                wm_ref[3 * dy + dx, rows, :] = value[:, 0:256]
                w_ref[3 * dy + dx, rows, :] = value[:, 256:768]
                part = lax.dot_general(weight, rest, dims, preferred_element_type=F32)
                total = total + (pltpu.roll(part, 32 * dx, 1) if dx else part)
            wr_ref[dy, rows, :] = total.astype(BF)


def arrange(convs, biases):
    vm = pl.BlockSpec(memory_space=pltpu.VMEM)
    bias = jnp.concatenate(
        [biases[0], biases[1], biases[2], jnp.zeros((32,), F32), biases[3], biases[4], biases[5], jnp.zeros((30,), F32)]
    ).reshape(512, 1)
    turned = [jnp.transpose(convs[0], (0, 2, 1)), jnp.transpose(convs[1], (0, 2, 1))]
    return pl.pallas_call(
        arrange_kernel,
        out_shape=(
            jax.ShapeDtypeStruct((9, 512, 256), BF),
            jax.ShapeDtypeStruct((9, 512, 512), BF),
            jax.ShapeDtypeStruct((3, 512, 128), BF),
        ),
        in_specs=[vm] * 9,
        out_specs=(vm, vm, vm),
        compiler_params=pltpu.CompilerParams(vmem_limit_bytes=40 * 2**20),
        cost_estimate=pl.CostEstimate(flops=4 * 10**9, bytes_accessed=16 * 10**6, transcendentals=0),
        name="arrange",
    )(*turned, *convs[2:], jnp.asarray(WIDE, BF), jnp.asarray(REST, BF), bias)

TILE_ROWS = 2048
TOTAL_ROWS = 9 * TILE_ROWS
HALF_ROWS = TOTAL_ROWS // 2


def tn(a, b):
    return lax.dot_general(a, b, (((0,), (0,)), ((), ())), preferred_element_type=F32)


def wgrad_kernel(core_ref, g_ref, xm_ref, xr_ref, a_ref, qp_ref, own_ref, sent_ref, xp, o_ref, sems):
    column = lax.broadcasted_iota(jnp.int32, (PITCH, 768), 0)
    core = (column >= LEFT) & (column < LEFT + COLS)
    core = jnp.concatenate([core] * 4, axis=0)
    size = 4 * PITCH

    def gather(i, carry):
        at = pl.ds(pl.multiple_of(i * size, size), size)
        left = jnp.concatenate([xm_ref[at, :], xr_ref[at, :], a_ref[at, :]], axis=1)
        xp[at, :] = jnp.where(core, nn(left, qp_ref[...]), 0.0).astype(BF)
        return carry
    lax.fori_loop(0, ROWS // 4, gather, 0)

    for k in range(9):
        dy, dx = divmod(k, 3)
        at = pl.ds(PITCH * (2 - dy), ROWS * PITCH)
        base = TILE_ROWS * k
        value = tn(g_ref[2 - dx, at, 0:256], xp[:, 256:768])
        low = value.astype(BF)
        for t in range(3):
            o_ref[base + 128 * t : base + 128 * t + 128, :] = low[0:128, 128 * t + 128 : 128 * t + 256]
        for t in range(4):
            o_ref[base + 384 + 128 * t : base + 512 + 128 * t, :] = low[128:256, 128 * t : 128 * t + 128]
        value = tn(g_ref[2 - dx, at, 256:512], xp[...])
        low = value.astype(BF)
        for t in range(5):
            o_ref[base + 896 + 96 * t : base + 992 + 96 * t, :] = low[0:96, 128 * t + 128 : 128 * t + 256]
        for t in range(6):
            o_ref[base + 1376 + 112 * t : base + 1488 + 112 * t, :] = low[128:240, 128 * t : 128 * t + 128]
    core = core_ref[0]
    copies = [
        pltpu.make_async_copy(
            o_ref.at[pl.ds(pl.multiple_of(at * HALF_ROWS, HALF_ROWS), HALF_ROWS), :], target, sems.at[n]
        )
        for n, (target, at) in enumerate(((own_ref, core), (sent_ref, 1 - core)))
    ]
    for copy in copies:
        copy.start()
    for copy in copies:
        copy.wait()


def wgrad(core, g, xm, xr, a, qp):
    vm = pl.BlockSpec(memory_space=pltpu.VMEM)
    hbm = pl.BlockSpec(memory_space=pl.ANY)
    return pl.pallas_call(
        wgrad_kernel,
        out_shape=(jax.ShapeDtypeStruct((HALF_ROWS, 128), BF),) * 2,
        in_specs=[pl.BlockSpec(memory_space=pltpu.SMEM)] + [vm] * 5,
        out_specs=(hbm, hbm),
        scratch_shapes=[
            pltpu.VMEM((ROWS * PITCH, 768), BF),
            pltpu.VMEM((TOTAL_ROWS, 128), BF),
            pltpu.SemaphoreType.DMA((2,)),
        ],
        compiler_params=pltpu.CompilerParams(vmem_limit_bytes=VMEM_MB * 2**20),
        name="wgrad",
    )(core, g, xm, xr, a, qp)

NOTE = 16


def half_sum_kernel(own_ref, got_ref, note_ref, got_note_ref, o_ref):
    count, height = o_ref.shape[0], o_ref.shape[1] - NOTE
    notes = jnp.concatenate([note_ref[0:8].astype(F32), got_note_ref[0:8].astype(F32)], axis=0).astype(BF)
    for b in range(count):
        rows = slice(height * b, height * (b + 1))
        o_ref[b, 0:height] = (own_ref[rows, :].astype(F32) + got_ref[rows, :].astype(F32)).astype(BF)
        o_ref[b, height:] = notes


def half_sum(own, got, note, got_note, count):
    height = HALF_ROWS // count
    steps = 4
    block = HALF_ROWS // steps
    return pl.pallas_call(
        half_sum_kernel,
        grid=(steps,),
        in_specs=[
            pl.BlockSpec((block, 128), lambda i: (i, 0)),
            pl.BlockSpec((block, 128), lambda i: (i, 0)),
            pl.BlockSpec((NOTE, 128), lambda i: (0, 0)),
            pl.BlockSpec((NOTE, 128), lambda i: (0, 0)),
        ],
        out_specs=pl.BlockSpec((count // steps, height + NOTE, 128), lambda i: (i, 0, 0)),
        out_shape=jax.ShapeDtypeStruct((count, height + NOTE, 128), BF),
        name="half_sum",
    )(own, got, note, got_note)


def spread_kernel(parts_ref, o_ref, note_ref):
    count, height = o_ref.shape[0], o_ref.shape[1]

    def add(b, carry):
        total, notes = carry
        return total + parts_ref[b, 0:height].astype(F32), notes + parts_ref[b, height:].astype(F32)
    zero = (jnp.zeros((height, 128), F32), jnp.zeros((NOTE, 128), F32))
    total, notes = lax.fori_loop(0, count, add, zero)
    note_ref[...] = notes
    total = total.astype(BF)

    def put(b, carry):
        o_ref[b] = total
        return carry
    lax.fori_loop(0, count, put, 0)


def spread_total(parts):
    count, height, _ = parts.shape
    vm = pl.BlockSpec(memory_space=pltpu.VMEM)
    return pl.pallas_call(
        spread_kernel,
        out_shape=(
            jax.ShapeDtypeStruct((count, height - NOTE, 128), BF),
            jax.ShapeDtypeStruct((NOTE, 128), F32),
        ),
        in_specs=[vm],
        out_specs=(vm, vm),
        compiler_params=pltpu.CompilerParams(vmem_limit_bytes=32 * 2**20),
        name="spread_total",
    )(parts)


def unpack_kernel(core_ref, mine_ref, other_ref, o1, o2, o3, o4, o5, o6, b_ref, all_ref, sems):
    k = pl.program_id(0)

    @pl.when(k == 0)
    def _():
        core = core_ref[0]
        copies = [
            pltpu.make_async_copy(
                source, all_ref.at[pl.ds(pl.multiple_of(at * HALF_ROWS, HALF_ROWS), HALF_ROWS), :], sems.at[n]
            )
            for n, (source, at) in enumerate(((mine_ref, core), (other_ref, 1 - core)))
        ]
        for copy in copies:
            copy.start()
        for copy in copies:
            copy.wait()
    first = pl.multiple_of(k * TILE_ROWS, TILE_ROWS)

    def tiles(base, height, count):
        return jnp.concatenate(
            [all_ref[pl.ds(first + base + height * t, height), :].astype(F32) for t in range(count)], axis=1
        )
    o1[0] = jnp.transpose(tiles(0, 128, 3))[64 : 64 + 281]
    o2[0] = jnp.transpose(tiles(384, 128, 4))[64 : 64 + 409]
    o3[0] = tiles(896, 96, 5)[:, 64 : 64 + 537]
    last = tiles(1376, 112, 6)
    o4[0] = last[0:64, 96:729]
    o5[0] = last[64:96, 32:729]
    o6[0] = last[96:98, 0:729]

    @pl.when(k == 4)
    def _():
        b_ref[0:128, :] = tiles(256, 128, 1)
        b_ref[128:256, :] = tiles(768, 128, 1)
        b_ref[256:352, :] = tiles(1280, 96, 1)
        b_ref[352:384, :] = jnp.zeros((32, 128), F32)
        b_ref[384:496, :] = last[:, 640:768]
        b_ref[496:512, :] = jnp.zeros((16, 128), F32)


def unpack(core, mine, other):
    shapes = ((281, 128), (409, 128), (96, 537), (64, 633), (32, 697), (2, 729))
    hbm = pl.BlockSpec(memory_space=pl.ANY)
    results = pl.pallas_call(
        unpack_kernel,
        grid_spec=pltpu.PrefetchScalarGridSpec(
            num_scalar_prefetch=1,
            grid=(9,),
            in_specs=[hbm, hbm],
            out_specs=tuple(pl.BlockSpec((1,) + s, lambda k, core: (k, 0, 0)) for s in shapes)
            + (pl.BlockSpec((512, 128), lambda k, core: (0, 0)),),
            scratch_shapes=[pltpu.VMEM((TOTAL_ROWS, 128), BF), pltpu.SemaphoreType.DMA((2,))],
        ),
        out_shape=tuple(jax.ShapeDtypeStruct((9,) + s, F32) for s in shapes)
        + (jax.ShapeDtypeStruct((512, 128), F32),),
        compiler_params=pltpu.CompilerParams(vmem_limit_bytes=32 * 2**20),
        name="unpack",
    )(core, mine, other)
    grads = list(results[:6])
    grads[0] = jnp.transpose(grads[0], (0, 2, 1))
    grads[1] = jnp.transpose(grads[1], (0, 2, 1))
    return grads, results[6]


SWAP = [(0, 1), (1, 0)]
CHIPS = ("chan", "xy")


def chip_parts(own, sent, scalars):
    high = lax.reduce_precision(scalars, 8, 7)
    middle = lax.reduce_precision(scalars - high, 8, 7)
    low = scalars - high - middle
    note = jnp.stack([high, middle, low]).astype(BF)
    note = jnp.pad(note, ((0, NOTE - 3), (0, 128 - scalars.shape[0])))
    got_note = lax.ppermute(note, "core", SWAP)
    got = lax.ppermute(sent, "core", SWAP)
    return half_sum(own, got, note, got_note, lax.axis_size(CHIPS))

SLOT = 64
WIN = 80
PAY = 12 * COLS + 16 * WIN
HALF = 27 * COLS


def slanted(x, shift):
    shift = shift % 128
    if shift % 8:
        x = pltpu.roll(x, shift % 8, 1)
    return pltpu.roll(x, shift - shift % 8, 1, stride=1, stride_axis=0)


def two_rows(lane, parts):
    swap = [pltpu.roll(part, 64, 1) for part in parts]
    first = [jnp.where(lane < 64, parts[2 * h], swap[2 * h + 1]) for h in range(2)]
    second = [jnp.where(lane < 64, swap[2 * h], parts[2 * h + 1]) for h in range(2)]
    return jnp.concatenate(first, axis=1), jnp.concatenate(second, axis=1)


def pack_kernel(f1_ref, f2_ref, above_ref, below_ref, o_ref, band, turn):
    eye = jnp.where(
        lax.broadcasted_iota(jnp.int32, (256, 256), 0) == lax.broadcasted_iota(jnp.int32, (256, 256), 1), 1.0, 0.0
    ).astype(BF)
    back = jnp.where(
        lax.broadcasted_iota(jnp.int32, (256, 256), 0) + lax.broadcasted_iota(jnp.int32, (256, 256), 1) == 255, 1.0, 0.0
    ).astype(BF)
    last = lax.broadcasted_iota(jnp.int32, (SLOT, 256), 1) == 255
    channel = lax.broadcasted_iota(jnp.int32, (SLOT, 256), 0) < CH // 4
    band[0:MD] = above_ref[...]
    band[MD : MD + ROWS] = f2_ref[...]
    band[MD + ROWS :] = below_ref[...]
    turn[...] = jnp.zeros(turn.shape, F32)

    def first(i, carry):
        both = jnp.concatenate([f1_ref[i], f1_ref[i + 12]], axis=0)
        value = nt(back, both).astype(BF)
        for z in range(4):
            o_ref[z, pl.ds(pl.multiple_of(i * COLS, COLS), COLS), :] = value[192 - COLS * z : 256 - COLS * z]
        return carry
    lax.fori_loop(0, 12, first, 0)

    def warped(t):
        upper = band[t].astype(F32)
        lower = band[t + 1].astype(F32)
        u = upper[49:50]
        v = upper[50:51]

        def across(x):
            return (1.0 - u) * x + u * jnp.where(last, 0.0, pltpu.roll(x, 255, 1))
        value = (1.0 - v) * across(upper) + v * across(lower)
        return jnp.where(channel, value, 0.0).astype(BF)

    def second(i, carry):
        both = jnp.concatenate([warped(i), warped(i + 16)], axis=0)
        turn[8:264, :] = nt(eye, both)
        for z in range(4):
            start = pl.multiple_of(12 * COLS + i * WIN, 16)
            o_ref[z, pl.ds(start, WIN), :] = turn[COLS * z + 4 : COLS * z + 4 + WIN, :].astype(BF)
        return carry
    lax.fori_loop(0, 16, second, 0)


def pack(f1, f2, above, below):
    vm = pl.BlockSpec(memory_space=pltpu.VMEM)
    return pl.pallas_call(
        pack_kernel,
        out_shape=jax.ShapeDtypeStruct((4, PAY, 128), BF),
        in_specs=[vm] * 4,
        out_specs=vm,
        scratch_shapes=[pltpu.VMEM((33, SLOT, 256), BF), pltpu.VMEM((288, 128), F32)],
        compiler_params=pltpu.CompilerParams(vmem_limit_bytes=32 * 2**20),
        name="pack",
    )(f1, f2, above, below)


def flip_matrix():
    total = lax.broadcasted_iota(jnp.int32, (COLS, COLS), 0) + lax.broadcasted_iota(jnp.int32, (COLS, COLS), 1)
    return jnp.where(total == COLS - 1, 1.0, 0.0).astype(BF)


def read_features(rx_ref, lane, first_rows, warped_rows):
    def first(i, carry):
        at = pl.ds(pl.multiple_of(i * COLS, COLS), COLS)
        one, two = two_rows(lane[:COLS], [rx_ref[q, at, :].astype(F32) for q in range(4)])
        first_rows(i, one.astype(BF))
        first_rows(i + 12, two.astype(BF))
        return carry
    lax.fori_loop(0, 12, first, 0)

    def second(i, carry):
        at = pl.ds(pl.multiple_of(12 * COLS + i * WIN, 16), WIN)
        one, two = two_rows(lane[:WIN], [rx_ref[q, at, :].astype(F32) for q in range(4)])
        warped_rows(i, one.astype(BF))
        warped_rows(i + 16, two.astype(BF))
        return carry
    lax.fori_loop(0, 16, second, 0)


def flip_four():
    i = lax.broadcasted_iota(jnp.int32, (4 * COLS, 4 * COLS), 0)
    j = lax.broadcasted_iota(jnp.int32, (4 * COLS, 4 * COLS), 1)
    here = ((i & (COLS - 1)) + (j & (COLS - 1)) == COLS - 1) & ((i & -COLS) == (j & -COLS))
    return jnp.where(here, 1.0, 0.0).astype(BF)


def cost_kernel(rx_ref, ex_ref, h0_ref, h1_ref, fs, ws, ms, vs, rs):
    lane = lax.broadcasted_iota(jnp.int32, (128, 128), 1)

    def put_first(i, value):
        fs[i] = value

    def put_warped(i, value):
        ws[i, 0:WIN] = value
    read_features(rx_ref, lane, put_first, put_warped)
    lane = lane[:COLS]
    flip = flip_four()

    for half, out in ((0, h0_ref), (1, h1_ref)):
        def group(g, carry, half=half, out=out):
            i = 12 * half + 4 * g
            ms[...] = nt(fs[pl.ds(i, 4)].reshape(4 * COLS, 256), ws[pl.ds(i, 12)].reshape(12 * 128, 256))
            for r in range(4):
                rows = slice(COLS * r, COLS * r + COLS)

                def band(dy, t, lo, hi, value, r=r, rows=rows):
                    block = slanted(ms[rows, 128 * (r + dy) : 128 * (r + dy) + 128], t - 63)
                    return jnp.where((lane >= lo) & (lane < hi), block * (1.0 / CH**0.5), value)
                for h in range(2):
                    value = fs[i + r, :, 128 * h : 128 * h + 128].astype(F32)
                    for s in range(2):
                        at = 64 * s + 49
                        value = band(2 * h + s, at, at, at + 9, value)
                        value = band(4 + 2 * h + s, at + 9, at + 9, at + 15, value)
                    vs[rows, 128 * h : 128 * h + 128] = value.astype(BF)
                value = jnp.zeros((COLS, 128), F32)
                for a in range(4):
                    value = band(4 + a, 3 * a - 6, 3 * a, 3 * a + 3, value)
                vs[rows, 256:384] = band(8, 12, 12, 21, value).astype(BF)
            turned = nn(flip, vs[...])
            for h in range(2):
                at = pl.multiple_of(768 * h + 4 * g * COLS, 4 * COLS)
                out[pl.ds(at, 4 * COLS), :] = turned[:, 128 * h : 128 * h + 128].astype(BF)
            rs[pl.ds(i, 4)] = turned[:, 256:384].reshape(4, COLS, 128) + ex_ref[pl.ds(i, 4)].astype(F32)
            return carry
        lax.fori_loop(0, 3, group, 0)
    for half, out in ((0, h0_ref), (1, h1_ref)):
        for b in range(3):
            total = rs[12 * half + b]
            for a in range(1, 4):
                total = total + pltpu.roll(rs[12 * half + 3 * a + b], 32 * a, 1)
            out[1536 + COLS * b : 1536 + COLS * b + COLS, :] = total.astype(BF)


def cost_volume(rx, extra):
    vm = pl.BlockSpec(memory_space=pltpu.VMEM)
    return pl.pallas_call(
        cost_kernel,
        out_shape=(jax.ShapeDtypeStruct((HALF, 128), BF),) * 2,
        in_specs=[vm] * 2,
        out_specs=(vm, vm),
        scratch_shapes=[
            pltpu.VMEM((ROWS, COLS, 256), BF),
            pltpu.VMEM((ROWS + 8, 128, 256), BF),
            pltpu.VMEM((4 * COLS, 12 * 128), F32),
            pltpu.VMEM((4 * COLS, 384), BF),
            pltpu.VMEM((ROWS, COLS, 128), F32),
        ],
        compiler_params=pltpu.CompilerParams(vmem_limit_bytes=32 * 2**20),
        name="cost_volume",
    )(rx, extra)


def cost_back_kernel(
    rx_ref, sh_hbm, w_hbm, wr_ref, o_ref, dr_ref, dm_ref, part, fs, ws, bs, gs, gw, sh, w_ref, sems
):
    loads = [pltpu.make_async_copy(sh_hbm, sh, sems.at[0]), pltpu.make_async_copy(w_hbm, w_ref, sems.at[1])]
    for load in loads:
        load.start()
    lane = lax.broadcasted_iota(jnp.int32, (128, 128), 1)
    zero = jnp.zeros((8, COLS, 256), BF)
    fs[0:8] = zero
    fs[32:40] = zero
    flip = flip_matrix()

    def put_first(i, value):
        fs[i + 8] = nn(flip, value).astype(BF)

    def put_warped(i, value):
        ws[i, 0:WIN] = value
        ws[i, WIN:] = jnp.zeros((128 - WIN, 256), BF)
    read_features(rx_ref, lane, put_first, put_warped)

    for load in loads:
        load.wait()

    def back_rest(i, carry):
        p = pl.multiple_of(i * 8 * PITCH, 8 * PITCH)
        total = None
        for dy in range(3):
            term = nn(sh[1, pl.ds(p + PITCH * (2 - dy), 8 * PITCH), :], wr_ref[dy])
            total = term if total is None else total + term
        part[...] = total
        for r in range(8):
            value = part[PITCH * r : PITCH * (r + 1), :]
            dr_ref[pl.ds(pl.multiple_of(p + PITCH * r, PITCH), PITCH), :] = (
                pltpu.roll(value, PITCH - 1, 0)
                + pltpu.roll(value, 96, 1)
                + pltpu.roll(pltpu.roll(value, 1, 0), 64, 1)
            )
        return carry
    lax.fori_loop(0, ROWS // 8, back_rest, 0)

    def back_main(i, carry):
        p = pl.multiple_of(i * 8 * PITCH, 8 * PITCH)
        total = None
        for dy in range(3):
            at = p + PITCH * (2 - dy)
            for dx in range(3):
                term = nn(sh[2 - dx, pl.ds(at, 8 * PITCH), :], w_ref[3 * dy + dx])
                total = term if total is None else total + term
        dm_ref[pl.ds(p, 8 * PITCH), :] = total.astype(BF)
        return carry
    lax.fori_loop(0, ROWS // 8, back_main, 0)

    def clear(i, carry):
        bs[i] = jnp.zeros((15, COLS, 128), BF)
        bs[i + 32] = jnp.zeros((15, COLS, 128), BF)
        return carry
    lax.fori_loop(0, 8, clear, 0)
    lane = lane[:COLS]
    ahead = lane - lax.broadcasted_iota(jnp.int32, (COLS, 128), 0)

    def row(i, carry):
        at = pl.ds(pl.multiple_of(i * PITCH + LEFT, 16), COLS)
        halves = [dm_ref[at, 128 * h : 128 * h + 128].astype(F32) for h in range(2)]
        rest = dr_ref[at, :].astype(BF).astype(F32)

        def band(source, t, lo, hi):
            shift = (-t) % 128
            extra = shift % 8
            block = pltpu.roll(source, shift - extra, 1, stride=1, stride_axis=0)
            block = jnp.where(((ahead + (extra - lo)) & 127) < hi - lo, block, 0.0)
            return pltpu.roll(block, extra, 1) if extra else block
        bs[i + 8, 0:3] = jnp.zeros((3, COLS, 128), BF)
        bs[i + 8, 12:15] = jnp.zeros((3, COLS, 128), BF)
        for dy in range(4):
            bs[i + 8, dy + 3] = band(halves[dy // 2], 64 * (dy % 2) + 49, 0, 9).astype(BF)
        for a in range(4):
            value = band(halves[a // 2], 64 * (a % 2) + 58, 0, 6) + band(rest, 3 * a - 6, 6, 9)
            bs[i + 8, a + 7] = value.astype(BF)
        bs[i + 8, 11] = band(rest, 12, 0, 9).astype(BF)
        return carry
    lax.fori_loop(0, ROWS, row, 0)

    def to_first(g, carry):
        i = 4 * g
        left = jnp.concatenate(
            [jnp.concatenate([bs[i + 8 + r, t - r + 3] for t in range(12)], axis=1) for r in range(4)], axis=0
        )
        total = nn(left, ws[pl.ds(i, 12)].reshape(12 * 128, 256)) * (1.0 / CH**0.5)
        for r in range(4):
            at = pl.ds(pl.multiple_of((i + r) * PITCH + LEFT, 16), COLS)
            gs[i + r] = total[COLS * r : COLS * r + COLS] + dm_ref[at, :].astype(F32)
        return carry
    lax.fori_loop(0, ROWS // 4, to_first, 0)

    def to_warped(g, carry):
        t = 4 * g
        left = jnp.concatenate(
            [jnp.concatenate([bs[t + m, 11 - m + n] for n in range(4)], axis=1) for m in range(12)], axis=0
        )
        right = fs[pl.ds(t, 12)].reshape(12 * COLS, 256)
        total = lax.dot_general(left, right, (((0,), (0,)), ((), ())), preferred_element_type=F32)
        gw[pl.ds(t, 4)] = (total * (1.0 / CH**0.5)).reshape(4, 128, 256)
        return carry
    lax.fori_loop(0, 8, to_warped, 0)

    def put(start, size, one, two):
        for z in range(4):
            h, odd = divmod(z, 2)
            a = one[:, 128 * h : 128 * h + 128]
            b = two[:, 128 * h : 128 * h + 128]
            if odd:
                a = pltpu.roll(a, 64, 1)
            else:
                b = pltpu.roll(b, 64, 1)
            low = lax.broadcasted_iota(jnp.int32, (size, 128), 1) < 64
            o_ref[z, pl.ds(start, size), :] = jnp.where(low, a, b).astype(BF)

    def send_first(i, carry):
        put(pl.multiple_of(i * COLS, COLS), COLS, gs[i], gs[i + 12])
        return carry
    lax.fori_loop(0, 12, send_first, 0)

    def send_warped(i, carry):
        put(pl.multiple_of(12 * COLS + i * WIN, 16), WIN, gw[i, 0:WIN], gw[i + 16, 0:WIN])
        return carry
    lax.fori_loop(0, 16, send_warped, 0)


def cost_back(rx, slopes, weight, weight_rest):
    vm = pl.BlockSpec(memory_space=pltpu.VMEM)
    hbm = pl.BlockSpec(memory_space=pl.ANY)
    size = ROWS * PITCH
    return pl.pallas_call(
        cost_back_kernel,
        out_shape=(jax.ShapeDtypeStruct((4, PAY, 128), BF), jax.ShapeDtypeStruct((size, 128), F32)),
        in_specs=[vm, hbm, hbm, vm],
        out_specs=(vm, vm),
        scratch_shapes=[
            pltpu.VMEM((size, 256), BF),
            pltpu.VMEM((8 * PITCH, 128), F32),
            pltpu.VMEM((ROWS + 16, COLS, 256), BF),
            pltpu.VMEM((ROWS + 8, 128, 256), BF),
            pltpu.VMEM((ROWS + 16, 15, COLS, 128), BF),
            pltpu.VMEM((ROWS, COLS, 256), F32),
            pltpu.VMEM((ROWS + 8, 128, 256), F32),
            pltpu.VMEM((3, (ROWS + 2) * PITCH, 512), BF),
            pltpu.VMEM((9, 512, 256), BF),
            pltpu.SemaphoreType.DMA((2,)),
        ],
        compiler_params=pltpu.CompilerParams(vmem_limit_bytes=VMEM_MB * 2**20),
        name="cost_back",
    )(rx, slopes, weight, weight_rest)


def turn_kernel(rp_ref, g1_ref, gw_ref, up_ref, down_ref, turn):
    eye = jnp.where(
        lax.broadcasted_iota(jnp.int32, (128, 128), 0) == lax.broadcasted_iota(jnp.int32, (128, 128), 1), 1.0, 0.0
    ).astype(BF)

    def first(i, carry):
        at = pl.ds(pl.multiple_of(i * COLS, COLS), COLS)
        value = nt(eye, jnp.concatenate([rp_ref[z, at, :] for z in range(4)], axis=0))
        g1_ref[i] = value[0:SLOT]
        g1_ref[i + 12] = value[SLOT:]
        return carry
    lax.fori_loop(0, 12, first, 0)

    def second(i, carry):
        at = pl.ds(pl.multiple_of(12 * COLS + i * WIN, 16), WIN)
        turn[...] = jnp.zeros(turn.shape, F32)
        for z in range(4):
            rows = slice(COLS * z + 4, COLS * z + 4 + WIN)
            turn[rows, :] = turn[rows, :] + rp_ref[z, at, :].astype(F32)
        value = jnp.transpose(turn[8:264, :])
        gw_ref[i] = value[0:SLOT]
        gw_ref[i + 16] = value[SLOT:]
        return carry
    lax.fori_loop(0, 16, second, 0)
    up_ref[...] = gw_ref[0:4].astype(BF)
    down_ref[...] = gw_ref[27:32].astype(BF)


def turn(rp):
    vm = pl.BlockSpec(memory_space=pltpu.VMEM)
    return pl.pallas_call(
        turn_kernel,
        out_shape=(
            jax.ShapeDtypeStruct((ROWS, SLOT, 256), F32),
            jax.ShapeDtypeStruct((ROWS + 8, SLOT, 256), F32),
            jax.ShapeDtypeStruct((4, SLOT, 256), BF),
            jax.ShapeDtypeStruct((5, SLOT, 256), BF),
        ),
        in_specs=[vm],
        out_specs=(vm,) * 4,
        scratch_shapes=[pltpu.VMEM((288, 128), F32)],
        compiler_params=pltpu.CompilerParams(vmem_limit_bytes=32 * 2**20),
        name="turn",
    )(rp)


def warp_back_kernel(gw_ref, from_above, from_below, f2_ref, above_ref, below_ref, g2_ref, gf_ref, full, band):
    first = lax.broadcasted_iota(jnp.int32, (SLOT, 256), 1) == 0
    last = lax.broadcasted_iota(jnp.int32, (SLOT, 256), 1) == 255
    channel = lax.broadcasted_iota(jnp.int32, (SLOT, 256), 0) < CH // 4
    band[0] = above_ref[3]
    band[1 : ROWS + 1] = f2_ref[...]
    band[ROWS + 1] = below_ref[0]
    full[...] = gw_ref[3:28]
    full[0:5] = full[0:5] + from_above[...].astype(F32)
    full[21:25] = full[21:25] + from_below[...].astype(F32)

    def spread(u, x):
        part = u * x
        return (x - part) + jnp.where(first, 0.0, pltpu.roll(part, 1, 1))

    def row(r, carry):
        upper = band[r + 1].astype(F32)
        lower = band[r + 2].astype(F32)
        before = band[r].astype(F32)
        u, v = upper[49:50], upper[50:51]
        grad = full[r + 1]
        g2_ref[r] = spread(u, (1.0 - v) * grad) + spread(before[49:50], before[50:51] * full[r])
        upper_next = jnp.where(last, 0.0, pltpu.roll(upper, 255, 1))
        lower_next = jnp.where(last, 0.0, pltpu.roll(lower, 255, 1))
        to_u = (1.0 - v) * (upper_next - upper) + v * (lower_next - lower)
        to_v = ((1.0 - u) * lower + u * lower_next) - ((1.0 - u) * upper + u * upper_next)
        along = jnp.sum(jnp.where(channel, grad * to_u, 0.0), axis=0, keepdims=True)
        down = jnp.sum(jnp.where(channel, grad * to_v, 0.0), axis=0, keepdims=True)
        gf_ref[r] = jnp.concatenate([along, down, jnp.zeros((6, 256), F32)], axis=0)
        return carry
    lax.fori_loop(0, ROWS, row, 0)


def warp_back(gw, from_above, from_below, f2, above, below):
    vm = pl.BlockSpec(memory_space=pltpu.VMEM)
    return pl.pallas_call(
        warp_back_kernel,
        out_shape=(
            jax.ShapeDtypeStruct((ROWS, SLOT, 256), F32),
            jax.ShapeDtypeStruct((ROWS, 8, 256), F32),
        ),
        in_specs=[vm] * 6,
        out_specs=(vm, vm),
        scratch_shapes=[pltpu.VMEM((ROWS + 1, SLOT, 256), F32), pltpu.VMEM((ROWS + 2, SLOT, 256), BF)],
        compiler_params=pltpu.CompilerParams(vmem_limit_bytes=32 * 2**20),
        name="warp_back",
    )(gw, from_above, from_below, f2, above, below)
WIDE, REST = lane_maps()
GATHER = gather_map()

PIX = ("xy", "core")


def ring(axis, steps):
    count = lax.axis_size(axis)
    return [(i, i + steps) for i in range(max(0, -steps), min(count, count - steps))]


def local(
    feat_one, feat_two, up_flow, up_feat, target_flow, valid_mask,
    conv_one, conv_two, conv_three, conv_four, conv_five, flow_head,
    bias_one, bias_two, bias_three, bias_four, bias_five, bias_head,
):
    convs = [conv_one, conv_two, conv_three, conv_four, conv_five, flow_head]
    biases = [bias_one, bias_two, bias_three, bias_four, bias_five, bias_head]
    channels = feat_one.shape[0]
    place = lax.axis_index("chan")
    f2 = jnp.concatenate([feat_two, up_flow, jnp.zeros((SLOT - channels - 2, ROWS, 256), BF)], axis=0)
    f2 = jnp.transpose(f2, (1, 0, 2))
    above = lax.ppermute(f2[ROWS - MD :], PIX, ring(PIX, 1))
    below = lax.ppermute(f2[: MD + 1], PIX, ring(PIX, -1))
    f1 = jnp.transpose(jnp.pad(feat_one, ((0, SLOT - channels), (0, 0), (0, 0))), (1, 0, 2))
    packed = pack(f1, f2, above, below)
    packed, convs, biases = lax.optimization_barrier((packed, convs, biases))
    features = lax.all_to_all(packed, "chan", split_axis=0, concat_axis=0, tiled=True)
    features, *weights = lax.optimization_barrier((features, *arrange(convs, biases)))

    flow_cols = lax.dynamic_slice_in_dim(up_flow, place * COLS, COLS, 2)
    high = target_flow.astype(BF)
    low = (target_flow - high.astype(F32)).astype(BF)
    one = jnp.ones((2, ROWS, COLS), BF)
    planes = jnp.concatenate([flow_cols, up_feat, one, valid_mask.astype(BF)[None], high, low], axis=0)
    extra = jnp.pad(jnp.transpose(planes, (1, 2, 0)), ((0, 0), (0, 0), (21, 96)))
    upper, lower = cost_volume(features, extra)
    top = lax.ppermute(lower, PIX, ring(PIX, 1))
    bottom = lax.ppermute(upper, PIX, ring(PIX, -1))
    tiles = [tile.reshape(27, COLS, 128) for tile in (top, upper, lower, bottom)]
    left = lax.ppermute(
        jnp.concatenate([tile[:, COLS - LEFT :] for tile in tiles], axis=0), "chan", ring("chan", 1)
    )
    right = lax.ppermute(
        jnp.concatenate([tile[:, :LEFT] for tile in tiles], axis=0), "chan", ring("chan", -1)
    )
    acts, slopes, main, rest, flow, sums = decode(
        top, upper, lower, bottom, left, right, *weights
    )
    core = lax.axis_index("core").astype(jnp.int32)[None]
    own, sent = wgrad(core, slopes, main, rest, acts, jnp.asarray(GATHER, BF))
    parts = chip_parts(own, sent, jnp.sum(sums[:, :, 96], axis=1))
    parts, slopes = lax.optimization_barrier((parts, slopes))
    parts = lax.all_to_all(parts, CHIPS, split_axis=0, concat_axis=0, tiled=True)
    payload, grad_rest = cost_back(features, slopes, weights[0], weights[2])
    parts, payload = lax.optimization_barrier((parts, payload))
    returned = lax.all_to_all(payload, "chan", split_axis=0, concat_axis=0, tiled=True)
    spread, notes = spread_total(parts)
    spread, returned = lax.optimization_barrier((spread, returned))
    mine = lax.all_to_all(spread, CHIPS, split_axis=0, concat_axis=0, tiled=True).reshape(HALF_ROWS, 128)
    grad_one, partial, to_above, to_below = turn(returned)
    from_above = lax.ppermute(to_below, PIX, ring(PIX, 1))
    from_below = lax.ppermute(to_above, PIX, ring(PIX, -1))
    grad_two, grad_flow = warp_back(partial, from_above, from_below, f2, above, below)
    grad_feat_one = jnp.transpose(grad_one[:, :channels], (1, 0, 2))
    grad_feat_two = jnp.transpose(grad_two[:, :channels], (1, 0, 2))
    flow_parts = jnp.transpose(grad_flow[:, :2], (1, 0, 2))
    total = lax.dynamic_slice_in_dim(flow_parts, place * COLS, COLS, 2)
    flow_parts = flow_parts.astype(BF)
    for step in range(1, 4):
        sent = lax.dynamic_slice_in_dim(flow_parts, lax.rem(place + step, 4) * COLS, COLS, 2)
        total = total + lax.ppermute(sent, "chan", [(i, (i + step) % 4) for i in range(4)]).astype(F32)

    def pixels(value):
        return jnp.transpose(value.reshape(ROWS, PITCH, -1)[:, LEFT : LEFT + COLS], (2, 0, 1))

    flow_out = pixels(flow[:, 96:98])
    small = pixels(grad_rest[:, 21:25])
    grad_up_flow = total + small[:2]
    mine, *outputs = lax.optimization_barrier(
        (mine, flow_out, grad_feat_one, grad_feat_two, grad_up_flow, small[2:])
    )
    flow_out, grad_feat_one, grad_feat_two, grad_up_flow, grad_up_feat = outputs
    weight_grads, bias_grads = unpack(core, mine, lax.ppermute(mine, "core", SWAP))
    scalars = jnp.sum(notes[:, :3], axis=0)
    bias_grads = [bias_grads[ROW0[n] : ROW0[n] + OUTS[n], 89] for n in range(6)]
    return (flow_out, scalars, grad_feat_one, grad_feat_two, grad_up_flow, grad_up_feat, *weight_grads, *bias_grads)


def solution(mesh):
    chan, pix = mesh.devices.shape
    cores = jax.sharding.Mesh(mesh.devices.reshape(chan, pix // 2, 2), ("chan", "xy", "core"))
    return jax.shard_map(
        local,
        mesh=cores,
        in_specs=(
            P("chan", PIX, None),
            P("chan", PIX, None),
            P(None, PIX, None),
            P(None, PIX, "chan"),
            P(None, PIX, "chan"),
            P(PIX, "chan"),
        )
        + (P(),) * 12,
        out_specs=(
            P(None, PIX, "chan"),
            P(),
            P("chan", PIX, None),
            P("chan", PIX, None),
            P(None, PIX, "chan"),
            P(None, PIX, "chan"),
        )
        + (P(),) * 12,
        check_vma=False,
    )
```

```python
import functools
import jax
import jax.numpy as jnp
import numpy as np
from jax import lax
from jax.experimental import pallas as pl
from jax.experimental.pallas import tpu as pltpu
from jax.sharding import PartitionSpec as P

CH = 196
MD = 4
CH_SLOT = 49
OUTS = (128, 128, 96, 64, 32, 2)
ROW0 = (0, 128, 256, 384, 448, 480)
DEPTH = (281, 409, 537, 633, 697, 729)


def start_lane(channel):
    if channel < 81:
        dy, dx = divmod(channel, 9)
        if dy < 4:
            return 0, 64 * dy + 55 + dx
        if dy < 8:
            if 2 <= dx < 8:
                return 0, 64 * (dy - 4) + 47 + dx
            return 1, 2 * (dy - 4) + dx
        return 1, 16 + dx
    if channel < 277:
        slot, inner = divmod(channel - 81, CH_SLOT)
        return 0, 64 * slot + inner
    return 1, 9 + 2 * (channel - 277)


def lane_maps():
    wide = np.zeros((729, 768), np.float32)
    rest = np.zeros((729, 128), np.float32)
    for c in range(729):
        if c < 32:
            wide[c, 704 + c] = 1
        elif c < 96:
            wide[c, 640 + c - 32] = 1
        elif c < 192:
            wide[c, 512 + c - 96] = 1
        elif c < 320:
            wide[c, 384 + c - 192] = 1
        elif c < 448:
            wide[c, 256 + c - 320] = 1
        else:
            block, lane = start_lane(c - 448)
            if block == 0:
                wide[c, lane] = 1
            else:
                rest[c, lane] = 1
    return wide, rest


def gather_map():
    table = np.zeros((1024, 768), np.float32)
    for c in range(281):
        block, lane = start_lane(c)
        table[288 * block + lane, 448 + c] = 1
    table[288 + 25, 729] = 1
    for i in range(128):
        table[384 + i, 320 + i] = 1
        table[512 + i, 192 + i] = 1
    for i in range(96):
        table[640 + i, 96 + i] = 1
    for i in range(64):
        table[768 + i, 32 + i] = 1
    for i in range(32):
        table[896 + 64 + i, i] = 1
    return table


def plane_map():
    table = np.zeros((11, 128), np.float32)
    for plane, lane in enumerate((9, 11, 13, 15, 25, 26, 27, 28, 29, 30, 31)):
        table[plane, lane] = 1
    return table

CH = 196
MD = 4
BF = jnp.bfloat16
F32 = jnp.float32
HALO = 12
PITCH = 96
ROWS = 24
COLS = 64
LEFT = 16
WROWS = ROWS + 2 * HALO
NPX = WROWS * PITCH
GUARD = 16
VMEM_MB = 62


def nt(a, b):
    return lax.dot_general(a, b, (((1,), (1,)), ((), ())), preferred_element_type=F32)


def nn(a, b):
    return lax.dot_general(a, b, (((1,), (0,)), ((), ())), preferred_element_type=F32)


def decode_kernel(
    top_ref, h0_ref, h1_ref, bottom_ref, left_ref, right_ref, wm_ref, w_ref, wr_ref,
    a_ref, g_ref, xm_ref, xr_ref, flow_ref, met_ref,
    xs, xq, sh, pre, part, mk, sems,
):
    lane = lax.broadcasted_iota(jnp.int32, (PITCH, 128), 1)
    core = pl.ds(HALO * PITCH, ROWS * PITCH)

    def rows(lo, hi, body, unroll=2):
        def step(i, carry):
            for u in range(unroll):
                body(pl.multiple_of(lo * PITCH + (i * unroll + u) * PITCH, PITCH))
            return carry
        lax.fori_loop(0, (hi - lo) // unroll, step, 0)

    def put_shifted(dst, p, lanes, value):
        height = value.shape[0]
        dst[0, pl.ds(p, PITCH), lanes] = pltpu.roll(value, 1, 0).astype(BF)
        dst[1, pl.ds(p, PITCH), lanes] = value.astype(BF)
        dst[2, pl.ds(p, PITCH), lanes] = pltpu.roll(value, height - 1, 0).astype(BF)

    def chunked(lo, hi, count, body):
        size = (hi - lo) * PITCH // count

        def step(i, carry):
            body(pl.multiple_of(lo * PITCH + i * size, 16), size)
            return carry
        lax.fori_loop(0, count, step, 0)

    for h, tile in enumerate((top_ref, h0_ref, h1_ref, bottom_ref)):
        def main_rows(i, carry, h=h, tile=tile):
            p = pl.multiple_of((12 * h + i) * PITCH, PITCH)
            for half in range(2):
                at = pl.multiple_of((12 * half + i) * COLS, COLS)
                value = jnp.concatenate(
                    [
                        left_ref[27 * h + 12 * half + i].astype(F32),
                        tile[pl.ds(at, COLS), :].astype(F32),
                        right_ref[27 * h + 12 * half + i].astype(F32),
                    ],
                    axis=0,
                )
                put_shifted(xs, p, slice(128 * half, 128 * half + 128), value)
            return carry
        lax.fori_loop(0, 12, main_rows, 0)

        def rest_rows(b, carry, h=h, tile=tile):
            packed = jnp.concatenate(
                [
                    left_ref[27 * h + 24 + b].astype(F32),
                    tile[pl.ds(pl.multiple_of(1536 + b * COLS, COLS), COLS), :].astype(F32),
                    right_ref[27 * h + 24 + b].astype(F32),
                ],
                axis=0,
            )
            for a in range(4):
                p = pl.multiple_of((12 * h + 3 * a + b) * PITCH, PITCH)
                value = jnp.where(lane < 32, pltpu.roll(packed, (128 - 32 * a) % 128, 1), 0.0)
                mk[pl.ds(p, PITCH), :] = jnp.broadcast_to(value[:, 25:26], (PITCH, 128))
                low = pltpu.roll(value, 1, 0)
                mid = pltpu.roll(value, 32, 1)
                high = pltpu.roll(pltpu.roll(value, PITCH - 1, 0), 64, 1)
                xq[pl.ds(p, PITCH), :] = (low + mid + high).astype(BF)
            return carry
        lax.fori_loop(0, 3, rest_rows, 0)

    keep = [
        pltpu.make_async_copy(xs.at[1, core, :], xm_ref, sems.at[1]),
        pltpu.make_async_copy(xq.at[core, :], xr_ref, sems.at[2]),
    ]
    for copy in keep:
        copy.start()

    def start_sums(lo, hi):
        p, size = lo * PITCH, (hi - lo) * PITCH
        left = jnp.concatenate([xq[pl.ds(p + PITCH * (dy - 1), size), :] for dy in range(3)], axis=1)
        total = nt(left, jnp.concatenate([wr_ref[dy] for dy in range(3)], axis=1))
        for dy in range(3):
            at = p + PITCH * (dy - 1)
            for dx in range(3):
                total = total + nt(xs[dx, pl.ds(at, size), :], wm_ref[3 * dy + dx])
        pre[pl.ds(p, size), :] = total

    first_lane = [0, 128, 256, 384, 384]
    lanes_of = [(0, 128), (0, 128), (0, 96), (0, 64), (64, 96)]
    kept = []

    def activate(layer, lo, hi):
        block = slice(first_lane[layer], first_lane[layer] + 128)
        inside = (lane >= lanes_of[layer][0]) & (lane < lanes_of[layer][1])
        piece = min(layer, 3)
        lanes = slice(128 * piece, 128 * piece + 128)
        for p in range(lo * PITCH, hi * PITCH, PITCH):
            value = pre[pl.ds(p, PITCH), block]
            sig = 0.5 * jnp.tanh(0.5 * value) + 0.5
            live = mk[pl.ds(p, PITCH), :] > 0.0
            if layer >= 3:
                live = live & inside
            act = value * sig
            slope = jnp.where(live, sig + act * (1.0 - sig), 0.0)
            if layer >= 3:
                slope = jnp.where(inside, slope, value)
            pre[pl.ds(p, PITCH), block] = slope
            put_shifted(sh, p, lanes, jnp.where(live, act, 0.0))

    def add_sums(layer, lo, hi):
        p, size = lo * PITCH, (hi - lo) * PITCH
        piece = min(layer, 3)
        out0 = min(128 * (layer + 1), 384)
        lanes = slice(128 * piece, 128 * piece + 128)
        left = jnp.concatenate(
            [sh[dx, pl.ds(p + PITCH * (dy - 1), size), lanes] for dy in range(3) for dx in range(3)], axis=1
        )
        right = jnp.concatenate([w_ref[k, out0:512, lanes] for k in range(9)], axis=1)
        pre[pl.ds(p, size), out0:512] = pre[pl.ds(p, size), out0:512] + nt(left, right)

    def bounds(lo, hi, shift):
        return [(lo, 18 - shift), (18 - shift, 33 - shift), (33 - shift, hi)]

    sums_of = [[functools.partial(start_sums, *r) for r in bounds(1, WROWS - 1, 0)]]
    for layer in range(5):
        sums_of.append(
            [functools.partial(add_sums, layer, *r) for r in bounds(layer + 2, WROWS - layer - 2, layer + 1)]
        )
    sums_of[0][0]()
    for layer in range(5):
        acts = [functools.partial(activate, layer, *r) for r in bounds(layer + 1, WROWS - layer - 1, layer)]
        sums_of[layer][1]()
        if layer == 4:
            kept[3].wait()
        acts[0]()
        sums_of[layer][2]()
        acts[1]()
        sums_of[layer + 1][0]()
        acts[2]()
        piece = min(layer, 3)
        copy = pltpu.make_async_copy(
            sh.at[1, core, 128 * piece : 128 * piece + 128],
            a_ref.at[:, 128 * layer : 128 * layer + 128],
            sems.at[3 + layer],
        )
        copy.start()
        kept.append(copy)
    sums_of[5][1]()
    sums_of[5][2]()

    is_flow = (lane >= 96) & (lane < 98)
    column = lax.broadcasted_iota(jnp.int32, (PITCH, 128), 0)
    core_column = (column >= LEFT) & (column < LEFT + COLS)
    met_ref[...] = jnp.zeros((3, PITCH, 128), F32)
    kept[0].wait()
    kept[1].wait()
    kept[2].wait()
    kept[4].wait()

    def loss(p):
        flow = pre[pl.ds(p, PITCH), 384:512]
        rest = xq[pl.ds(p, PITCH), :].astype(F32)
        target = pltpu.roll(rest, 96 - 60, 1) + pltpu.roll(rest, 96 - 62, 1)
        diff = jnp.where(is_flow, flow - target, 0.0)
        square = diff * diff
        other = jnp.where(lane == 96, pltpu.roll(square, 127, 1), pltpu.roll(square, 1, 1))
        error = jnp.sqrt(square + other + 1.0)
        mask = jnp.broadcast_to(rest[:, 59:60], (PITCH, 128))
        put_shifted(sh, p, slice(384, 512), jnp.where(is_flow, mask * diff / error, 0.0))
        return flow, mask, error

    def loss_rim(p):
        loss(p)

    def loss_core(p):
        flow, mask, error = loss(p)
        r = lax.div(p, PITCH) - HALO
        turned = jnp.transpose(flow)
        for n in range(2):
            flow_ref[n, pl.ds(r, 1), :] = turned[96 + n : 97 + n, LEFT : LEFT + COLS]
        mask = jnp.where(core_column, mask, 0.0)
        met_ref[0] += mask * (error - 1.0)
        met_ref[1] += mask / (1.0 + jnp.exp(-4.0 * (error - 2.0)))
        met_ref[2] += mask

    rows(6, HALO, loss_rim)
    rows(HALO, HALO + ROWS, loss_core)
    rows(HALO + ROWS, WROWS - 6, loss_rim)

    def back(layer, lo, hi):
        p, size = lo * PITCH, (hi - lo) * PITCH
        piece = min(layer, 3)
        out0 = min(128 * (layer + 1), 384)
        left = jnp.concatenate(
            [sh[2 - dx, pl.ds(p - PITCH * (dy - 1), size), out0:512] for dy in range(3) for dx in range(3)], axis=1
        )
        right = jnp.concatenate([w_ref[k, out0:512, 128 * piece : 128 * piece + 128] for k in range(9)], axis=0)
        part[pl.ds(p, size), :] = nn(left, right)

    def slope(layer, lo, hi):
        block = slice(first_lane[layer], first_lane[layer] + 128)
        inside = (lane >= lanes_of[layer][0]) & (lane < lanes_of[layer][1])
        piece = min(layer, 3)
        lanes = slice(128 * piece, 128 * piece + 128)
        for p in range(lo * PITCH, hi * PITCH, PITCH):
            value = part[pl.ds(p, PITCH), :] * pre[pl.ds(p, PITCH), block]
            if layer >= 3:
                value = jnp.where(inside, value, sh[1, pl.ds(p, PITCH), lanes].astype(F32))
            put_shifted(sh, p, lanes, value)

    def back_bounds(layer):
        lo, hi = HALO - layer - 1, HALO + ROWS + layer + 1
        return [(lo, 16 + layer), (16 + layer, 26 + layer), (26 + layer, hi)]

    back(4, *back_bounds(4)[0])
    for layer in range(4, -1, -1):
        parts = back_bounds(layer)
        back(layer, *parts[1])
        slope(layer, *parts[0])
        back(layer, *parts[2])
        slope(layer, *parts[1])
        if layer > 0:
            back(layer - 1, *back_bounds(layer - 1)[0])
        slope(layer, *parts[2])
        if layer < 4:
            lanes = slice(128 * layer, 128 * layer + 128)
            copy = pltpu.make_async_copy(
                sh.at[:, pl.ds((HALO - 1) * PITCH, (ROWS + 2) * PITCH), lanes], g_ref.at[:, :, lanes], sems.at[8 + layer]
            )
            copy.start()
            keep.append(copy)

    for copy in keep:
        copy.wait()


def decode(*operands):
    size = ROWS * PITCH
    vm = pl.BlockSpec(memory_space=pltpu.VMEM)
    hbm = pl.BlockSpec(memory_space=pl.ANY)
    return pl.pallas_call(
        decode_kernel,
        out_shape=(
            jax.ShapeDtypeStruct((size, 640), BF),
            jax.ShapeDtypeStruct((3, (ROWS + 2) * PITCH, 512), BF),
            jax.ShapeDtypeStruct((size, 256), BF),
            jax.ShapeDtypeStruct((size, 128), BF),
            jax.ShapeDtypeStruct((2, ROWS, COLS), F32),
            jax.ShapeDtypeStruct((3, PITCH, 128), F32),
        ),
        in_specs=[vm] * 9,
        out_specs=(hbm, hbm, hbm, hbm, vm, vm),
        scratch_shapes=[
            pltpu.VMEM((3, NPX, 256), BF),
            pltpu.VMEM((NPX, 128), BF),
            pltpu.VMEM((3, NPX, 512), BF),
            pltpu.VMEM((NPX, 512), F32),
            pltpu.VMEM((NPX, 128), F32),
            pltpu.VMEM((NPX, 128), F32),
            pltpu.SemaphoreType.DMA((12,)),
        ],
        compiler_params=pltpu.CompilerParams(vmem_limit_bytes=VMEM_MB * 2**20),
        name="decode",
    )(*operands)


def arrange_kernel(c1, c2, c3, c4, c5, c6, wide_ref, rest_ref, bias_ref, wm_ref, w_ref, wr_ref):
    for rows in (slice(352, 384), slice(480, 512)):
        wm_ref[:, rows, :] = jnp.zeros((9, 32, 256), BF)
        w_ref[:, rows, :] = jnp.zeros((9, 32, 512), BF)
    wr_ref[:, 352:384, :] = jnp.zeros((3, 32, 128), BF)
    wr_ref[:, 480:512, :] = jnp.zeros((3, 32, 128), BF)
    lane = lax.broadcasted_iota(jnp.int32, (512, 128), 1)
    bias = bias_ref[...]
    high = bias.astype(BF).astype(F32)
    bias = jnp.where(lane == 57, high, jnp.where(lane == 58, bias - high, 0.0))

    for n, ref in enumerate((c1, c2, c3, c4, c5, c6)):
        outs, depth = OUTS[n], DEPTH[n]
        rows = slice(ROW0[n], ROW0[n] + outs)
        wide = wide_ref[729 - depth :, :]
        rest = rest_ref[729 - depth :, :]
        dims = (((0,), (0,)), ((), ())) if n < 2 else (((1,), (0,)), ((), ()))
        for dy in range(3):
            total = bias[rows] if dy == 1 else jnp.zeros((outs, 128), F32)
            for dx in range(3):
                weight = ref[3 * dy + dx]
                value = lax.dot_general(weight, wide, dims, preferred_element_type=F32).astype(BF)
                wm_ref[3 * dy + dx, rows, :] = value[:, 0:256]
                w_ref[3 * dy + dx, rows, :] = value[:, 256:768]
                part = lax.dot_general(weight, rest, dims, preferred_element_type=F32)
                total = total + (pltpu.roll(part, 32 * dx, 1) if dx else part)
            wr_ref[dy, rows, :] = total.astype(BF)


def arrange(convs, biases):
    vm = pl.BlockSpec(memory_space=pltpu.VMEM)
    bias = jnp.concatenate(
        [biases[0], biases[1], biases[2], jnp.zeros((32,), F32), biases[3], biases[4], biases[5], jnp.zeros((30,), F32)]
    ).reshape(512, 1)
    turned = [jnp.transpose(convs[0], (0, 2, 1)), jnp.transpose(convs[1], (0, 2, 1))]
    return pl.pallas_call(
        arrange_kernel,
        out_shape=(
            jax.ShapeDtypeStruct((9, 512, 256), BF),
            jax.ShapeDtypeStruct((9, 512, 512), BF),
            jax.ShapeDtypeStruct((3, 512, 128), BF),
        ),
        in_specs=[vm] * 9,
        out_specs=(vm, vm, vm),
        compiler_params=pltpu.CompilerParams(vmem_limit_bytes=40 * 2**20),
        cost_estimate=pl.CostEstimate(flops=4 * 10**9, bytes_accessed=16 * 10**6, transcendentals=0),
        name="arrange",
    )(*turned, *convs[2:], jnp.asarray(WIDE, BF), jnp.asarray(REST, BF), bias)

TILE_ROWS = 2048
TOTAL_ROWS = 9 * TILE_ROWS
HALF_ROWS = TOTAL_ROWS // 2


def tn(a, b):
    return lax.dot_general(a, b, (((0,), (0,)), ((), ())), preferred_element_type=F32)


def wgrad_kernel(core_ref, g_hbm, xm_ref, xr_ref, a_ref, qp_ref, own_ref, sent_ref, g_ref, xp, o_ref, loads, stores):
    for d in range(3):
        pltpu.make_async_copy(g_hbm.at[d], g_ref.at[d], loads.at[d]).start()
    column = lax.broadcasted_iota(jnp.int32, (PITCH, 128), 0)
    core = (column >= LEFT) & (column < LEFT + COLS)
    core = jnp.concatenate([core] * 4, axis=0)
    size = 4 * PITCH

    def gather(i, carry):
        at = pl.ds(pl.multiple_of(i * size, size), size)
        left = jnp.concatenate([xm_ref[at, :], xr_ref[at, :], a_ref[at, 0:128]], axis=1)
        parts = [
            nn(a_ref[at, 128:640], qp_ref[512:1024, 0:256]),
            nn(a_ref[at, 0:256], qp_ref[384:640, 256:384]),
            nn(left, qp_ref[0:512, 384:768]),
        ]
        value = jnp.concatenate(parts, axis=1)
        for t in range(6):
            lanes = slice(128 * t, 128 * t + 128)
            xp[at, lanes] = jnp.where(core, value[:, lanes], 0.0).astype(BF)
        return carry
    lax.fori_loop(0, ROWS // 4, gather, 0)
    for d in range(3):
        pltpu.make_async_copy(g_hbm.at[d], g_ref.at[d], loads.at[d]).wait()

    part_rows = TILE_ROWS // 2

    def store(n, act):
        half, place = divmod(n, 9)
        for target, mine in ((own_ref, True), (sent_ref, False)):
            @pl.when((core_ref[0] == half) == mine)
            def _():
                act(
                    pltpu.make_async_copy(
                        o_ref.at[pl.ds(part_rows * n, part_rows), :],
                        target.at[pl.ds(part_rows * place, part_rows), :],
                        stores.at[n],
                    )
                )

    for k in range(9):
        dy, dx = divmod(k, 3)
        at = pl.ds(PITCH * (2 - dy), ROWS * PITCH)
        base = TILE_ROWS * k
        low = tn(g_ref[2 - dx, at, 0:256], xp[:, 256:768]).astype(BF)
        for t in range(3):
            o_ref[base + 128 * t : base + 128 * t + 128, :] = low[0:128, 128 * t + 128 : 128 * t + 256]
        for t in range(4):
            o_ref[base + 384 + 128 * t : base + 512 + 128 * t, :] = low[128:256, 128 * t : 128 * t + 128]
        low = tn(g_ref[2 - dx, at, 256:512], xp[...]).astype(BF)
        for t in range(5):
            o_ref[base + 896 + 96 * t : base + 992 + 96 * t, :] = low[0:96, 128 * t + 128 : 128 * t + 256]
        for t in range(6):
            o_ref[base + 1376 + 112 * t : base + 1488 + 112 * t, :] = low[128:240, 128 * t : 128 * t + 128]
        store(2 * k, lambda copy: copy.start())
        store(2 * k + 1, lambda copy: copy.start())
    for n in range(18):
        store(n, lambda copy: copy.wait())


def wgrad(core, g, xm, xr, a, qp):
    vm = pl.BlockSpec(memory_space=pltpu.VMEM)
    hbm = pl.BlockSpec(memory_space=pl.ANY)
    return pl.pallas_call(
        wgrad_kernel,
        out_shape=(jax.ShapeDtypeStruct((HALF_ROWS, 128), BF),) * 2,
        in_specs=[pl.BlockSpec(memory_space=pltpu.SMEM), hbm] + [vm] * 4,
        out_specs=(hbm, hbm),
        scratch_shapes=[
            pltpu.VMEM((3, (ROWS + 2) * PITCH, 512), BF),
            pltpu.VMEM((ROWS * PITCH, 768), BF),
            pltpu.VMEM((TOTAL_ROWS, 128), BF),
            pltpu.SemaphoreType.DMA((3,)),
            pltpu.SemaphoreType.DMA((18,)),
        ],
        compiler_params=pltpu.CompilerParams(vmem_limit_bytes=VMEM_MB * 2**20),
        name="wgrad",
    )(core, g, xm, xr, a, qp)

NOTE = 16


def half_sum_kernel(own_ref, got_ref, note_ref, got_note_ref, o_ref):
    count, height = o_ref.shape[0], o_ref.shape[1] - NOTE
    notes = jnp.concatenate([note_ref[0:8].astype(F32), got_note_ref[0:8].astype(F32)], axis=0).astype(BF)
    for b in range(count):
        rows = slice(height * b, height * (b + 1))
        o_ref[b, 0:height] = (own_ref[rows, :].astype(F32) + got_ref[rows, :].astype(F32)).astype(BF)
        o_ref[b, height:] = notes


def half_sum(own, got, note, got_note, count):
    height = HALF_ROWS // count
    steps = min(count, 16)
    block = HALF_ROWS // steps
    return pl.pallas_call(
        half_sum_kernel,
        grid=(steps,),
        in_specs=[
            pl.BlockSpec((block, 128), lambda i: (i, 0)),
            pl.BlockSpec((block, 128), lambda i: (i, 0)),
            pl.BlockSpec((NOTE, 128), lambda i: (0, 0)),
            pl.BlockSpec((NOTE, 128), lambda i: (0, 0)),
        ],
        out_specs=pl.BlockSpec((count // steps, height + NOTE, 128), lambda i: (i, 0, 0)),
        out_shape=jax.ShapeDtypeStruct((count, height + NOTE, 128), BF),
        name="half_sum",
    )(own, got, note, got_note)


def spread_kernel(parts_ref, o_ref, note_ref):
    count, height = o_ref.shape[0], o_ref.shape[1]

    def add(b, carry):
        total, notes = carry
        return total + parts_ref[b, 0:height].astype(F32), notes + parts_ref[b, height:].astype(F32)
    zero = (jnp.zeros((height, 128), F32), jnp.zeros((NOTE, 128), F32))
    total, notes = lax.fori_loop(0, count, add, zero)
    note_ref[...] = notes
    total = total.astype(BF)

    def put(b, carry):
        o_ref[b] = total
        return carry
    lax.fori_loop(0, count, put, 0)


def spread_total(parts):
    count, height, _ = parts.shape
    vm = pl.BlockSpec(memory_space=pltpu.VMEM)
    return pl.pallas_call(
        spread_kernel,
        out_shape=(
            jax.ShapeDtypeStruct((count, height - NOTE, 128), BF),
            jax.ShapeDtypeStruct((NOTE, 128), F32),
        ),
        in_specs=[vm],
        out_specs=(vm, vm),
        compiler_params=pltpu.CompilerParams(vmem_limit_bytes=32 * 2**20),
        name="spread_total",
    )(parts)


def unpack_kernel(
    core_ref, mine_ref, other_ref, o1, o2, o3, o4, o5, o6, b1, b2, b3, b4, b5, b6, all_ref, sems
):
    k = pl.program_id(0)

    @pl.when(k == 0)
    def _():
        core = core_ref[0]
        copies = [
            pltpu.make_async_copy(
                source, all_ref.at[pl.ds(pl.multiple_of(at * HALF_ROWS, HALF_ROWS), HALF_ROWS), :], sems.at[n]
            )
            for n, (source, at) in enumerate(((mine_ref, core), (other_ref, 1 - core)))
        ]
        for copy in copies:
            copy.start()
        for copy in copies:
            copy.wait()
    first = pl.multiple_of(k * TILE_ROWS, TILE_ROWS)

    def tiles(base, height, count):
        return jnp.concatenate(
            [all_ref[pl.ds(first + base + height * t, height), :].astype(F32) for t in range(count)], axis=1
        )
    o1[0] = jnp.transpose(tiles(0, 128, 3))[64 : 64 + 281]
    o2[0] = jnp.transpose(tiles(384, 128, 4))[64 : 64 + 409]
    o3[0] = tiles(896, 96, 5)[:, 64 : 64 + 537]
    last = tiles(1376, 112, 6)
    o4[0] = last[0:64, 96:729]
    o5[0] = last[64:96, 32:729]
    o6[0] = last[96:98, 0:729]

    @pl.when(k == 4)
    def _():
        biases = [tiles(256, 128, 1), tiles(768, 128, 1), tiles(1280, 96, 1), last[:, 640:768]]
        biases = [jnp.transpose(value)[89:90] for value in biases]
        b1[...] = biases[0]
        b2[...] = biases[1]
        b3[...] = biases[2]
        b4[...] = biases[3][:, 0:64]
        b5[...] = biases[3][:, 64:96]
        b6[...] = biases[3][:, 96:98]


def unpack(core, mine, other):
    shapes = ((281, 128), (409, 128), (96, 537), (64, 633), (32, 697), (2, 729))
    hbm = pl.BlockSpec(memory_space=pl.ANY)
    results = pl.pallas_call(
        unpack_kernel,
        grid_spec=pltpu.PrefetchScalarGridSpec(
            num_scalar_prefetch=1,
            grid=(9,),
            in_specs=[hbm, hbm],
            out_specs=tuple(pl.BlockSpec((1,) + s, lambda k, core: (k, 0, 0)) for s in shapes)
            + tuple(pl.BlockSpec((1, outs), lambda k, core: (0, 0)) for outs in OUTS),
            scratch_shapes=[pltpu.VMEM((TOTAL_ROWS, 128), BF), pltpu.SemaphoreType.DMA((2,))],
        ),
        out_shape=tuple(jax.ShapeDtypeStruct((9,) + s, F32) for s in shapes)
        + tuple(jax.ShapeDtypeStruct((1, outs), F32) for outs in OUTS),
        compiler_params=pltpu.CompilerParams(vmem_limit_bytes=32 * 2**20),
        name="unpack",
    )(core, mine, other)
    grads = list(results[:6])
    grads[0] = jnp.transpose(grads[0], (0, 2, 1))
    grads[1] = jnp.transpose(grads[1], (0, 2, 1))
    return grads, [bias.reshape(-1) for bias in results[6:]]


SWAP = [(0, 1), (1, 0)]
CHIPS = ("chan", "xy")


def chip_parts(own, sent, scalars):
    high = lax.reduce_precision(scalars, 8, 7)
    middle = lax.reduce_precision(scalars - high, 8, 7)
    low = scalars - high - middle
    note = jnp.stack([high, middle, low]).astype(BF)
    note = jnp.pad(note, ((0, NOTE - 3), (0, 128 - scalars.shape[0])))
    got_note = lax.ppermute(note, "core", SWAP)
    got = lax.ppermute(sent, "core", SWAP)
    return half_sum(own, got, note, got_note, lax.axis_size(CHIPS))

SLOT = 64
WIN = 80
PAY = 12 * COLS + 16 * WIN
HALF = 27 * COLS


def slanted(x, shift):
    shift = shift % 128
    if shift % 8:
        x = pltpu.roll(x, shift % 8, 1)
    return pltpu.roll(x, shift - shift % 8, 1, stride=1, stride_axis=0)


def two_rows(lane, parts):
    swap = [pltpu.roll(part, 64, 1) for part in parts]
    first = [jnp.where(lane < 64, parts[2 * h], swap[2 * h + 1]) for h in range(2)]
    second = [jnp.where(lane < 64, swap[2 * h], parts[2 * h + 1]) for h in range(2)]
    return jnp.concatenate(first, axis=1), jnp.concatenate(second, axis=1)


def diagonal(size, back):
    i = lax.broadcasted_iota(jnp.int32, (size, size), 0)
    j = lax.broadcasted_iota(jnp.int32, (size, size), 1)
    return jnp.where(i + j == size - 1 if back else i == j, 1.0, 0.0).astype(BF)


def pack_first_kernel(f1_ref, o_hbm, o_ref, sem):
    back = diagonal(256, True)

    def first(i, carry):
        both = jnp.concatenate([f1_ref[i], f1_ref[i + 12]], axis=0)
        value = nt(back, both).astype(BF)
        for z in range(4):
            o_ref[z, pl.ds(pl.multiple_of(i * COLS, COLS), COLS), :] = value[192 - COLS * z : 256 - COLS * z]
        return carry
    lax.fori_loop(0, 12, first, 0)
    copy = pltpu.make_async_copy(o_ref, o_hbm.at[:, pl.ds(0, 12 * COLS), :], sem)
    copy.start()
    copy.wait()


def pack_first(f1):
    return pl.pallas_call(
        pack_first_kernel,
        out_shape=jax.ShapeDtypeStruct((4, PAY, 128), BF),
        in_specs=[pl.BlockSpec(memory_space=pltpu.VMEM)],
        out_specs=pl.BlockSpec(memory_space=pl.ANY),
        scratch_shapes=[pltpu.VMEM((4, 12 * COLS, 128), BF), pltpu.SemaphoreType.DMA],
        compiler_params=pltpu.CompilerParams(vmem_limit_bytes=32 * 2**20),
        name="pack_first",
    )(f1)


def pack_warped_kernel(f2_ref, above_ref, below_ref, first_hbm, o_hbm, o_ref, band, turn, sem):
    eye = diagonal(256, False)
    last = lax.broadcasted_iota(jnp.int32, (SLOT, 256), 1) == 255
    channel = lax.broadcasted_iota(jnp.int32, (SLOT, 256), 0) < CH // 4
    band[0:MD] = above_ref[...]
    band[MD : MD + ROWS] = f2_ref[...]
    band[MD + ROWS :] = below_ref[...]
    turn[...] = jnp.zeros(turn.shape, F32)

    def warped(t):
        upper = band[t].astype(F32)
        lower = band[t + 1].astype(F32)
        u = upper[49:50]
        v = upper[50:51]

        def across(x):
            return (1.0 - u) * x + u * jnp.where(last, 0.0, pltpu.roll(x, 255, 1))
        value = (1.0 - v) * across(upper) + v * across(lower)
        return jnp.where(channel, value, 0.0).astype(BF)

    def second(i, carry):
        both = jnp.concatenate([warped(i), warped(i + 16)], axis=0)
        turn[8:264, :] = nt(eye, both)
        for z in range(4):
            start = pl.multiple_of(i * WIN, 16)
            o_ref[z, pl.ds(start, WIN), :] = turn[COLS * z + 4 : COLS * z + 4 + WIN, :].astype(BF)
        return carry
    lax.fori_loop(0, 16, second, 0)
    copy = pltpu.make_async_copy(o_ref, o_hbm.at[:, pl.ds(12 * COLS, 16 * WIN), :], sem)
    copy.start()
    copy.wait()


def pack_warped(f2, above, below, packed):
    vm = pl.BlockSpec(memory_space=pltpu.VMEM)
    hbm = pl.BlockSpec(memory_space=pl.ANY)
    return pl.pallas_call(
        pack_warped_kernel,
        out_shape=jax.ShapeDtypeStruct((4, PAY, 128), BF),
        in_specs=[vm, vm, vm, hbm],
        out_specs=hbm,
        input_output_aliases={3: 0},
        scratch_shapes=[
            pltpu.VMEM((4, 16 * WIN, 128), BF),
            pltpu.VMEM((33, SLOT, 256), BF),
            pltpu.VMEM((288, 128), F32),
            pltpu.SemaphoreType.DMA,
        ],
        compiler_params=pltpu.CompilerParams(vmem_limit_bytes=32 * 2**20),
        name="pack_warped",
    )(f2, above, below, packed)


def flip_matrix():
    total = lax.broadcasted_iota(jnp.int32, (COLS, COLS), 0) + lax.broadcasted_iota(jnp.int32, (COLS, COLS), 1)
    return jnp.where(total == COLS - 1, 1.0, 0.0).astype(BF)


def read_features(rx_ref, lane, first_rows, warped_rows):
    def first(i, carry):
        at = pl.ds(pl.multiple_of(i * COLS, COLS), COLS)
        one, two = two_rows(lane[:COLS], [rx_ref[q, at, :].astype(F32) for q in range(4)])
        first_rows(i, one.astype(BF))
        first_rows(i + 12, two.astype(BF))
        return carry
    lax.fori_loop(0, 12, first, 0)

    def second(i, carry):
        at = pl.ds(pl.multiple_of(12 * COLS + i * WIN, 16), WIN)
        one, two = two_rows(lane[:WIN], [rx_ref[q, at, :].astype(F32) for q in range(4)])
        warped_rows(i, one.astype(BF))
        warped_rows(i + 16, two.astype(BF))
        return carry
    lax.fori_loop(0, 16, second, 0)


def flip_four():
    i = lax.broadcasted_iota(jnp.int32, (4 * COLS, 4 * COLS), 0)
    j = lax.broadcasted_iota(jnp.int32, (4 * COLS, 4 * COLS), 1)
    here = ((i & (COLS - 1)) + (j & (COLS - 1)) == COLS - 1) & ((i & -COLS) == (j & -COLS))
    return jnp.where(here, 1.0, 0.0).astype(BF)


def cost_kernel(rx_ref, ex_ref, h0_ref, h1_ref, fs, ws, ms, vs, rs):
    lane = lax.broadcasted_iota(jnp.int32, (128, 128), 1)

    def put_first(i, value):
        fs[i] = value

    def put_warped(i, value):
        ws[i, 0:WIN] = value
    read_features(rx_ref, lane, put_first, put_warped)
    lane = lane[:COLS]
    flip = flip_four()

    for half, out in ((0, h0_ref), (1, h1_ref)):
        def group(g, carry, half=half, out=out):
            i = 12 * half + 4 * g
            ms[...] = nt(fs[pl.ds(i, 4)].reshape(4 * COLS, 256), ws[pl.ds(i, 12)].reshape(12 * 128, 256))
            for r in range(4):
                rows = slice(COLS * r, COLS * r + COLS)

                def band(dy, t, here, value, r=r, rows=rows):
                    block = slanted(ms[rows, 128 * (r + dy) : 128 * (r + dy) + 128], t - 63)
                    return jnp.where(here, block * (1.0 / CH**0.5), value)
                for h in range(2):
                    value = fs[i + r, :, 128 * h : 128 * h + 128].astype(F32)
                    for s in range(2):
                        at = 64 * s + 47
                        value = band(2 * h + s, at + 8, (lane >= at + 8) & (lane < at + 17), value)
                        value = band(4 + 2 * h + s, at, (lane >= at + 2) & (lane < at + 8), value)
                    vs[rows, 128 * h : 128 * h + 128] = value.astype(BF)
                value = jnp.zeros((COLS, 128), F32)
                for a in range(4):
                    here = (lane == 2 * a) | (lane == 2 * a + 1) | (lane == 2 * a + 8)
                    value = band(4 + a, 2 * a, here, value)
                vs[rows, 256:384] = band(8, 16, (lane >= 16) & (lane < 25), value).astype(BF)
            turned = nn(flip, vs[...])
            for h in range(2):
                at = pl.multiple_of(768 * h + 4 * g * COLS, 4 * COLS)
                out[pl.ds(at, 4 * COLS), :] = turned[:, 128 * h : 128 * h + 128].astype(BF)
            rs[pl.ds(i, 4)] = turned[:, 256:384].reshape(4, COLS, 128) + ex_ref[pl.ds(i, 4)].astype(F32)
            return carry
        lax.fori_loop(0, 3, group, 0)
    for half, out in ((0, h0_ref), (1, h1_ref)):
        for b in range(3):
            total = rs[12 * half + b]
            for a in range(1, 4):
                total = total + pltpu.roll(rs[12 * half + 3 * a + b], 32 * a, 1)
            out[1536 + COLS * b : 1536 + COLS * b + COLS, :] = total.astype(BF)


def cost_volume(rx, extra):
    vm = pl.BlockSpec(memory_space=pltpu.VMEM)
    return pl.pallas_call(
        cost_kernel,
        out_shape=(jax.ShapeDtypeStruct((HALF, 128), BF),) * 2,
        in_specs=[vm] * 2,
        out_specs=(vm, vm),
        scratch_shapes=[
            pltpu.VMEM((ROWS, COLS, 256), BF),
            pltpu.VMEM((ROWS + 8, 128, 256), BF),
            pltpu.VMEM((4 * COLS, 12 * 128), F32),
            pltpu.VMEM((4 * COLS, 384), BF),
            pltpu.VMEM((ROWS, COLS, 128), F32),
        ],
        compiler_params=pltpu.CompilerParams(vmem_limit_bytes=32 * 2**20),
        name="cost_volume",
    )(rx, extra)


def cost_back_kernel(
    rx_ref, sh_hbm, w_hbm, wr_ref, o_ref, plane_ref, dr_ref, dm_ref, part, fs, ws, bs, gs, gw, sh, w_ref, sems
):
    loads = [pltpu.make_async_copy(sh_hbm, sh, sems.at[0]), pltpu.make_async_copy(w_hbm, w_ref, sems.at[1])]
    for load in loads:
        load.start()
    lane = lax.broadcasted_iota(jnp.int32, (128, 128), 1)
    zero = jnp.zeros((8, COLS, 256), BF)
    fs[0:8] = zero
    fs[32:40] = zero
    flip = flip_matrix()

    def put_first(i, value):
        fs[i + 8] = nn(flip, value).astype(BF)

    def put_warped(i, value):
        ws[i, 0:WIN] = value
        ws[i, WIN:] = jnp.zeros((128 - WIN, 256), BF)
    read_features(rx_ref, lane, put_first, put_warped)

    for load in loads:
        load.wait()

    def back_rest(i, carry):
        p = pl.multiple_of(i * 8 * PITCH, 8 * PITCH)
        total = None
        for dy in range(3):
            term = nn(sh[1, pl.ds(p + PITCH * (2 - dy), 8 * PITCH), :], wr_ref[dy])
            total = term if total is None else total + term
        part[...] = total
        for r in range(8):
            value = part[PITCH * r : PITCH * (r + 1), :]
            value = (
                pltpu.roll(value, PITCH - 1, 0)
                + pltpu.roll(value, 96, 1)
                + pltpu.roll(pltpu.roll(value, 1, 0), 64, 1)
            )
            dr_ref[pl.ds(pl.multiple_of(p + PITCH * r, PITCH), PITCH), :] = value
            turned = jnp.transpose(value)
            for n in range(4):
                plane_ref[n, pl.ds(8 * i + r, 1), :] = turned[9 + 2 * n : 10 + 2 * n, LEFT : LEFT + COLS]
        return carry
    lax.fori_loop(0, ROWS // 8, back_rest, 0)

    def back_main(i, carry):
        p = pl.multiple_of(i * 8 * PITCH, 8 * PITCH)
        total = None
        for dy in range(3):
            at = p + PITCH * (2 - dy)
            for dx in range(3):
                term = nn(sh[2 - dx, pl.ds(at, 8 * PITCH), :], w_ref[3 * dy + dx])
                total = term if total is None else total + term
        dm_ref[pl.ds(p, 8 * PITCH), :] = total.astype(BF)
        return carry
    lax.fori_loop(0, ROWS // 8, back_main, 0)

    def clear(i, carry):
        bs[i] = jnp.zeros((15, COLS, 128), BF)
        bs[i + 32] = jnp.zeros((15, COLS, 128), BF)
        return carry
    lax.fori_loop(0, 8, clear, 0)
    lane = lane[:COLS]
    ahead = lane - lax.broadcasted_iota(jnp.int32, (COLS, 128), 0)

    def row(i, carry):
        at = pl.ds(pl.multiple_of(i * PITCH + LEFT, 16), COLS)
        halves = [pltpu.roll(dm_ref[at, 128 * h : 128 * h + 128].astype(F32), 1, 1) for h in range(2)]
        rest = dr_ref[at, :].astype(BF).astype(F32)

        def band(source, t, first, last, far=None):
            shift = (-t) % 128
            extra = shift % 8
            block = pltpu.roll(source, shift - extra, 1, stride=1, stride_axis=0)
            offset = (ahead + extra) & 127
            here = (offset >= first) & (offset <= last)
            if far is not None:
                here = here | (offset == far)
            block = jnp.where(here, block, 0.0)
            return pltpu.roll(block, extra, 1) if extra else block
        bs[i + 8, 0:3] = jnp.zeros((3, COLS, 128), BF)
        bs[i + 8, 12:15] = jnp.zeros((3, COLS, 128), BF)
        for dy in range(4):
            bs[i + 8, dy + 3] = band(halves[dy // 2], 64 * (dy % 2) + 56, 0, 8).astype(BF)
        for a in range(4):
            value = band(halves[a // 2], 64 * (a % 2) + 48, 2, 7) + band(rest, 2 * a, 0, 1, 8)
            bs[i + 8, a + 7] = value.astype(BF)
        bs[i + 8, 11] = band(rest, 16, 0, 8).astype(BF)
        return carry
    lax.fori_loop(0, ROWS, row, 0)

    def to_first(g, carry):
        i = 4 * g
        left = jnp.concatenate(
            [jnp.concatenate([bs[i + 8 + r, t - r + 3] for t in range(12)], axis=1) for r in range(4)], axis=0
        )
        total = nn(left, ws[pl.ds(i, 12)].reshape(12 * 128, 256)) * (1.0 / CH**0.5)
        for r in range(4):
            at = pl.ds(pl.multiple_of((i + r) * PITCH + LEFT, 16), COLS)
            gs[i + r] = total[COLS * r : COLS * r + COLS] + dm_ref[at, :].astype(F32)
        return carry
    lax.fori_loop(0, ROWS // 4, to_first, 0)

    def to_warped(g, carry):
        t = 4 * g
        left = jnp.concatenate(
            [jnp.concatenate([bs[t + m, 11 - m + n] for n in range(4)], axis=1) for m in range(12)], axis=0
        )
        right = fs[pl.ds(t, 12)].reshape(12 * COLS, 256)
        total = lax.dot_general(left, right, (((0,), (0,)), ((), ())), preferred_element_type=F32)
        gw[pl.ds(t, 4)] = (total * (1.0 / CH**0.5)).reshape(4, 128, 256)
        return carry
    lax.fori_loop(0, 8, to_warped, 0)

    def put(start, size, one, two):
        for z in range(4):
            h, odd = divmod(z, 2)
            a = one[:, 128 * h : 128 * h + 128]
            b = two[:, 128 * h : 128 * h + 128]
            if odd:
                a = pltpu.roll(a, 64, 1)
            else:
                b = pltpu.roll(b, 64, 1)
            low = lax.broadcasted_iota(jnp.int32, (size, 128), 1) < 64
            o_ref[z, pl.ds(start, size), :] = jnp.where(low, a, b).astype(BF)

    def send_first(i, carry):
        put(pl.multiple_of(i * COLS, COLS), COLS, gs[i], gs[i + 12])
        return carry
    lax.fori_loop(0, 12, send_first, 0)

    def send_warped(i, carry):
        put(pl.multiple_of(12 * COLS + i * WIN, 16), WIN, gw[i, 0:WIN], gw[i + 16, 0:WIN])
        return carry
    lax.fori_loop(0, 16, send_warped, 0)


def cost_back(rx, slopes, weight, weight_rest):
    vm = pl.BlockSpec(memory_space=pltpu.VMEM)
    hbm = pl.BlockSpec(memory_space=pl.ANY)
    size = ROWS * PITCH
    return pl.pallas_call(
        cost_back_kernel,
        out_shape=(jax.ShapeDtypeStruct((4, PAY, 128), BF), jax.ShapeDtypeStruct((4, ROWS, COLS), F32)),
        in_specs=[vm, hbm, hbm, vm],
        out_specs=(vm, vm),
        scratch_shapes=[
            pltpu.VMEM((size, 128), F32),
            pltpu.VMEM((size, 256), BF),
            pltpu.VMEM((8 * PITCH, 128), F32),
            pltpu.VMEM((ROWS + 16, COLS, 256), BF),
            pltpu.VMEM((ROWS + 8, 128, 256), BF),
            pltpu.VMEM((ROWS + 16, 15, COLS, 128), BF),
            pltpu.VMEM((ROWS, COLS, 256), F32),
            pltpu.VMEM((ROWS + 8, 128, 256), F32),
            pltpu.VMEM((3, (ROWS + 2) * PITCH, 512), BF),
            pltpu.VMEM((9, 512, 256), BF),
            pltpu.SemaphoreType.DMA((2,)),
        ],
        compiler_params=pltpu.CompilerParams(vmem_limit_bytes=VMEM_MB * 2**20),
        name="cost_back",
    )(rx, slopes, weight, weight_rest)


def turn_kernel(rp_ref, g1_ref, gw_ref, up_ref, down_ref, turn):
    eye = jnp.where(
        lax.broadcasted_iota(jnp.int32, (128, 128), 0) == lax.broadcasted_iota(jnp.int32, (128, 128), 1), 1.0, 0.0
    ).astype(BF)

    def first(i, carry):
        at = pl.ds(pl.multiple_of(i * COLS, COLS), COLS)
        value = nt(eye, jnp.concatenate([rp_ref[z, at, :] for z in range(4)], axis=0))
        g1_ref[i] = value[0:SLOT]
        g1_ref[i + 12] = value[SLOT:]
        return carry
    lax.fori_loop(0, 12, first, 0)

    def second(i, carry):
        at = pl.ds(pl.multiple_of(12 * COLS + i * WIN, 16), WIN)
        turn[...] = jnp.zeros(turn.shape, F32)
        for z in range(4):
            rows = slice(COLS * z + 4, COLS * z + 4 + WIN)
            turn[rows, :] = turn[rows, :] + rp_ref[z, at, :].astype(F32)
        value = jnp.transpose(turn[8:264, :])
        gw_ref[i] = value[0:SLOT]
        gw_ref[i + 16] = value[SLOT:]
        return carry
    lax.fori_loop(0, 16, second, 0)
    up_ref[...] = gw_ref[0:4].astype(BF)
    down_ref[...] = gw_ref[27:32].astype(BF)


def turn(rp):
    vm = pl.BlockSpec(memory_space=pltpu.VMEM)
    return pl.pallas_call(
        turn_kernel,
        out_shape=(
            jax.ShapeDtypeStruct((ROWS, SLOT, 256), F32),
            jax.ShapeDtypeStruct((ROWS + 8, SLOT, 256), F32),
            jax.ShapeDtypeStruct((4, SLOT, 256), BF),
            jax.ShapeDtypeStruct((5, SLOT, 256), BF),
        ),
        in_specs=[vm],
        out_specs=(vm,) * 4,
        scratch_shapes=[pltpu.VMEM((288, 128), F32)],
        compiler_params=pltpu.CompilerParams(vmem_limit_bytes=32 * 2**20),
        name="turn",
    )(rp)


def warp_back_kernel(gw_ref, from_above, from_below, f2_ref, above_ref, below_ref, g2_ref, gf_ref, full, band):
    first = lax.broadcasted_iota(jnp.int32, (SLOT, 256), 1) == 0
    last = lax.broadcasted_iota(jnp.int32, (SLOT, 256), 1) == 255
    channel = lax.broadcasted_iota(jnp.int32, (SLOT, 256), 0) < CH // 4
    band[0] = above_ref[3]
    band[1 : ROWS + 1] = f2_ref[...]
    band[ROWS + 1] = below_ref[0]
    full[...] = gw_ref[3:28]
    full[0:5] = full[0:5] + from_above[...].astype(F32)
    full[21:25] = full[21:25] + from_below[...].astype(F32)

    def spread(u, x):
        part = u * x
        return (x - part) + jnp.where(first, 0.0, pltpu.roll(part, 1, 1))

    def row(r, carry):
        upper = band[r + 1].astype(F32)
        lower = band[r + 2].astype(F32)
        before = band[r].astype(F32)
        u, v = upper[49:50], upper[50:51]
        grad = full[r + 1]
        g2_ref[r] = spread(u, (1.0 - v) * grad) + spread(before[49:50], before[50:51] * full[r])
        upper_next = jnp.where(last, 0.0, pltpu.roll(upper, 255, 1))
        lower_next = jnp.where(last, 0.0, pltpu.roll(lower, 255, 1))
        to_u = (1.0 - v) * (upper_next - upper) + v * (lower_next - lower)
        to_v = ((1.0 - u) * lower + u * lower_next) - ((1.0 - u) * upper + u * upper_next)
        along = jnp.sum(jnp.where(channel, grad * to_u, 0.0), axis=0, keepdims=True)
        down = jnp.sum(jnp.where(channel, grad * to_v, 0.0), axis=0, keepdims=True)
        gf_ref[r] = jnp.concatenate([along, down, jnp.zeros((6, 256), F32)], axis=0)
        return carry
    lax.fori_loop(0, ROWS, row, 0)


def warp_back(gw, from_above, from_below, f2, above, below):
    vm = pl.BlockSpec(memory_space=pltpu.VMEM)
    return pl.pallas_call(
        warp_back_kernel,
        out_shape=(
            jax.ShapeDtypeStruct((ROWS, SLOT, 256), F32),
            jax.ShapeDtypeStruct((ROWS, 8, 256), F32),
        ),
        in_specs=[vm] * 6,
        out_specs=(vm, vm),
        scratch_shapes=[pltpu.VMEM((ROWS + 1, SLOT, 256), F32), pltpu.VMEM((ROWS + 2, SLOT, 256), BF)],
        compiler_params=pltpu.CompilerParams(vmem_limit_bytes=32 * 2**20),
        name="warp_back",
    )(gw, from_above, from_below, f2, above, below)
WIDE, REST = lane_maps()
GATHER = gather_map()
PLANES = plane_map()

PIX = ("xy", "core")


def ring(axis, steps):
    count = lax.axis_size(axis)
    return [(i, i + steps) for i in range(max(0, -steps), min(count, count - steps))]


def local(
    feat_one, feat_two, up_flow, up_feat, target_flow, valid_mask,
    conv_one, conv_two, conv_three, conv_four, conv_five, flow_head,
    bias_one, bias_two, bias_three, bias_four, bias_five, bias_head,
):
    convs = [conv_one, conv_two, conv_three, conv_four, conv_five, flow_head]
    biases = [bias_one, bias_two, bias_three, bias_four, bias_five, bias_head]
    channels = feat_one.shape[0]
    place = lax.axis_index("chan")
    f2 = jnp.concatenate([feat_two, up_flow, jnp.zeros((SLOT - channels - 2, ROWS, 256), BF)], axis=0)
    f2 = jnp.transpose(f2, (1, 0, 2))
    above = lax.ppermute(f2[ROWS - MD :], PIX, ring(PIX, 1))
    below = lax.ppermute(f2[: MD + 1], PIX, ring(PIX, -1))
    f1 = jnp.transpose(jnp.pad(feat_one, ((0, SLOT - channels), (0, 0), (0, 0))), (1, 0, 2))
    packed = pack_warped(f2, above, below, pack_first(f1))
    packed, biases = lax.optimization_barrier((packed, biases))
    features = lax.all_to_all(packed, "chan", split_axis=0, concat_axis=0, tiled=True)
    features, *weights = lax.optimization_barrier((features, *arrange(convs, biases)))

    flow_cols = lax.dynamic_slice_in_dim(up_flow, place * COLS, COLS, 2)
    high = target_flow.astype(BF)
    low = (target_flow - high.astype(F32)).astype(BF)
    one = jnp.ones((2, ROWS, COLS), BF)
    planes = jnp.concatenate([flow_cols, up_feat, one, valid_mask.astype(BF)[None], high, low], axis=0)
    extra = lax.dot_general(
        planes, jnp.asarray(PLANES, BF), (((0,), (0,)), ((), ())), preferred_element_type=F32
    ).astype(BF)
    upper, lower = cost_volume(features, extra)
    top = lax.ppermute(lower, PIX, ring(PIX, 1))
    bottom = lax.ppermute(upper, PIX, ring(PIX, -1))
    tiles = [tile.reshape(27, COLS, 128) for tile in (top, upper, lower, bottom)]
    left = lax.ppermute(
        jnp.concatenate([tile[:, COLS - LEFT :] for tile in tiles], axis=0), "chan", ring("chan", 1)
    )
    right = lax.ppermute(
        jnp.concatenate([tile[:, :LEFT] for tile in tiles], axis=0), "chan", ring("chan", -1)
    )
    acts, slopes, main, rest, flow_out, sums = decode(
        top, upper, lower, bottom, left, right, *weights
    )
    core = lax.axis_index("core").astype(jnp.int32)[None]
    own, sent = wgrad(core, slopes, main, rest, acts, jnp.asarray(GATHER, BF))
    parts = chip_parts(own, sent, jnp.sum(sums[:, :, 96], axis=1))
    parts, slopes = lax.optimization_barrier((parts, slopes))
    parts = lax.all_to_all(parts, CHIPS, split_axis=0, concat_axis=0, tiled=True)
    payload, small = cost_back(features, slopes, weights[0], weights[2])
    parts, payload = lax.optimization_barrier((parts, payload))
    returned = lax.all_to_all(payload, "chan", split_axis=0, concat_axis=0, tiled=True)
    spread, notes = spread_total(parts)
    spread, returned = lax.optimization_barrier((spread, returned))
    mine = lax.all_to_all(spread, CHIPS, split_axis=0, concat_axis=0, tiled=True).reshape(HALF_ROWS, 128)
    grad_one, partial, to_above, to_below = turn(returned)
    from_above = lax.ppermute(to_below, PIX, ring(PIX, 1))
    from_below = lax.ppermute(to_above, PIX, ring(PIX, -1))
    grad_two, grad_flow = warp_back(partial, from_above, from_below, f2, above, below)
    grad_feat_one = jnp.transpose(grad_one[:, :channels], (1, 0, 2))
    grad_feat_two = jnp.transpose(grad_two[:, :channels], (1, 0, 2))
    flow_parts = jnp.transpose(grad_flow[:, :2], (1, 0, 2))
    total = lax.dynamic_slice_in_dim(flow_parts, place * COLS, COLS, 2)
    flow_parts = flow_parts.astype(BF)
    for step in range(1, 4):
        sent = lax.dynamic_slice_in_dim(flow_parts, lax.rem(place + step, 4) * COLS, COLS, 2)
        total = total + lax.ppermute(sent, "chan", [(i, (i + step) % 4) for i in range(4)]).astype(F32)

    grad_up_flow = total + small[:2]
    mine, *outputs = lax.optimization_barrier(
        (mine, flow_out, grad_feat_one, grad_feat_two, grad_up_flow, small[2:])
    )
    flow_out, grad_feat_one, grad_feat_two, grad_up_flow, grad_up_feat = outputs
    weight_grads, bias_grads = unpack(core, mine, lax.ppermute(mine, "core", SWAP))
    scalars = jnp.sum(notes[:, :3], axis=0)
    return (flow_out, scalars, grad_feat_one, grad_feat_two, grad_up_flow, grad_up_feat, *weight_grads, *bias_grads)


def solution(mesh):
    chan, pix = mesh.devices.shape
    cores = jax.sharding.Mesh(mesh.devices.reshape(chan, pix // 2, 2), ("chan", "xy", "core"))
    return jax.shard_map(
        local,
        mesh=cores,
        in_specs=(
            P("chan", PIX, None),
            P("chan", PIX, None),
            P(None, PIX, None),
            P(None, PIX, "chan"),
            P(None, PIX, "chan"),
            P(PIX, "chan"),
        )
        + (P(),) * 12,
        out_specs=(
            P(None, PIX, "chan"),
            P(),
            P("chan", PIX, None),
            P("chan", PIX, None),
            P(None, PIX, "chan"),
            P(None, PIX, "chan"),
        )
        + (P(),) * 12,
        check_vma=False,
    )
```

```python
import functools
import jax
import jax.numpy as jnp
import numpy as np
from jax import lax
from jax.experimental import pallas as pl
from jax.experimental.pallas import tpu as pltpu
from jax.sharding import PartitionSpec as P

CH = 196
MD = 4
CH_SLOT = 49
OUTS = (128, 128, 96, 64, 32, 2)
ROW0 = (0, 128, 256, 384, 448, 480)
DEPTH = (281, 409, 537, 633, 697, 729)


def start_lane(channel):
    if channel < 81:
        dy, dx = divmod(channel, 9)
        if dy < 4:
            return 0, 64 * dy + 55 + dx
        if dy < 8:
            if 2 <= dx < 8:
                return 0, 64 * (dy - 4) + 47 + dx
            return 1, 2 * (dy - 4) + dx
        return 1, 16 + dx
    if channel < 277:
        slot, inner = divmod(channel - 81, CH_SLOT)
        return 0, 64 * slot + inner
    return 1, 9 + 2 * (channel - 277)


def lane_maps():
    wide = np.zeros((729, 768), np.float32)
    rest = np.zeros((729, 128), np.float32)
    for c in range(729):
        if c < 32:
            wide[c, 704 + c] = 1
        elif c < 96:
            wide[c, 640 + c - 32] = 1
        elif c < 192:
            wide[c, 512 + c - 96] = 1
        elif c < 320:
            wide[c, 384 + c - 192] = 1
        elif c < 448:
            wide[c, 256 + c - 320] = 1
        else:
            block, lane = start_lane(c - 448)
            if block == 0:
                wide[c, lane] = 1
            else:
                rest[c, lane] = 1
    return wide, rest


def gather_map():
    table = np.zeros((1024, 768), np.float32)
    for c in range(281):
        block, lane = start_lane(c)
        table[288 * block + lane, 448 + c] = 1
    table[288 + 25, 729] = 1
    for i in range(128):
        table[384 + i, 320 + i] = 1
        table[512 + i, 192 + i] = 1
    for i in range(96):
        table[640 + i, 96 + i] = 1
    for i in range(64):
        table[768 + i, 32 + i] = 1
    for i in range(32):
        table[896 + 64 + i, i] = 1
    return table


def plane_map():
    table = np.zeros((11, 128), np.float32)
    for plane, lane in enumerate((9, 11, 13, 15, 25, 26, 27, 28, 29, 30, 31)):
        table[plane, lane] = 1
    return table

CH = 196
MD = 4
BF = jnp.bfloat16
F32 = jnp.float32
HALO = 12
PITCH = 96
ROWS = 24
COLS = 64
LEFT = 16
WROWS = ROWS + 2 * HALO
NPX = WROWS * PITCH
GUARD = 16
VMEM_MB = 62


def nt(a, b):
    return lax.dot_general(a, b, (((1,), (1,)), ((), ())), preferred_element_type=F32)


def nn(a, b):
    return lax.dot_general(a, b, (((1,), (0,)), ((), ())), preferred_element_type=F32)


def decode_kernel(
    top_ref, h0_ref, h1_ref, bottom_ref, left_ref, right_ref, wm_ref, w_ref, wr_ref,
    a_ref, g_ref, xm_ref, xr_ref, flow_ref, met_ref,
    xs, xq, sh, pre, part, mk, sems,
):
    lane = lax.broadcasted_iota(jnp.int32, (PITCH, 128), 1)
    core = pl.ds(HALO * PITCH, ROWS * PITCH)

    def rows(lo, hi, body, unroll=2):
        def step(i, carry):
            for u in range(unroll):
                body(pl.multiple_of(lo * PITCH + (i * unroll + u) * PITCH, PITCH))
            return carry
        lax.fori_loop(0, (hi - lo) // unroll, step, 0)

    def put_shifted(dst, p, lanes, value):
        height = value.shape[0]
        dst[0, pl.ds(p, PITCH), lanes] = pltpu.roll(value, 1, 0).astype(BF)
        dst[1, pl.ds(p, PITCH), lanes] = value.astype(BF)
        dst[2, pl.ds(p, PITCH), lanes] = pltpu.roll(value, height - 1, 0).astype(BF)

    def chunked(lo, hi, count, body):
        size = (hi - lo) * PITCH // count

        def step(i, carry):
            body(pl.multiple_of(lo * PITCH + i * size, 16), size)
            return carry
        lax.fori_loop(0, count, step, 0)

    for h, tile in enumerate((top_ref, h0_ref, h1_ref, bottom_ref)):
        def main_rows(step, carry, h=h, tile=tile):
            for i, half in [(3 * step + u, half) for u in range(3) for half in range(2)]:
                p = pl.multiple_of((12 * h + i) * PITCH, PITCH)
                at = pl.multiple_of((12 * half + i) * COLS, COLS)
                value = jnp.concatenate(
                    [
                        left_ref[27 * h + 12 * half + i].astype(F32),
                        tile[pl.ds(at, COLS), :].astype(F32),
                        right_ref[27 * h + 12 * half + i].astype(F32),
                    ],
                    axis=0,
                )
                put_shifted(xs, p, slice(128 * half, 128 * half + 128), value)
            return carry
        lax.fori_loop(0, 4, main_rows, 0)

        def rest_rows(b, carry, h=h, tile=tile):
            packed = jnp.concatenate(
                [
                    left_ref[27 * h + 24 + b].astype(F32),
                    tile[pl.ds(pl.multiple_of(1536 + b * COLS, COLS), COLS), :].astype(F32),
                    right_ref[27 * h + 24 + b].astype(F32),
                ],
                axis=0,
            )
            for a in range(4):
                p = pl.multiple_of((12 * h + 3 * a + b) * PITCH, PITCH)
                value = jnp.where(lane < 32, pltpu.roll(packed, (128 - 32 * a) % 128, 1), 0.0)
                mk[pl.ds(p, PITCH), :] = jnp.broadcast_to(value[:, 25:26], (PITCH, 128))
                low = pltpu.roll(value, 1, 0)
                mid = pltpu.roll(value, 32, 1)
                high = pltpu.roll(pltpu.roll(value, PITCH - 1, 0), 64, 1)
                xq[pl.ds(p, PITCH), :] = (low + mid + high).astype(BF)
            return carry
        for b in range(3):
            rest_rows(b, 0)

    keep = [
        pltpu.make_async_copy(xs.at[1, core, :], xm_ref, sems.at[1]),
        pltpu.make_async_copy(xq.at[core, :], xr_ref, sems.at[2]),
    ]
    for copy in keep:
        copy.start()

    def start_sums(lo, hi):
        p, size = lo * PITCH, (hi - lo) * PITCH
        left = jnp.concatenate([xq[pl.ds(p + PITCH * (dy - 1), size), :] for dy in range(3)], axis=1)
        total = nt(left, jnp.concatenate([wr_ref[dy] for dy in range(3)], axis=1))
        for dy in range(3):
            at = p + PITCH * (dy - 1)
            for dx in range(3):
                total = total + nt(xs[dx, pl.ds(at, size), :], wm_ref[3 * dy + dx])
        pre[pl.ds(p, size), :] = total

    first_lane = [0, 128, 256, 384, 384]
    lanes_of = [(0, 128), (0, 128), (0, 96), (0, 64), (64, 96)]
    kept = []

    def activate(layer, lo, hi):
        block = slice(first_lane[layer], first_lane[layer] + 128)
        inside = (lane >= lanes_of[layer][0]) & (lane < lanes_of[layer][1])
        piece = min(layer, 3)
        lanes = slice(128 * piece, 128 * piece + 128)
        for p in range(lo * PITCH, hi * PITCH, PITCH):
            value = pre[pl.ds(p, PITCH), block]
            sig = 0.5 * jnp.tanh(0.5 * value) + 0.5
            live = mk[pl.ds(p, PITCH), :] > 0.0
            if layer >= 3:
                live = live & inside
            act = value * sig
            slope = jnp.where(live, sig + act * (1.0 - sig), 0.0)
            if layer >= 3:
                slope = jnp.where(inside, slope, value)
            pre[pl.ds(p, PITCH), block] = slope
            put_shifted(sh, p, lanes, jnp.where(live, act, 0.0))

    def add_sums(layer, lo, hi):
        p, size = lo * PITCH, (hi - lo) * PITCH
        piece = min(layer, 3)
        out0 = min(128 * (layer + 1), 384)
        lanes = slice(128 * piece, 128 * piece + 128)
        left = jnp.concatenate(
            [sh[dx, pl.ds(p + PITCH * (dy - 1), size), lanes] for dy in range(3) for dx in range(3)], axis=1
        )
        right = jnp.concatenate([w_ref[k, out0:512, lanes] for k in range(9)], axis=1)
        pre[pl.ds(p, size), out0:512] = pre[pl.ds(p, size), out0:512] + nt(left, right)

    def bounds(lo, hi, shift):
        return [(lo, 18 - shift), (18 - shift, 33 - shift), (33 - shift, hi)]

    sums_of = [[functools.partial(start_sums, *r) for r in bounds(1, WROWS - 1, 0)]]
    for layer in range(5):
        sums_of.append(
            [functools.partial(add_sums, layer, *r) for r in bounds(layer + 2, WROWS - layer - 2, layer + 1)]
        )
    sums_of[0][0]()
    for layer in range(5):
        acts = [functools.partial(activate, layer, *r) for r in bounds(layer + 1, WROWS - layer - 1, layer)]
        sums_of[layer][1]()
        if layer == 4:
            kept[3].wait()
        acts[0]()
        sums_of[layer][2]()
        acts[1]()
        sums_of[layer + 1][0]()
        acts[2]()
        piece = min(layer, 3)
        copy = pltpu.make_async_copy(
            sh.at[1, core, 128 * piece : 128 * piece + 128],
            a_ref.at[:, 128 * layer : 128 * layer + 128],
            sems.at[3 + layer],
        )
        copy.start()
        kept.append(copy)
    sums_of[5][1]()
    sums_of[5][2]()

    is_flow = (lane >= 96) & (lane < 98)
    column = lax.broadcasted_iota(jnp.int32, (PITCH, 128), 0)
    core_column = (column >= LEFT) & (column < LEFT + COLS)
    met_ref[...] = jnp.zeros((3, PITCH, 128), F32)
    kept[0].wait()
    kept[1].wait()
    kept[2].wait()
    kept[4].wait()

    def loss(p):
        flow = pre[pl.ds(p, PITCH), 384:512]
        rest = xq[pl.ds(p, PITCH), :].astype(F32)
        target = pltpu.roll(rest, 96 - 60, 1) + pltpu.roll(rest, 96 - 62, 1)
        diff = jnp.where(is_flow, flow - target, 0.0)
        square = diff * diff
        other = jnp.where(lane == 96, pltpu.roll(square, 127, 1), pltpu.roll(square, 1, 1))
        error = jnp.sqrt(square + other + 1.0)
        mask = jnp.broadcast_to(rest[:, 59:60], (PITCH, 128))
        put_shifted(sh, p, slice(384, 512), jnp.where(is_flow, mask * diff / error, 0.0))
        return flow, mask, error

    def loss_rim(p):
        loss(p)

    def loss_core(p):
        flow, mask, error = loss(p)
        r = lax.div(p, PITCH) - HALO
        turned = jnp.transpose(flow)
        for n in range(2):
            flow_ref[n, pl.ds(r, 1), :] = turned[96 + n : 97 + n, LEFT : LEFT + COLS]
        mask = jnp.where(core_column, mask, 0.0)
        met_ref[0] += mask * (error - 1.0)
        met_ref[1] += mask / (1.0 + jnp.exp(-4.0 * (error - 2.0)))
        met_ref[2] += mask

    rows(6, HALO, loss_rim)
    rows(HALO, HALO + ROWS, loss_core)
    rows(HALO + ROWS, WROWS - 6, loss_rim)

    def back(layer, lo, hi):
        p, size = lo * PITCH, (hi - lo) * PITCH
        piece = min(layer, 3)
        out0 = min(128 * (layer + 1), 384)
        left = jnp.concatenate(
            [sh[2 - dx, pl.ds(p - PITCH * (dy - 1), size), out0:512] for dy in range(3) for dx in range(3)], axis=1
        )
        right = jnp.concatenate([w_ref[k, out0:512, 128 * piece : 128 * piece + 128] for k in range(9)], axis=0)
        part[pl.ds(p, size), :] = nn(left, right)

    def slope(layer, lo, hi):
        block = slice(first_lane[layer], first_lane[layer] + 128)
        inside = (lane >= lanes_of[layer][0]) & (lane < lanes_of[layer][1])
        piece = min(layer, 3)
        lanes = slice(128 * piece, 128 * piece + 128)
        for p in range(lo * PITCH, hi * PITCH, PITCH):
            value = part[pl.ds(p, PITCH), :] * pre[pl.ds(p, PITCH), block]
            if layer >= 3:
                value = jnp.where(inside, value, sh[1, pl.ds(p, PITCH), lanes].astype(F32))
            put_shifted(sh, p, lanes, value)

    def back_bounds(layer):
        lo, hi = HALO - layer - 1, HALO + ROWS + layer + 1
        return [(lo, 16 + layer), (16 + layer, 26 + layer), (26 + layer, hi)]

    back(4, *back_bounds(4)[0])
    for layer in range(4, -1, -1):
        parts = back_bounds(layer)
        back(layer, *parts[1])
        slope(layer, *parts[0])
        back(layer, *parts[2])
        slope(layer, *parts[1])
        if layer > 0:
            back(layer - 1, *back_bounds(layer - 1)[0])
        slope(layer, *parts[2])
        if layer < 4:
            lanes = slice(128 * layer, 128 * layer + 128)
            copy = pltpu.make_async_copy(
                sh.at[:, pl.ds((HALO - 1) * PITCH, (ROWS + 2) * PITCH), lanes], g_ref.at[:, :, lanes], sems.at[8 + layer]
            )
            copy.start()
            keep.append(copy)

    for copy in keep:
        copy.wait()


def decode(*operands):
    size = ROWS * PITCH
    vm = pl.BlockSpec(memory_space=pltpu.VMEM)
    hbm = pl.BlockSpec(memory_space=pl.ANY)
    return pl.pallas_call(
        decode_kernel,
        out_shape=(
            jax.ShapeDtypeStruct((size, 640), BF),
            jax.ShapeDtypeStruct((3, (ROWS + 2) * PITCH, 512), BF),
            jax.ShapeDtypeStruct((size, 256), BF),
            jax.ShapeDtypeStruct((size, 128), BF),
            jax.ShapeDtypeStruct((2, ROWS, COLS), F32),
            jax.ShapeDtypeStruct((3, PITCH, 128), F32),
        ),
        in_specs=[vm] * 9,
        out_specs=(hbm, hbm, hbm, hbm, vm, vm),
        scratch_shapes=[
            pltpu.VMEM((3, NPX, 256), BF),
            pltpu.VMEM((NPX, 128), BF),
            pltpu.VMEM((3, NPX, 512), BF),
            pltpu.VMEM((NPX, 512), F32),
            pltpu.VMEM((NPX, 128), F32),
            pltpu.VMEM((NPX, 128), F32),
            pltpu.SemaphoreType.DMA((12,)),
        ],
        compiler_params=pltpu.CompilerParams(vmem_limit_bytes=VMEM_MB * 2**20),
        name="decode",
    )(*operands)


def arrange_kernel(c1, c2, c3, c4, c5, c6, wide_ref, rest_ref, bias_ref, wm_ref, w_ref, wr_ref):
    for rows in (slice(352, 384), slice(480, 512)):
        wm_ref[:, rows, :] = jnp.zeros((9, 32, 256), BF)
        w_ref[:, rows, :] = jnp.zeros((9, 32, 512), BF)
    wr_ref[:, 352:384, :] = jnp.zeros((3, 32, 128), BF)
    wr_ref[:, 480:512, :] = jnp.zeros((3, 32, 128), BF)
    lane = lax.broadcasted_iota(jnp.int32, (512, 128), 1)
    bias = bias_ref[...]
    high = bias.astype(BF).astype(F32)
    bias = jnp.where(lane == 57, high, jnp.where(lane == 58, bias - high, 0.0))

    for n, ref in enumerate((c1, c2, c3, c4, c5, c6)):
        outs, depth = OUTS[n], DEPTH[n]
        rows = slice(ROW0[n], ROW0[n] + outs)
        wide = wide_ref[729 - depth :, :]
        rest = rest_ref[729 - depth :, :]
        dims = (((0,), (0,)), ((), ())) if n < 2 else (((1,), (0,)), ((), ()))
        for dy in range(3):
            total = bias[rows] if dy == 1 else jnp.zeros((outs, 128), F32)
            for dx in range(3):
                weight = ref[3 * dy + dx]
                value = lax.dot_general(weight, wide, dims, preferred_element_type=F32).astype(BF)
                wm_ref[3 * dy + dx, rows, :] = value[:, 0:256]
                w_ref[3 * dy + dx, rows, :] = value[:, 256:768]
                part = lax.dot_general(weight, rest, dims, preferred_element_type=F32)
                total = total + (pltpu.roll(part, 32 * dx, 1) if dx else part)
            wr_ref[dy, rows, :] = total.astype(BF)


def arrange(convs, biases):
    vm = pl.BlockSpec(memory_space=pltpu.VMEM)
    bias = jnp.concatenate(
        [biases[0], biases[1], biases[2], jnp.zeros((32,), F32), biases[3], biases[4], biases[5], jnp.zeros((30,), F32)]
    ).reshape(512, 1)
    turned = [jnp.transpose(convs[0], (0, 2, 1)), jnp.transpose(convs[1], (0, 2, 1))]
    return pl.pallas_call(
        arrange_kernel,
        out_shape=(
            jax.ShapeDtypeStruct((9, 512, 256), BF),
            jax.ShapeDtypeStruct((9, 512, 512), BF),
            jax.ShapeDtypeStruct((3, 512, 128), BF),
        ),
        in_specs=[vm] * 9,
        out_specs=(vm, vm, vm),
        compiler_params=pltpu.CompilerParams(vmem_limit_bytes=40 * 2**20),
        cost_estimate=pl.CostEstimate(flops=4 * 10**9, bytes_accessed=16 * 10**6, transcendentals=0),
        name="arrange",
    )(*turned, *convs[2:], jnp.asarray(WIDE, BF), jnp.asarray(REST, BF), bias)

TILE_ROWS = 2048
TOTAL_ROWS = 9 * TILE_ROWS
HALF_ROWS = TOTAL_ROWS // 2


def tn(a, b):
    return lax.dot_general(a, b, (((0,), (0,)), ((), ())), preferred_element_type=F32)


def wgrad_kernel(core_ref, g_hbm, xm_ref, xr_ref, a_ref, qp_ref, own_ref, sent_ref, g_ref, xp, o_ref, loads, stores):
    for d in range(3):
        pltpu.make_async_copy(g_hbm.at[d], g_ref.at[d], loads.at[d]).start()
    column = lax.broadcasted_iota(jnp.int32, (PITCH, 128), 0)
    core = (column >= LEFT) & (column < LEFT + COLS)
    core = jnp.concatenate([core] * 4, axis=0)
    size = 4 * PITCH

    def gather(i, carry):
        at = pl.ds(pl.multiple_of(i * size, size), size)
        left = jnp.concatenate([xm_ref[at, :], xr_ref[at, :], a_ref[at, 0:128]], axis=1)
        parts = [
            nn(a_ref[at, 128:640], qp_ref[512:1024, 0:256]),
            nn(a_ref[at, 0:256], qp_ref[384:640, 256:384]),
            nn(left, qp_ref[0:512, 384:768]),
        ]
        value = jnp.concatenate(parts, axis=1)
        for t in range(6):
            lanes = slice(128 * t, 128 * t + 128)
            xp[at, lanes] = jnp.where(core, value[:, lanes], 0.0).astype(BF)
        return carry
    lax.fori_loop(0, ROWS // 4, gather, 0)
    for d in range(3):
        pltpu.make_async_copy(g_hbm.at[d], g_ref.at[d], loads.at[d]).wait()

    part_rows = TILE_ROWS // 2

    def store(n, act):
        half, place = divmod(n, 9)
        for target, mine in ((own_ref, True), (sent_ref, False)):
            @pl.when((core_ref[0] == half) == mine)
            def _():
                act(
                    pltpu.make_async_copy(
                        o_ref.at[pl.ds(part_rows * n, part_rows), :],
                        target.at[pl.ds(part_rows * place, part_rows), :],
                        stores.at[n],
                    )
                )

    for k in range(9):
        dy, dx = divmod(k, 3)
        at = pl.ds(PITCH * (2 - dy), ROWS * PITCH)
        base = TILE_ROWS * k
        low = tn(g_ref[2 - dx, at, 0:256], xp[:, 256:768]).astype(BF)
        for t in range(3):
            o_ref[base + 128 * t : base + 128 * t + 128, :] = low[0:128, 128 * t + 128 : 128 * t + 256]
        for t in range(4):
            o_ref[base + 384 + 128 * t : base + 512 + 128 * t, :] = low[128:256, 128 * t : 128 * t + 128]
        low = tn(g_ref[2 - dx, at, 256:512], xp[...]).astype(BF)
        for t in range(5):
            o_ref[base + 896 + 96 * t : base + 992 + 96 * t, :] = low[0:96, 128 * t + 128 : 128 * t + 256]
        for t in range(6):
            o_ref[base + 1376 + 112 * t : base + 1488 + 112 * t, :] = low[128:240, 128 * t : 128 * t + 128]
        store(2 * k, lambda copy: copy.start())
        store(2 * k + 1, lambda copy: copy.start())
    for n in range(18):
        store(n, lambda copy: copy.wait())


def wgrad(core, g, xm, xr, a, qp):
    vm = pl.BlockSpec(memory_space=pltpu.VMEM)
    hbm = pl.BlockSpec(memory_space=pl.ANY)
    return pl.pallas_call(
        wgrad_kernel,
        out_shape=(jax.ShapeDtypeStruct((HALF_ROWS, 128), BF),) * 2,
        in_specs=[pl.BlockSpec(memory_space=pltpu.SMEM), hbm] + [vm] * 4,
        out_specs=(hbm, hbm),
        scratch_shapes=[
            pltpu.VMEM((3, (ROWS + 2) * PITCH, 512), BF),
            pltpu.VMEM((ROWS * PITCH, 768), BF),
            pltpu.VMEM((TOTAL_ROWS, 128), BF),
            pltpu.SemaphoreType.DMA((3,)),
            pltpu.SemaphoreType.DMA((18,)),
        ],
        compiler_params=pltpu.CompilerParams(vmem_limit_bytes=VMEM_MB * 2**20),
        name="wgrad",
    )(core, g, xm, xr, a, qp)

NOTE = 16


def half_sum_kernel(own_ref, got_ref, note_ref, got_note_ref, o_ref):
    count, height = o_ref.shape[0], o_ref.shape[1] - NOTE
    notes = jnp.concatenate([note_ref[0:8].astype(F32), got_note_ref[0:8].astype(F32)], axis=0).astype(BF)
    for b in range(count):
        rows = slice(height * b, height * (b + 1))
        o_ref[b, 0:height] = (own_ref[rows, :].astype(F32) + got_ref[rows, :].astype(F32)).astype(BF)
        o_ref[b, height:] = notes


def half_sum(own, got, note, got_note, count):
    height = HALF_ROWS // count
    steps = 4
    block = HALF_ROWS // steps
    return pl.pallas_call(
        half_sum_kernel,
        grid=(steps,),
        in_specs=[
            pl.BlockSpec((block, 128), lambda i: (i, 0)),
            pl.BlockSpec((block, 128), lambda i: (i, 0)),
            pl.BlockSpec((NOTE, 128), lambda i: (0, 0)),
            pl.BlockSpec((NOTE, 128), lambda i: (0, 0)),
        ],
        out_specs=pl.BlockSpec((count // steps, height + NOTE, 128), lambda i: (i, 0, 0)),
        out_shape=jax.ShapeDtypeStruct((count, height + NOTE, 128), BF),
        name="half_sum",
    )(own, got, note, got_note)


def spread_kernel(parts_ref, o_ref, note_ref):
    count, height = o_ref.shape[0], o_ref.shape[1]

    def add(b, carry):
        total, notes = carry
        return total + parts_ref[b, 0:height].astype(F32), notes + parts_ref[b, height:].astype(F32)
    zero = (jnp.zeros((height, 128), F32), jnp.zeros((NOTE, 128), F32))
    total, notes = lax.fori_loop(0, count, add, zero)
    note_ref[...] = notes
    total = total.astype(BF)

    def put(b, carry):
        o_ref[b] = total
        return carry
    lax.fori_loop(0, count, put, 0)


def spread_total(parts):
    count, height, _ = parts.shape
    vm = pl.BlockSpec(memory_space=pltpu.VMEM)
    return pl.pallas_call(
        spread_kernel,
        out_shape=(
            jax.ShapeDtypeStruct((count, height - NOTE, 128), BF),
            jax.ShapeDtypeStruct((NOTE, 128), F32),
        ),
        in_specs=[vm],
        out_specs=(vm, vm),
        compiler_params=pltpu.CompilerParams(vmem_limit_bytes=32 * 2**20),
        name="spread_total",
    )(parts)


def unpack_kernel(
    core_ref, mine_ref, other_ref, o1, o2, o3, o4, o5, o6, b1, b2, b3, b4, b5, b6, all_ref, sems
):
    k = pl.program_id(0)

    @pl.when(k == 0)
    def _():
        core = core_ref[0]
        copies = [
            pltpu.make_async_copy(
                source, all_ref.at[pl.ds(pl.multiple_of(at * HALF_ROWS, HALF_ROWS), HALF_ROWS), :], sems.at[n]
            )
            for n, (source, at) in enumerate(((mine_ref, core), (other_ref, 1 - core)))
        ]
        for copy in copies:
            copy.start()
        for copy in copies:
            copy.wait()
    first = pl.multiple_of(k * TILE_ROWS, TILE_ROWS)

    def tiles(base, height, count):
        return jnp.concatenate(
            [all_ref[pl.ds(first + base + height * t, height), :].astype(F32) for t in range(count)], axis=1
        )
    o1[0] = jnp.transpose(tiles(0, 128, 3))[64 : 64 + 281]
    o2[0] = jnp.transpose(tiles(384, 128, 4))[64 : 64 + 409]
    o3[0] = tiles(896, 96, 5)[:, 64 : 64 + 537]
    last = tiles(1376, 112, 6)
    o4[0] = last[0:64, 96:729]
    o5[0] = last[64:96, 32:729]
    o6[0] = last[96:98, 0:729]

    @pl.when(k == 4)
    def _():
        biases = [tiles(256, 128, 1), tiles(768, 128, 1), tiles(1280, 96, 1), last[:, 640:768]]
        biases = [jnp.transpose(value)[89:90] for value in biases]
        b1[...] = biases[0]
        b2[...] = biases[1]
        b3[...] = biases[2]
        b4[...] = biases[3][:, 0:64]
        b5[...] = biases[3][:, 64:96]
        b6[...] = biases[3][:, 96:98]


def unpack(core, mine, other):
    shapes = ((281, 128), (409, 128), (96, 537), (64, 633), (32, 697), (2, 729))
    hbm = pl.BlockSpec(memory_space=pl.ANY)
    results = pl.pallas_call(
        unpack_kernel,
        grid_spec=pltpu.PrefetchScalarGridSpec(
            num_scalar_prefetch=1,
            grid=(9,),
            in_specs=[hbm, hbm],
            out_specs=tuple(pl.BlockSpec((1,) + s, lambda k, core: (k, 0, 0)) for s in shapes)
            + tuple(pl.BlockSpec((1, outs), lambda k, core: (0, 0)) for outs in OUTS),
            scratch_shapes=[pltpu.VMEM((TOTAL_ROWS, 128), BF), pltpu.SemaphoreType.DMA((2,))],
        ),
        out_shape=tuple(jax.ShapeDtypeStruct((9,) + s, F32) for s in shapes)
        + tuple(jax.ShapeDtypeStruct((1, outs), F32) for outs in OUTS),
        compiler_params=pltpu.CompilerParams(vmem_limit_bytes=32 * 2**20),
        name="unpack",
    )(core, mine, other)
    grads = list(results[:6])
    grads[0] = jnp.transpose(grads[0], (0, 2, 1))
    grads[1] = jnp.transpose(grads[1], (0, 2, 1))
    return grads, [bias.reshape(-1) for bias in results[6:]]


SWAP = [(0, 1), (1, 0)]
CHIPS = ("chan", "xy")


def chip_parts(own, sent, scalars):
    high = lax.reduce_precision(scalars, 8, 7)
    middle = lax.reduce_precision(scalars - high, 8, 7)
    low = scalars - high - middle
    note = jnp.stack([high, middle, low]).astype(BF)
    note = jnp.pad(note, ((0, NOTE - 3), (0, 128 - scalars.shape[0])))
    got_note = lax.ppermute(note, "core", SWAP)
    got = lax.ppermute(sent, "core", SWAP)
    return half_sum(own, got, note, got_note, lax.axis_size(CHIPS))

SLOT = 64
WIN = 80
PAY = 12 * COLS + 16 * WIN
HALF = 27 * COLS


def slanted(x, shift):
    shift = shift % 128
    if shift % 8:
        x = pltpu.roll(x, shift % 8, 1)
    return pltpu.roll(x, shift - shift % 8, 1, stride=1, stride_axis=0)


def two_rows(lane, parts):
    swap = [pltpu.roll(part, 64, 1) for part in parts]
    first = [jnp.where(lane < 64, parts[2 * h], swap[2 * h + 1]) for h in range(2)]
    second = [jnp.where(lane < 64, swap[2 * h], parts[2 * h + 1]) for h in range(2)]
    return jnp.concatenate(first, axis=1), jnp.concatenate(second, axis=1)


def diagonal(size, back):
    i = lax.broadcasted_iota(jnp.int32, (size, size), 0)
    j = lax.broadcasted_iota(jnp.int32, (size, size), 1)
    return jnp.where(i + j == size - 1 if back else i == j, 1.0, 0.0).astype(BF)


def pack_first_kernel(f1_ref, o_hbm, o_ref, sem):
    back = diagonal(256, True)

    def first(step, carry):
        for i in (3 * step, 3 * step + 1, 3 * step + 2):
            both = jnp.concatenate([f1_ref[i], f1_ref[i + 12]], axis=0)
            value = nt(back, both).astype(BF)
            for z in range(4):
                o_ref[z, pl.ds(pl.multiple_of(i * COLS, COLS), COLS), :] = value[192 - COLS * z : 256 - COLS * z]
        return carry
    lax.fori_loop(0, 4, first, 0)
    copy = pltpu.make_async_copy(o_ref, o_hbm.at[:, pl.ds(0, 12 * COLS), :], sem)
    copy.start()
    copy.wait()


def pack_first(f1):
    return pl.pallas_call(
        pack_first_kernel,
        out_shape=jax.ShapeDtypeStruct((4, PAY, 128), BF),
        in_specs=[pl.BlockSpec(memory_space=pltpu.VMEM)],
        out_specs=pl.BlockSpec(memory_space=pl.ANY),
        scratch_shapes=[pltpu.VMEM((4, 12 * COLS, 128), BF), pltpu.SemaphoreType.DMA],
        compiler_params=pltpu.CompilerParams(vmem_limit_bytes=32 * 2**20),
        name="pack_first",
    )(f1)


def pack_warped_kernel(f2_ref, above_ref, below_ref, first_hbm, o_hbm, o_ref, band, turn, sem):
    eye = diagonal(256, False)
    last = lax.broadcasted_iota(jnp.int32, (SLOT, 256), 1) == 255
    channel = lax.broadcasted_iota(jnp.int32, (SLOT, 256), 0) < CH // 4
    band[0:MD] = above_ref[...]
    band[MD : MD + ROWS] = f2_ref[...]
    band[MD + ROWS :] = below_ref[...]
    turn[...] = jnp.zeros(turn.shape, F32)

    def warped(t):
        upper = band[t].astype(F32)
        lower = band[t + 1].astype(F32)
        u = upper[49:50]
        v = upper[50:51]

        def across(x):
            return (1.0 - u) * x + u * jnp.where(last, 0.0, pltpu.roll(x, 255, 1))
        value = (1.0 - v) * across(upper) + v * across(lower)
        return jnp.where(channel, value, 0.0).astype(BF)

    def second(step, carry):
        for u in range(4):
            i = 4 * step + u
            both = jnp.concatenate([warped(i), warped(i + 16)], axis=0)
            turn[u, 8:264, :] = nt(eye, both)
            for z in range(4):
                start = pl.multiple_of(i * WIN, 16)
                o_ref[z, pl.ds(start, WIN), :] = turn[u, COLS * z + 4 : COLS * z + 4 + WIN, :].astype(BF)
        return carry
    lax.fori_loop(0, 4, second, 0)
    copy = pltpu.make_async_copy(o_ref, o_hbm.at[:, pl.ds(12 * COLS, 16 * WIN), :], sem)
    copy.start()
    copy.wait()


def pack_warped(f2, above, below, packed):
    vm = pl.BlockSpec(memory_space=pltpu.VMEM)
    hbm = pl.BlockSpec(memory_space=pl.ANY)
    return pl.pallas_call(
        pack_warped_kernel,
        out_shape=jax.ShapeDtypeStruct((4, PAY, 128), BF),
        in_specs=[vm, vm, vm, hbm],
        out_specs=hbm,
        input_output_aliases={3: 0},
        scratch_shapes=[
            pltpu.VMEM((4, 16 * WIN, 128), BF),
            pltpu.VMEM((33, SLOT, 256), BF),
            pltpu.VMEM((4, 288, 128), F32),
            pltpu.SemaphoreType.DMA,
        ],
        compiler_params=pltpu.CompilerParams(vmem_limit_bytes=32 * 2**20),
        name="pack_warped",
    )(f2, above, below, packed)


def flip_matrix():
    total = lax.broadcasted_iota(jnp.int32, (COLS, COLS), 0) + lax.broadcasted_iota(jnp.int32, (COLS, COLS), 1)
    return jnp.where(total == COLS - 1, 1.0, 0.0).astype(BF)


def read_features(rx_ref, lane, first_rows, warped_rows):
    def first(step, carry):
        for i in (3 * step, 3 * step + 1, 3 * step + 2):
            at = pl.ds(pl.multiple_of(i * COLS, COLS), COLS)
            one, two = two_rows(lane[:COLS], [rx_ref[q, at, :].astype(F32) for q in range(4)])
            first_rows(i, one.astype(BF))
            first_rows(i + 12, two.astype(BF))
        return carry
    lax.fori_loop(0, 4, first, 0)

    def second(step, carry):
        for i in (4 * step, 4 * step + 1, 4 * step + 2, 4 * step + 3):
            at = pl.ds(pl.multiple_of(12 * COLS + i * WIN, 16), WIN)
            one, two = two_rows(lane[:WIN], [rx_ref[q, at, :].astype(F32) for q in range(4)])
            warped_rows(i, one.astype(BF))
            warped_rows(i + 16, two.astype(BF))
        return carry
    lax.fori_loop(0, 4, second, 0)


def flip_four():
    i = lax.broadcasted_iota(jnp.int32, (4 * COLS, 4 * COLS), 0)
    j = lax.broadcasted_iota(jnp.int32, (4 * COLS, 4 * COLS), 1)
    here = ((i & (COLS - 1)) + (j & (COLS - 1)) == COLS - 1) & ((i & -COLS) == (j & -COLS))
    return jnp.where(here, 1.0, 0.0).astype(BF)


def cost_kernel(rx_ref, ex_ref, h0_ref, h1_ref, fs, ws, ms, vs, rs):
    lane = lax.broadcasted_iota(jnp.int32, (128, 128), 1)

    def put_first(i, value):
        fs[i] = value

    def put_warped(i, value):
        ws[i, 0:WIN] = value
    read_features(rx_ref, lane, put_first, put_warped)
    lane = lane[:COLS]
    flip = flip_four()

    for half, out in ((0, h0_ref), (1, h1_ref)):
        def group(g, carry, half=half, out=out):
            i = 12 * half + 4 * g
            ms[...] = nt(fs[pl.ds(i, 4)].reshape(4 * COLS, 256), ws[pl.ds(i, 12)].reshape(12 * 128, 256))
            for r in range(4):
                rows = slice(COLS * r, COLS * r + COLS)

                def band(dy, t, here, value, r=r, rows=rows):
                    block = slanted(ms[rows, 128 * (r + dy) : 128 * (r + dy) + 128], t - 63)
                    return jnp.where(here, block * (1.0 / CH**0.5), value)
                for h in range(2):
                    value = fs[i + r, :, 128 * h : 128 * h + 128].astype(F32)
                    for s in range(2):
                        at = 64 * s + 47
                        value = band(2 * h + s, at + 8, (lane >= at + 8) & (lane < at + 17), value)
                        value = band(4 + 2 * h + s, at, (lane >= at + 2) & (lane < at + 8), value)
                    vs[rows, 128 * h : 128 * h + 128] = value.astype(BF)
                value = jnp.zeros((COLS, 128), F32)
                for a in range(4):
                    here = (lane == 2 * a) | (lane == 2 * a + 1) | (lane == 2 * a + 8)
                    value = band(4 + a, 2 * a, here, value)
                vs[rows, 256:384] = band(8, 16, (lane >= 16) & (lane < 25), value).astype(BF)
            turned = nn(flip, vs[...])
            for h in range(2):
                at = pl.multiple_of(768 * h + 4 * g * COLS, 4 * COLS)
                out[pl.ds(at, 4 * COLS), :] = turned[:, 128 * h : 128 * h + 128].astype(BF)
            rs[pl.ds(i, 4)] = turned[:, 256:384].reshape(4, COLS, 128) + ex_ref[pl.ds(i, 4)].astype(F32)
            return carry
        lax.fori_loop(0, 3, group, 0)
    for half, out in ((0, h0_ref), (1, h1_ref)):
        for b in range(3):
            total = rs[12 * half + b]
            for a in range(1, 4):
                total = total + pltpu.roll(rs[12 * half + 3 * a + b], 32 * a, 1)
            out[1536 + COLS * b : 1536 + COLS * b + COLS, :] = total.astype(BF)


def cost_volume(rx, extra):
    vm = pl.BlockSpec(memory_space=pltpu.VMEM)
    return pl.pallas_call(
        cost_kernel,
        out_shape=(jax.ShapeDtypeStruct((HALF, 128), BF),) * 2,
        in_specs=[vm] * 2,
        out_specs=(vm, vm),
        scratch_shapes=[
            pltpu.VMEM((ROWS, COLS, 256), BF),
            pltpu.VMEM((ROWS + 8, 128, 256), BF),
            pltpu.VMEM((4 * COLS, 12 * 128), F32),
            pltpu.VMEM((4 * COLS, 384), BF),
            pltpu.VMEM((ROWS, COLS, 128), F32),
        ],
        compiler_params=pltpu.CompilerParams(vmem_limit_bytes=32 * 2**20),
        name="cost_volume",
    )(rx, extra)


def cost_back_kernel(
    place_ref, rx_ref, sh_hbm, w_hbm, wr_ref, o0, o1, o2, o3, plane_ref,
    o_ref, dr_ref, dm_ref, part, fs, ws, bs, gs, gw, sh, w_ref, sems
):
    loads = [pltpu.make_async_copy(sh_hbm, sh, sems.at[0]), pltpu.make_async_copy(w_hbm, w_ref, sems.at[1])]
    for load in loads:
        load.start()
    lane = lax.broadcasted_iota(jnp.int32, (128, 128), 1)
    zero = jnp.zeros((8, COLS, 256), BF)
    fs[0:8] = zero
    fs[32:40] = zero
    flip = flip_matrix()

    def put_first(i, value):
        fs[i + 8] = nn(flip, value).astype(BF)

    def put_warped(i, value):
        ws[i, 0:WIN] = value
        ws[i, WIN:] = jnp.zeros((128 - WIN, 256), BF)
    read_features(rx_ref, lane, put_first, put_warped)

    for load in loads:
        load.wait()

    def back_rest(i, carry):
        p = pl.multiple_of(i * 8 * PITCH, 8 * PITCH)
        total = None
        for dy in range(3):
            term = nn(sh[1, pl.ds(p + PITCH * (2 - dy), 8 * PITCH), :], wr_ref[dy])
            total = term if total is None else total + term
        part[...] = total
        for r in range(8):
            value = part[PITCH * r : PITCH * (r + 1), :]
            value = (
                pltpu.roll(value, PITCH - 1, 0)
                + pltpu.roll(value, 96, 1)
                + pltpu.roll(pltpu.roll(value, 1, 0), 64, 1)
            )
            dr_ref[pl.ds(pl.multiple_of(p + PITCH * r, PITCH), PITCH), :] = value
            turned = jnp.transpose(value)
            for n in range(4):
                plane_ref[n, pl.ds(8 * i + r, 1), :] = turned[9 + 2 * n : 10 + 2 * n, LEFT : LEFT + COLS]
        return carry
    lax.fori_loop(0, ROWS // 8, back_rest, 0)

    def back_main(i, carry):
        p = pl.multiple_of(i * 8 * PITCH, 8 * PITCH)
        total = None
        for dy in range(3):
            at = p + PITCH * (2 - dy)
            for dx in range(3):
                term = nn(sh[2 - dx, pl.ds(at, 8 * PITCH), :], w_ref[3 * dy + dx])
                total = term if total is None else total + term
        dm_ref[pl.ds(p, 8 * PITCH), :] = total.astype(BF)
        return carry
    lax.fori_loop(0, ROWS // 8, back_main, 0)

    def clear(i, carry):
        bs[i] = jnp.zeros((15, COLS, 128), BF)
        bs[i + 32] = jnp.zeros((15, COLS, 128), BF)
        return carry
    lax.fori_loop(0, 8, clear, 0)
    lane = lane[:COLS]
    ahead = lane - lax.broadcasted_iota(jnp.int32, (COLS, 128), 0)

    def row(i):
        at = pl.ds(pl.multiple_of(i * PITCH + LEFT, 16), COLS)
        halves = [pltpu.roll(dm_ref[at, 128 * h : 128 * h + 128].astype(F32), 1, 1) for h in range(2)]
        rest = dr_ref[at, :].astype(BF).astype(F32)

        def band(source, t, first, last, far=None):
            shift = (-t) % 128
            extra = shift % 8
            block = pltpu.roll(source, shift - extra, 1, stride=1, stride_axis=0)
            offset = (ahead + extra) & 127
            here = (offset >= first) & (offset <= last)
            if far is not None:
                here = here | (offset == far)
            block = jnp.where(here, block, 0.0)
            return pltpu.roll(block, extra, 1) if extra else block
        bs[i + 8, 0:3] = jnp.zeros((3, COLS, 128), BF)
        bs[i + 8, 12:15] = jnp.zeros((3, COLS, 128), BF)
        for dy in range(4):
            bs[i + 8, dy + 3] = band(halves[dy // 2], 64 * (dy % 2) + 56, 0, 8).astype(BF)
        for a in range(4):
            value = band(halves[a // 2], 64 * (a % 2) + 48, 2, 7) + band(rest, 2 * a, 0, 1, 8)
            bs[i + 8, a + 7] = value.astype(BF)
        bs[i + 8, 11] = band(rest, 16, 0, 8).astype(BF)
    def three_rows(step, carry):
        for u in range(3):
            row(3 * step + u)
        return carry
    lax.fori_loop(0, ROWS // 3, three_rows, 0)

    def to_first(g, carry):
        i = 4 * g
        left = jnp.concatenate(
            [jnp.concatenate([bs[i + 8 + r, t - r + 3] for t in range(12)], axis=1) for r in range(4)], axis=0
        )
        total = nn(left, ws[pl.ds(i, 12)].reshape(12 * 128, 256)) * (1.0 / CH**0.5)
        for r in range(4):
            at = pl.ds(pl.multiple_of((i + r) * PITCH + LEFT, 16), COLS)
            gs[i + r] = total[COLS * r : COLS * r + COLS] + dm_ref[at, :].astype(F32)
        return carry
    lax.fori_loop(0, ROWS // 4, to_first, 0)

    def to_warped(g, carry):
        t = 4 * g
        left = jnp.concatenate(
            [jnp.concatenate([bs[t + m, 11 - m + n] for n in range(4)], axis=1) for m in range(12)], axis=0
        )
        right = fs[pl.ds(t, 12)].reshape(12 * COLS, 256)
        total = lax.dot_general(left, right, (((0,), (0,)), ((), ())), preferred_element_type=F32)
        gw[pl.ds(t, 4)] = (total * (1.0 / CH**0.5)).reshape(4, 128, 256)
        return carry
    lax.fori_loop(0, 8, to_warped, 0)

    def put(start, size, one, two):
        for z in range(4):
            h, odd = divmod(z, 2)
            a = one[:, 128 * h : 128 * h + 128]
            b = two[:, 128 * h : 128 * h + 128]
            if odd:
                a = pltpu.roll(a, 64, 1)
            else:
                b = pltpu.roll(b, 64, 1)
            low = lax.broadcasted_iota(jnp.int32, (size, 128), 1) < 64
            o_ref[(z - place_ref[0]) & 3, pl.ds(start, size), :] = jnp.where(low, a, b).astype(BF)

    def send_first(step, carry):
        for i in (3 * step, 3 * step + 1, 3 * step + 2):
            put(pl.multiple_of(i * COLS, COLS), COLS, gs[i], gs[i + 12])
        return carry
    lax.fori_loop(0, 4, send_first, 0)

    def send_warped(step, carry):
        for i in (4 * step, 4 * step + 1, 4 * step + 2, 4 * step + 3):
            put(pl.multiple_of(12 * COLS + i * WIN, 16), WIN, gw[i, 0:WIN], gw[i + 16, 0:WIN])
        return carry
    lax.fori_loop(0, 4, send_warped, 0)
    copies = [pltpu.make_async_copy(o_ref.at[s], out, sems.at[s]) for s, out in enumerate((o0, o1, o2, o3))]
    for copy in copies:
        copy.start()
    for copy in copies:
        copy.wait()


def cost_back(place, rx, slopes, weight, weight_rest):
    vm = pl.BlockSpec(memory_space=pltpu.VMEM)
    hbm = pl.BlockSpec(memory_space=pl.ANY)
    size = ROWS * PITCH
    return pl.pallas_call(
        cost_back_kernel,
        out_shape=(jax.ShapeDtypeStruct((PAY, 128), BF),) * 4 + (jax.ShapeDtypeStruct((4, ROWS, COLS), F32),),
        in_specs=[pl.BlockSpec(memory_space=pltpu.SMEM), vm, hbm, hbm, vm],
        out_specs=(hbm,) * 4 + (vm,),
        scratch_shapes=[
            pltpu.VMEM((4, PAY, 128), BF),
            pltpu.VMEM((size, 128), F32),
            pltpu.VMEM((size, 256), BF),
            pltpu.VMEM((8 * PITCH, 128), F32),
            pltpu.VMEM((ROWS + 16, COLS, 256), BF),
            pltpu.VMEM((ROWS + 8, 128, 256), BF),
            pltpu.VMEM((ROWS + 16, 15, COLS, 128), BF),
            pltpu.VMEM((ROWS, COLS, 256), F32),
            pltpu.VMEM((ROWS + 8, 128, 256), F32),
            pltpu.VMEM((3, (ROWS + 2) * PITCH, 512), BF),
            pltpu.VMEM((9, 512, 256), BF),
            pltpu.SemaphoreType.DMA((4,)),
        ],
        compiler_params=pltpu.CompilerParams(vmem_limit_bytes=VMEM_MB * 2**20),
        name="cost_back",
    )(place, rx, slopes, weight, weight_rest)


def turn_kernel(place_ref, r0, r1, r2, r3, g1_ref, gw_ref, up_ref, down_ref, turn, both):
    eye = jnp.where(
        lax.broadcasted_iota(jnp.int32, (128, 128), 0) == lax.broadcasted_iota(jnp.int32, (128, 128), 1), 1.0, 0.0
    ).astype(BF)
    sources = [
        (ref, pl.multiple_of(((place_ref[0] - s) & 3) * COLS, COLS)) for s, ref in enumerate((r0, r1, r2, r3))
    ]

    def first(i, carry):
        at = pl.ds(pl.multiple_of(i * COLS, COLS), COLS)
        for ref, column in sources:
            both[pl.ds(column, COLS), :] = ref[at, :]
        value = nt(eye, both[...])
        g1_ref[i] = value[0:SLOT]
        g1_ref[i + 12] = value[SLOT:]
        return carry
    lax.fori_loop(0, 12, first, 0)

    def second(i, carry):
        at = pl.ds(pl.multiple_of(12 * COLS + i * WIN, 16), WIN)
        turn[...] = jnp.zeros(turn.shape, F32)
        for ref, column in sources:
            rows = pl.ds(pl.multiple_of(column + 8, 8), WIN)
            turn[rows, :] = turn[rows, :] + ref[at, :].astype(F32)
        value = jnp.transpose(turn[12:268, :])
        gw_ref[i] = value[0:SLOT]
        gw_ref[i + 16] = value[SLOT:]
        return carry
    lax.fori_loop(0, 16, second, 0)
    up_ref[...] = gw_ref[0:4].astype(BF)
    down_ref[...] = gw_ref[27:32].astype(BF)


def turn(place, parts):
    vm = pl.BlockSpec(memory_space=pltpu.VMEM)
    return pl.pallas_call(
        turn_kernel,
        out_shape=(
            jax.ShapeDtypeStruct((ROWS, SLOT, 256), F32),
            jax.ShapeDtypeStruct((ROWS + 8, SLOT, 256), F32),
            jax.ShapeDtypeStruct((4, SLOT, 256), BF),
            jax.ShapeDtypeStruct((5, SLOT, 256), BF),
        ),
        in_specs=[pl.BlockSpec(memory_space=pltpu.SMEM)] + [vm] * 4,
        out_specs=(vm,) * 4,
        scratch_shapes=[pltpu.VMEM((288, 128), F32), pltpu.VMEM((256, 128), BF)],
        compiler_params=pltpu.CompilerParams(vmem_limit_bytes=32 * 2**20),
        name="turn",
    )(place, *parts)


def warp_back_kernel(gw_ref, from_above, from_below, f2_ref, above_ref, below_ref, g2_ref, gf_ref, full, band):
    first = lax.broadcasted_iota(jnp.int32, (SLOT, 256), 1) == 0
    last = lax.broadcasted_iota(jnp.int32, (SLOT, 256), 1) == 255
    channel = lax.broadcasted_iota(jnp.int32, (SLOT, 256), 0) < CH // 4
    band[0] = above_ref[3]
    band[1 : ROWS + 1] = f2_ref[...]
    band[ROWS + 1] = below_ref[0]
    full[...] = gw_ref[3:28]
    full[0:5] = full[0:5] + from_above[...].astype(F32)
    full[21:25] = full[21:25] + from_below[...].astype(F32)

    def spread(u, x):
        part = u * x
        return (x - part) + jnp.where(first, 0.0, pltpu.roll(part, 1, 1))

    def row(r, carry):
        upper = band[r + 1].astype(F32)
        lower = band[r + 2].astype(F32)
        before = band[r].astype(F32)
        u, v = upper[49:50], upper[50:51]
        grad = full[r + 1]
        g2_ref[r] = spread(u, (1.0 - v) * grad) + spread(before[49:50], before[50:51] * full[r])
        upper_next = jnp.where(last, 0.0, pltpu.roll(upper, 255, 1))
        lower_next = jnp.where(last, 0.0, pltpu.roll(lower, 255, 1))
        to_u = (1.0 - v) * (upper_next - upper) + v * (lower_next - lower)
        to_v = ((1.0 - u) * lower + u * lower_next) - ((1.0 - u) * upper + u * upper_next)
        along = jnp.sum(jnp.where(channel, grad * to_u, 0.0), axis=0, keepdims=True)
        down = jnp.sum(jnp.where(channel, grad * to_v, 0.0), axis=0, keepdims=True)
        gf_ref[r] = jnp.concatenate([along, down, jnp.zeros((6, 256), F32)], axis=0)
        return carry
    lax.fori_loop(0, ROWS, row, 0)


def warp_back(gw, from_above, from_below, f2, above, below):
    vm = pl.BlockSpec(memory_space=pltpu.VMEM)
    return pl.pallas_call(
        warp_back_kernel,
        out_shape=(
            jax.ShapeDtypeStruct((ROWS, SLOT, 256), F32),
            jax.ShapeDtypeStruct((ROWS, 8, 256), F32),
        ),
        in_specs=[vm] * 6,
        out_specs=(vm, vm),
        scratch_shapes=[pltpu.VMEM((ROWS + 1, SLOT, 256), F32), pltpu.VMEM((ROWS + 2, SLOT, 256), BF)],
        compiler_params=pltpu.CompilerParams(vmem_limit_bytes=32 * 2**20),
        name="warp_back",
    )(gw, from_above, from_below, f2, above, below)
WIDE, REST = lane_maps()
GATHER = gather_map()
PLANES = plane_map()

PIX = ("xy", "core")


def ring(axis, steps):
    count = lax.axis_size(axis)
    return [(i, i + steps) for i in range(max(0, -steps), min(count, count - steps))]


def around(value, step):
    return lax.ppermute(value, "chan", [(i, (i + step) % 4) for i in range(4)])


def local(
    feat_one, feat_two, up_flow, up_feat, target_flow, valid_mask,
    conv_one, conv_two, conv_three, conv_four, conv_five, flow_head,
    bias_one, bias_two, bias_three, bias_four, bias_five, bias_head,
):
    convs = [conv_one, conv_two, conv_three, conv_four, conv_five, flow_head]
    biases = [bias_one, bias_two, bias_three, bias_four, bias_five, bias_head]
    channels = feat_one.shape[0]
    place = lax.axis_index("chan")
    f2 = jnp.concatenate([feat_two, up_flow, jnp.zeros((SLOT - channels - 2, ROWS, 256), BF)], axis=0)
    f2 = jnp.transpose(f2, (1, 0, 2))
    above = lax.ppermute(f2[ROWS - MD :], PIX, ring(PIX, 1))
    below = lax.ppermute(f2[: MD + 1], PIX, ring(PIX, -1))
    f1 = jnp.transpose(jnp.pad(feat_one, ((0, SLOT - channels), (0, 0), (0, 0))), (1, 0, 2))
    packed = pack_warped(f2, above, below, pack_first(f1))
    packed, biases = lax.optimization_barrier((packed, biases))
    features = lax.all_to_all(packed, "chan", split_axis=0, concat_axis=0, tiled=True)
    features, *weights = lax.optimization_barrier((features, *arrange(convs, biases)))

    flow_cols = lax.dynamic_slice_in_dim(up_flow, place * COLS, COLS, 2)
    high = target_flow.astype(BF)
    low = (target_flow - high.astype(F32)).astype(BF)
    one = jnp.ones((2, ROWS, COLS), BF)
    planes = jnp.concatenate([flow_cols, up_feat, one, valid_mask.astype(BF)[None], high, low], axis=0)
    extra = lax.dot_general(
        planes, jnp.asarray(PLANES, BF), (((0,), (0,)), ((), ())), preferred_element_type=F32
    ).astype(BF)
    upper, lower = cost_volume(features, extra)
    top = lax.ppermute(lower, PIX, ring(PIX, 1))
    bottom = lax.ppermute(upper, PIX, ring(PIX, -1))
    tiles = [tile.reshape(27, COLS, 128) for tile in (top, upper, lower, bottom)]
    left = lax.ppermute(
        jnp.concatenate([tile[:, COLS - LEFT :] for tile in tiles], axis=0), "chan", ring("chan", 1)
    )
    right = lax.ppermute(
        jnp.concatenate([tile[:, :LEFT] for tile in tiles], axis=0), "chan", ring("chan", -1)
    )
    acts, slopes, main, rest, flow_out, sums = decode(
        top, upper, lower, bottom, left, right, *weights
    )
    core = lax.axis_index("core").astype(jnp.int32)[None]
    own, sent = wgrad(core, slopes, main, rest, acts, jnp.asarray(GATHER, BF))
    parts = chip_parts(own, sent, jnp.sum(sums[:, :, 96], axis=1))
    parts, slopes = lax.optimization_barrier((parts, slopes))
    parts = lax.all_to_all(parts, CHIPS, split_axis=0, concat_axis=0, tiled=True)
    here = place.astype(jnp.int32)[None]
    *payload, small = cost_back(here, features, slopes, weights[0], weights[2])
    returned = [payload[0]] + [around(payload[step], step) for step in range(1, 4)]
    parts, _ = lax.optimization_barrier((parts, payload[0]))
    spread, notes = spread_total(parts)
    spread, *returned = lax.optimization_barrier((spread, *returned))
    mine = lax.all_to_all(spread, CHIPS, split_axis=0, concat_axis=0, tiled=True).reshape(HALF_ROWS, 128)
    grad_one, partial, to_above, to_below = turn(here, returned)
    from_above = lax.ppermute(to_below, PIX, ring(PIX, 1))
    from_below = lax.ppermute(to_above, PIX, ring(PIX, -1))
    grad_two, grad_flow = warp_back(partial, from_above, from_below, f2, above, below)
    grad_feat_one = jnp.transpose(grad_one[:, :channels], (1, 0, 2))
    grad_feat_two = jnp.transpose(grad_two[:, :channels], (1, 0, 2))
    flow_parts = jnp.transpose(grad_flow[:, :2], (1, 0, 2))
    total = lax.dynamic_slice_in_dim(flow_parts, place * COLS, COLS, 2)
    flow_parts = flow_parts.astype(BF)
    for step in range(1, 4):
        sent = lax.dynamic_slice_in_dim(flow_parts, lax.rem(place + step, 4) * COLS, COLS, 2)
        total = total + lax.ppermute(sent, "chan", [(i, (i + step) % 4) for i in range(4)]).astype(F32)

    grad_up_flow = total + small[:2]
    mine, *outputs = lax.optimization_barrier(
        (mine, flow_out, grad_feat_one, grad_feat_two, grad_up_flow, small[2:])
    )
    flow_out, grad_feat_one, grad_feat_two, grad_up_flow, grad_up_feat = outputs
    weight_grads, bias_grads = unpack(core, mine, lax.ppermute(mine, "core", SWAP))
    scalars = jnp.sum(notes[:, :3], axis=0)
    return (flow_out, scalars, grad_feat_one, grad_feat_two, grad_up_flow, grad_up_feat, *weight_grads, *bias_grads)


def solution(mesh):
    chan, pix = mesh.devices.shape
    cores = jax.sharding.Mesh(mesh.devices.reshape(chan, pix // 2, 2), ("chan", "xy", "core"))
    return jax.shard_map(
        local,
        mesh=cores,
        in_specs=(
            P("chan", PIX, None),
            P("chan", PIX, None),
            P(None, PIX, None),
            P(None, PIX, "chan"),
            P(None, PIX, "chan"),
            P(PIX, "chan"),
        )
        + (P(),) * 12,
        out_specs=(
            P(None, PIX, "chan"),
            P(),
            P("chan", PIX, None),
            P("chan", PIX, None),
            P(None, PIX, "chan"),
            P(None, PIX, "chan"),
        )
        + (P(),) * 12,
        check_vma=False,
    )
```

```python
import functools
import jax
import jax.numpy as jnp
import numpy as np
from jax import lax
from jax.experimental import pallas as pl
from jax.experimental.pallas import tpu as pltpu
from jax.sharding import PartitionSpec as P

CH = 196
MD = 4
CH_SLOT = 49
OUTS = (128, 128, 96, 64, 32, 2)
ROW0 = (0, 128, 256, 384, 448, 480)
DEPTH = (281, 409, 537, 633, 697, 729)


def start_lane(channel):
    if channel < 81:
        dy, dx = divmod(channel, 9)
        if dy < 4:
            return 0, 64 * dy + 55 + dx
        if dy < 8:
            if 2 <= dx < 8:
                return 0, 64 * (dy - 4) + 47 + dx
            return 1, 2 * (dy - 4) + dx
        return 1, 16 + dx
    if channel < 277:
        slot, inner = divmod(channel - 81, CH_SLOT)
        return 0, 64 * slot + inner
    return 1, 9 + 2 * (channel - 277)


def lane_maps():
    wide = np.zeros((729, 768), np.float32)
    rest = np.zeros((729, 128), np.float32)
    for c in range(729):
        if c < 32:
            wide[c, 704 + c] = 1
        elif c < 96:
            wide[c, 640 + c - 32] = 1
        elif c < 192:
            wide[c, 512 + c - 96] = 1
        elif c < 320:
            wide[c, 384 + c - 192] = 1
        elif c < 448:
            wide[c, 256 + c - 320] = 1
        else:
            block, lane = start_lane(c - 448)
            if block == 0:
                wide[c, lane] = 1
            else:
                rest[c, lane] = 1
    return wide, rest


def gather_map():
    table = np.zeros((1024, 768), np.float32)
    for c in range(281):
        block, lane = start_lane(c)
        table[288 * block + lane, 448 + c] = 1
    table[288 + 25, 729] = 1
    for i in range(128):
        table[384 + i, 320 + i] = 1
        table[512 + i, 192 + i] = 1
    for i in range(96):
        table[640 + i, 96 + i] = 1
    for i in range(64):
        table[768 + i, 32 + i] = 1
    for i in range(32):
        table[896 + 64 + i, i] = 1
    return table


def plane_map():
    table = np.zeros((11, 128), np.float32)
    for plane, lane in enumerate((9, 11, 13, 15, 25, 26, 27, 28, 29, 30, 31)):
        table[plane, lane] = 1
    return table

CH = 196
MD = 4
BF = jnp.bfloat16
F32 = jnp.float32
HALO = 12
PITCH = 96
ROWS = 24
COLS = 64
LEFT = 16
WROWS = ROWS + 2 * HALO
NPX = WROWS * PITCH
GUARD = 16
VMEM_MB = 62


def nt(a, b):
    return lax.dot_general(a, b, (((1,), (1,)), ((), ())), preferred_element_type=F32)


def nn(a, b):
    return lax.dot_general(a, b, (((1,), (0,)), ((), ())), preferred_element_type=F32)


def decode_kernel(
    top_ref, h0_ref, h1_ref, bottom_ref, left_ref, right_ref, wm_ref, w_ref, wr_ref,
    a_ref, g_ref, xm_ref, xr_ref, flow_ref, met_ref,
    xs, xq, sh, pre, part, mk, sems,
):
    lane = lax.broadcasted_iota(jnp.int32, (PITCH, 128), 1)
    core = pl.ds(HALO * PITCH, ROWS * PITCH)

    def rows(lo, hi, body, unroll=2):
        def step(i, carry):
            for u in range(unroll):
                body(pl.multiple_of(lo * PITCH + (i * unroll + u) * PITCH, PITCH))
            return carry
        lax.fori_loop(0, (hi - lo) // unroll, step, 0)

    def put_shifted(dst, p, lanes, value):
        height = value.shape[0]
        dst[0, pl.ds(p, PITCH), lanes] = pltpu.roll(value, 1, 0).astype(BF)
        dst[1, pl.ds(p, PITCH), lanes] = value.astype(BF)
        dst[2, pl.ds(p, PITCH), lanes] = pltpu.roll(value, height - 1, 0).astype(BF)

    def chunked(lo, hi, count, body):
        size = (hi - lo) * PITCH // count

        def step(i, carry):
            body(pl.multiple_of(lo * PITCH + i * size, 16), size)
            return carry
        lax.fori_loop(0, count, step, 0)

    for h, tile in enumerate((top_ref, h0_ref, h1_ref, bottom_ref)):
        def main_rows(step, carry, h=h, tile=tile):
            for i, half in [(3 * step + u, half) for u in range(3) for half in range(2)]:
                p = pl.multiple_of((12 * h + i) * PITCH, PITCH)
                at = pl.multiple_of((12 * half + i) * COLS, COLS)
                value = jnp.concatenate(
                    [
                        left_ref[27 * h + 12 * half + i].astype(F32),
                        tile[pl.ds(at, COLS), :].astype(F32),
                        right_ref[27 * h + 12 * half + i].astype(F32),
                    ],
                    axis=0,
                )
                put_shifted(xs, p, slice(128 * half, 128 * half + 128), value)
            return carry
        lax.fori_loop(0, 4, main_rows, 0)

        def rest_rows(b, carry, h=h, tile=tile):
            packed = jnp.concatenate(
                [
                    left_ref[27 * h + 24 + b].astype(F32),
                    tile[pl.ds(pl.multiple_of(1536 + b * COLS, COLS), COLS), :].astype(F32),
                    right_ref[27 * h + 24 + b].astype(F32),
                ],
                axis=0,
            )
            for a in range(4):
                p = pl.multiple_of((12 * h + 3 * a + b) * PITCH, PITCH)
                value = jnp.where(lane < 32, pltpu.roll(packed, (128 - 32 * a) % 128, 1), 0.0)
                mk[pl.ds(p, PITCH), :] = jnp.broadcast_to(value[:, 25:26], (PITCH, 128))
                low = pltpu.roll(value, 1, 0)
                mid = pltpu.roll(value, 32, 1)
                high = pltpu.roll(pltpu.roll(value, PITCH - 1, 0), 64, 1)
                xq[pl.ds(p, PITCH), :] = (low + mid + high).astype(BF)
            return carry
        for b in range(3):
            rest_rows(b, 0)

    keep = [
        pltpu.make_async_copy(xs.at[1, core, :], xm_ref, sems.at[1]),
        pltpu.make_async_copy(xq.at[core, :], xr_ref, sems.at[2]),
    ]
    for copy in keep:
        copy.start()

    def start_sums(lo, hi):
        p, size = lo * PITCH, (hi - lo) * PITCH
        left = jnp.concatenate([xq[pl.ds(p + PITCH * (dy - 1), size), :] for dy in range(3)], axis=1)
        total = nt(left, jnp.concatenate([wr_ref[dy] for dy in range(3)], axis=1))
        for dy in range(3):
            at = p + PITCH * (dy - 1)
            for dx in range(3):
                total = total + nt(xs[dx, pl.ds(at, size), :], wm_ref[3 * dy + dx])
        pre[pl.ds(p, size), :] = total

    first_lane = [0, 128, 256, 384, 384]
    lanes_of = [(0, 128), (0, 128), (0, 96), (0, 64), (64, 96)]
    kept = []

    def activate(layer, lo, hi):
        block = slice(first_lane[layer], first_lane[layer] + 128)
        inside = (lane >= lanes_of[layer][0]) & (lane < lanes_of[layer][1])
        piece = min(layer, 3)
        lanes = slice(128 * piece, 128 * piece + 128)
        for p in range(lo * PITCH, hi * PITCH, PITCH):
            value = pre[pl.ds(p, PITCH), block]
            sig = 0.5 * jnp.tanh(0.5 * value) + 0.5
            live = mk[pl.ds(p, PITCH), :] > 0.0
            if layer >= 3:
                live = live & inside
            act = value * sig
            slope = jnp.where(live, sig + act * (1.0 - sig), 0.0)
            if layer >= 3:
                slope = jnp.where(inside, slope, value)
            pre[pl.ds(p, PITCH), block] = slope
            put_shifted(sh, p, lanes, jnp.where(live, act, 0.0))

    def add_sums(layer, lo, hi):
        p, size = lo * PITCH, (hi - lo) * PITCH
        piece = min(layer, 3)
        out0 = min(128 * (layer + 1), 384)
        lanes = slice(128 * piece, 128 * piece + 128)
        left = jnp.concatenate(
            [sh[dx, pl.ds(p + PITCH * (dy - 1), size), lanes] for dy in range(3) for dx in range(3)], axis=1
        )
        right = jnp.concatenate([w_ref[k, out0:512, lanes] for k in range(9)], axis=1)
        pre[pl.ds(p, size), out0:512] = pre[pl.ds(p, size), out0:512] + nt(left, right)

    def bounds(lo, hi, shift):
        return [(lo, 18 - shift), (18 - shift, 33 - shift), (33 - shift, hi)]

    sums_of = [[functools.partial(start_sums, *r) for r in bounds(1, WROWS - 1, 0)]]
    for layer in range(5):
        sums_of.append(
            [functools.partial(add_sums, layer, *r) for r in bounds(layer + 2, WROWS - layer - 2, layer + 1)]
        )
    sums_of[0][0]()
    for layer in range(5):
        acts = [functools.partial(activate, layer, *r) for r in bounds(layer + 1, WROWS - layer - 1, layer)]
        sums_of[layer][1]()
        if layer == 4:
            kept[3].wait()
        acts[0]()
        sums_of[layer][2]()
        acts[1]()
        sums_of[layer + 1][0]()
        acts[2]()
        piece = min(layer, 3)
        copy = pltpu.make_async_copy(
            sh.at[1, core, 128 * piece : 128 * piece + 128],
            a_ref.at[:, 128 * layer : 128 * layer + 128],
            sems.at[3 + layer],
        )
        copy.start()
        kept.append(copy)
    sums_of[5][1]()
    sums_of[5][2]()

    is_flow = (lane >= 96) & (lane < 98)
    column = lax.broadcasted_iota(jnp.int32, (PITCH, 128), 0)
    core_column = (column >= LEFT) & (column < LEFT + COLS)
    met_ref[...] = jnp.zeros((3, PITCH, 128), F32)
    kept[0].wait()
    kept[1].wait()
    kept[2].wait()
    kept[4].wait()

    def loss(p):
        flow = pre[pl.ds(p, PITCH), 384:512]
        rest = xq[pl.ds(p, PITCH), :].astype(F32)
        target = pltpu.roll(rest, 96 - 60, 1) + pltpu.roll(rest, 96 - 62, 1)
        diff = jnp.where(is_flow, flow - target, 0.0)
        square = diff * diff
        other = jnp.where(lane == 96, pltpu.roll(square, 127, 1), pltpu.roll(square, 1, 1))
        error = jnp.sqrt(square + other + 1.0)
        mask = jnp.broadcast_to(rest[:, 59:60], (PITCH, 128))
        put_shifted(sh, p, slice(384, 512), jnp.where(is_flow, mask * diff / error, 0.0))
        return flow, mask, error

    def loss_rim(p):
        loss(p)

    def loss_core(p):
        flow, mask, error = loss(p)
        r = lax.div(p, PITCH) - HALO
        turned = jnp.transpose(flow)
        for n in range(2):
            flow_ref[n, pl.ds(r, 1), :] = turned[96 + n : 97 + n, LEFT : LEFT + COLS]
        mask = jnp.where(core_column, mask, 0.0)
        met_ref[0] += mask * (error - 1.0)
        met_ref[1] += mask / (1.0 + jnp.exp(-4.0 * (error - 2.0)))
        met_ref[2] += mask

    rows(6, HALO, loss_rim)
    rows(HALO, HALO + ROWS, loss_core)
    rows(HALO + ROWS, WROWS - 6, loss_rim)

    def back(layer, lo, hi):
        p, size = lo * PITCH, (hi - lo) * PITCH
        piece = min(layer, 3)
        out0 = min(128 * (layer + 1), 384)
        left = jnp.concatenate(
            [sh[2 - dx, pl.ds(p - PITCH * (dy - 1), size), out0:512] for dy in range(3) for dx in range(3)], axis=1
        )
        right = jnp.concatenate([w_ref[k, out0:512, 128 * piece : 128 * piece + 128] for k in range(9)], axis=0)
        part[pl.ds(p, size), :] = nn(left, right)

    def slope(layer, lo, hi):
        block = slice(first_lane[layer], first_lane[layer] + 128)
        inside = (lane >= lanes_of[layer][0]) & (lane < lanes_of[layer][1])
        piece = min(layer, 3)
        lanes = slice(128 * piece, 128 * piece + 128)
        for p in range(lo * PITCH, hi * PITCH, PITCH):
            value = part[pl.ds(p, PITCH), :] * pre[pl.ds(p, PITCH), block]
            if layer >= 3:
                value = jnp.where(inside, value, sh[1, pl.ds(p, PITCH), lanes].astype(F32))
            put_shifted(sh, p, lanes, value)

    def back_bounds(layer):
        lo, hi = HALO - layer - 1, HALO + ROWS + layer + 1
        return [(lo, 16 + layer), (16 + layer, 26 + layer), (26 + layer, hi)]

    back(4, *back_bounds(4)[0])
    for layer in range(4, -1, -1):
        parts = back_bounds(layer)
        back(layer, *parts[1])
        slope(layer, *parts[0])
        back(layer, *parts[2])
        slope(layer, *parts[1])
        if layer > 0:
            back(layer - 1, *back_bounds(layer - 1)[0])
        slope(layer, *parts[2])
        if layer < 4:
            lanes = slice(128 * layer, 128 * layer + 128)
            copy = pltpu.make_async_copy(
                sh.at[:, pl.ds((HALO - 1) * PITCH, (ROWS + 2) * PITCH), lanes], g_ref.at[:, :, lanes], sems.at[8 + layer]
            )
            copy.start()
            keep.append(copy)

    for copy in keep:
        copy.wait()


def decode(*operands):
    size = ROWS * PITCH
    vm = pl.BlockSpec(memory_space=pltpu.VMEM)
    hbm = pl.BlockSpec(memory_space=pl.ANY)
    return pl.pallas_call(
        decode_kernel,
        out_shape=(
            jax.ShapeDtypeStruct((size, 640), BF),
            jax.ShapeDtypeStruct((3, (ROWS + 2) * PITCH, 512), BF),
            jax.ShapeDtypeStruct((size, 256), BF),
            jax.ShapeDtypeStruct((size, 128), BF),
            jax.ShapeDtypeStruct((2, ROWS, COLS), F32),
            jax.ShapeDtypeStruct((3, PITCH, 128), F32),
        ),
        in_specs=[vm] * 9,
        out_specs=(hbm, hbm, hbm, hbm, vm, vm),
        scratch_shapes=[
            pltpu.VMEM((3, NPX, 256), BF),
            pltpu.VMEM((NPX, 128), BF),
            pltpu.VMEM((3, NPX, 512), BF),
            pltpu.VMEM((NPX, 512), F32),
            pltpu.VMEM((NPX, 128), F32),
            pltpu.VMEM((NPX, 128), F32),
            pltpu.SemaphoreType.DMA((12,)),
        ],
        compiler_params=pltpu.CompilerParams(vmem_limit_bytes=VMEM_MB * 2**20),
        name="decode",
    )(*operands)


def arrange_kernel(c1, c2, c3, c4, c5, c6, wide_ref, rest_ref, bias_ref, wm_ref, w_ref, wr_ref):
    for rows in (slice(352, 384), slice(480, 512)):
        wm_ref[:, rows, :] = jnp.zeros((9, 32, 256), BF)
        w_ref[:, rows, :] = jnp.zeros((9, 32, 512), BF)
    wr_ref[:, 352:384, :] = jnp.zeros((3, 32, 128), BF)
    wr_ref[:, 480:512, :] = jnp.zeros((3, 32, 128), BF)
    lane = lax.broadcasted_iota(jnp.int32, (512, 128), 1)
    bias = bias_ref[...]
    high = bias.astype(BF).astype(F32)
    bias = jnp.where(lane == 57, high, jnp.where(lane == 58, bias - high, 0.0))

    for n, ref in enumerate((c1, c2, c3, c4, c5, c6)):
        outs, depth = OUTS[n], DEPTH[n]
        rows = slice(ROW0[n], ROW0[n] + outs)
        wide = wide_ref[729 - depth :, :]
        rest = rest_ref[729 - depth :, :]
        dims = (((0,), (0,)), ((), ())) if n < 2 else (((1,), (0,)), ((), ()))
        for dy in range(3):
            total = bias[rows] if dy == 1 else jnp.zeros((outs, 128), F32)
            for dx in range(3):
                weight = ref[3 * dy + dx]
                value = lax.dot_general(weight, wide, dims, preferred_element_type=F32).astype(BF)
                wm_ref[3 * dy + dx, rows, :] = value[:, 0:256]
                w_ref[3 * dy + dx, rows, :] = value[:, 256:768]
                part = lax.dot_general(weight, rest, dims, preferred_element_type=F32)
                total = total + (pltpu.roll(part, 32 * dx, 1) if dx else part)
            wr_ref[dy, rows, :] = total.astype(BF)


def arrange(convs, biases):
    vm = pl.BlockSpec(memory_space=pltpu.VMEM)
    bias = jnp.concatenate(
        [biases[0], biases[1], biases[2], jnp.zeros((32,), F32), biases[3], biases[4], biases[5], jnp.zeros((30,), F32)]
    ).reshape(512, 1)
    turned = [jnp.transpose(convs[0], (0, 2, 1)), jnp.transpose(convs[1], (0, 2, 1))]
    return pl.pallas_call(
        arrange_kernel,
        out_shape=(
            jax.ShapeDtypeStruct((9, 512, 256), BF),
            jax.ShapeDtypeStruct((9, 512, 512), BF),
            jax.ShapeDtypeStruct((3, 512, 128), BF),
        ),
        in_specs=[vm] * 9,
        out_specs=(vm, vm, vm),
        compiler_params=pltpu.CompilerParams(vmem_limit_bytes=40 * 2**20),
        cost_estimate=pl.CostEstimate(flops=4 * 10**9, bytes_accessed=16 * 10**6, transcendentals=0),
        name="arrange",
    )(*turned, *convs[2:], jnp.asarray(WIDE, BF), jnp.asarray(REST, BF), bias)

TILE_ROWS = 2048
TOTAL_ROWS = 9 * TILE_ROWS
HALF_ROWS = TOTAL_ROWS // 2


def tn(a, b):
    return lax.dot_general(a, b, (((0,), (0,)), ((), ())), preferred_element_type=F32)


def wgrad_kernel(core_ref, g_hbm, xm_ref, xr_ref, a_ref, qp_ref, own_ref, sent_ref, g_ref, xp, o_ref, loads, stores):
    for d in range(3):
        pltpu.make_async_copy(g_hbm.at[d], g_ref.at[d], loads.at[d]).start()
    column = lax.broadcasted_iota(jnp.int32, (PITCH, 128), 0)
    core = (column >= LEFT) & (column < LEFT + COLS)
    core = jnp.concatenate([core] * 4, axis=0)
    size = 4 * PITCH

    def gather(i, carry):
        at = pl.ds(pl.multiple_of(i * size, size), size)
        left = jnp.concatenate([xm_ref[at, :], xr_ref[at, :], a_ref[at, 0:128]], axis=1)
        parts = [
            nn(a_ref[at, 128:640], qp_ref[512:1024, 0:256]),
            nn(a_ref[at, 0:256], qp_ref[384:640, 256:384]),
            nn(left, qp_ref[0:512, 384:768]),
        ]
        value = jnp.concatenate(parts, axis=1)
        for t in range(6):
            lanes = slice(128 * t, 128 * t + 128)
            xp[at, lanes] = jnp.where(core, value[:, lanes], 0.0).astype(BF)
        return carry
    lax.fori_loop(0, ROWS // 4, gather, 0)
    for d in range(3):
        pltpu.make_async_copy(g_hbm.at[d], g_ref.at[d], loads.at[d]).wait()

    part_rows = TILE_ROWS // 2

    def store(n, act):
        half, place = divmod(n, 9)
        for target, mine in ((own_ref, True), (sent_ref, False)):
            @pl.when((core_ref[0] == half) == mine)
            def _():
                act(
                    pltpu.make_async_copy(
                        o_ref.at[pl.ds(part_rows * n, part_rows), :],
                        target.at[pl.ds(part_rows * place, part_rows), :],
                        stores.at[n],
                    )
                )

    for k in range(9):
        dy, dx = divmod(k, 3)
        at = pl.ds(PITCH * (2 - dy), ROWS * PITCH)
        base = TILE_ROWS * k
        low = tn(g_ref[2 - dx, at, 0:256], xp[:, 256:768]).astype(BF)
        for t in range(3):
            o_ref[base + 128 * t : base + 128 * t + 128, :] = low[0:128, 128 * t + 128 : 128 * t + 256]
        for t in range(4):
            o_ref[base + 384 + 128 * t : base + 512 + 128 * t, :] = low[128:256, 128 * t : 128 * t + 128]
        low = tn(g_ref[2 - dx, at, 256:512], xp[...]).astype(BF)
        for t in range(5):
            o_ref[base + 896 + 96 * t : base + 992 + 96 * t, :] = low[0:96, 128 * t + 128 : 128 * t + 256]
        for t in range(6):
            o_ref[base + 1376 + 112 * t : base + 1488 + 112 * t, :] = low[128:240, 128 * t : 128 * t + 128]
        store(2 * k, lambda copy: copy.start())
        store(2 * k + 1, lambda copy: copy.start())
    for n in range(18):
        store(n, lambda copy: copy.wait())


def wgrad(core, g, xm, xr, a, qp):
    vm = pl.BlockSpec(memory_space=pltpu.VMEM)
    hbm = pl.BlockSpec(memory_space=pl.ANY)
    return pl.pallas_call(
        wgrad_kernel,
        out_shape=(jax.ShapeDtypeStruct((HALF_ROWS, 128), BF),) * 2,
        in_specs=[pl.BlockSpec(memory_space=pltpu.SMEM), hbm] + [vm] * 4,
        out_specs=(hbm, hbm),
        scratch_shapes=[
            pltpu.VMEM((3, (ROWS + 2) * PITCH, 512), BF),
            pltpu.VMEM((ROWS * PITCH, 768), BF),
            pltpu.VMEM((TOTAL_ROWS, 128), BF),
            pltpu.SemaphoreType.DMA((3,)),
            pltpu.SemaphoreType.DMA((18,)),
        ],
        compiler_params=pltpu.CompilerParams(vmem_limit_bytes=VMEM_MB * 2**20),
        name="wgrad",
    )(core, g, xm, xr, a, qp)

NOTE = 16


def half_sum_kernel(own_ref, got_ref, note_ref, got_note_ref, o_ref):
    count, height = o_ref.shape[0], o_ref.shape[1] - NOTE
    notes = jnp.concatenate([note_ref[0:8].astype(F32), got_note_ref[0:8].astype(F32)], axis=0).astype(BF)
    for b in range(count):
        rows = slice(height * b, height * (b + 1))
        o_ref[b, 0:height] = (own_ref[rows, :].astype(F32) + got_ref[rows, :].astype(F32)).astype(BF)
        o_ref[b, height:] = notes


def half_sum(own, got, note, got_note, count):
    height = HALF_ROWS // count
    steps = 2
    block = HALF_ROWS // steps
    return pl.pallas_call(
        half_sum_kernel,
        grid=(steps,),
        in_specs=[
            pl.BlockSpec((block, 128), lambda i: (i, 0)),
            pl.BlockSpec((block, 128), lambda i: (i, 0)),
            pl.BlockSpec((NOTE, 128), lambda i: (0, 0)),
            pl.BlockSpec((NOTE, 128), lambda i: (0, 0)),
        ],
        out_specs=pl.BlockSpec((count // steps, height + NOTE, 128), lambda i: (i, 0, 0)),
        out_shape=jax.ShapeDtypeStruct((count, height + NOTE, 128), BF),
        compiler_params=pltpu.CompilerParams(vmem_limit_bytes=32 * 2**20),
        name="half_sum",
    )(own, got, note, got_note)


def spread_kernel(parts_ref, o_ref, note_ref):
    count, height = o_ref.shape[0], o_ref.shape[1]

    def add(b, carry):
        total, notes = carry
        return total + parts_ref[b, 0:height].astype(F32), notes + parts_ref[b, height:].astype(F32)
    zero = (jnp.zeros((height, 128), F32), jnp.zeros((NOTE, 128), F32))
    total, notes = lax.fori_loop(0, count, add, zero)
    note_ref[...] = notes
    total = total.astype(BF)

    def put(b, carry):
        o_ref[b] = total
        return carry
    lax.fori_loop(0, count, put, 0)


def spread_total(parts):
    count, height, _ = parts.shape
    vm = pl.BlockSpec(memory_space=pltpu.VMEM)
    return pl.pallas_call(
        spread_kernel,
        out_shape=(
            jax.ShapeDtypeStruct((count, height - NOTE, 128), BF),
            jax.ShapeDtypeStruct((NOTE, 128), F32),
        ),
        in_specs=[vm],
        out_specs=(vm, vm),
        compiler_params=pltpu.CompilerParams(vmem_limit_bytes=32 * 2**20),
        name="spread_total",
    )(parts)


def unpack_kernel(
    core_ref, mine_ref, other_ref, o1, o2, o3, o4, o5, o6, b1, b2, b3, b4, b5, b6, all_ref, sems
):
    k = pl.program_id(0)

    @pl.when(k == 0)
    def _():
        core = core_ref[0]
        copies = [
            pltpu.make_async_copy(
                source, all_ref.at[pl.ds(pl.multiple_of(at * HALF_ROWS, HALF_ROWS), HALF_ROWS), :], sems.at[n]
            )
            for n, (source, at) in enumerate(((mine_ref, core), (other_ref, 1 - core)))
        ]
        for copy in copies:
            copy.start()
        for copy in copies:
            copy.wait()
    def tiles(j, base, height, count):
        first = pl.multiple_of((3 * k + j) * TILE_ROWS, TILE_ROWS)
        return jnp.concatenate(
            [all_ref[pl.ds(first + base + height * t, height), :].astype(F32) for t in range(count)], axis=1
        )
    for j in range(3):
        o1[j] = jnp.transpose(tiles(j, 0, 128, 3))[64 : 64 + 281]
        o2[j] = jnp.transpose(tiles(j, 384, 128, 4))[64 : 64 + 409]
        o3[j] = tiles(j, 896, 96, 5)[:, 64 : 64 + 537]
        last = tiles(j, 1376, 112, 6)
        o4[j] = last[0:64, 96:729]
        o5[j] = last[64:96, 32:729]
        o6[j] = last[96:98, 0:729]

    @pl.when(k == 1)
    def _():
        biases = [tiles(1, 256, 128, 1), tiles(1, 768, 128, 1), tiles(1, 1280, 96, 1), tiles(1, 1936, 112, 1)]
        biases = [jnp.transpose(value)[89:90] for value in biases]
        b1[...] = biases[0]
        b2[...] = biases[1]
        b3[...] = biases[2]
        b4[...] = biases[3][:, 0:64]
        b5[...] = biases[3][:, 64:96]
        b6[...] = biases[3][:, 96:98]


def unpack(core, mine, other):
    shapes = ((281, 128), (409, 128), (96, 537), (64, 633), (32, 697), (2, 729))
    hbm = pl.BlockSpec(memory_space=pl.ANY)
    results = pl.pallas_call(
        unpack_kernel,
        grid_spec=pltpu.PrefetchScalarGridSpec(
            num_scalar_prefetch=1,
            grid=(3,),
            in_specs=[hbm, hbm],
            out_specs=tuple(pl.BlockSpec((3,) + s, lambda k, core: (k, 0, 0)) for s in shapes)
            + tuple(pl.BlockSpec((1, outs), lambda k, core: (0, 0)) for outs in OUTS),
            scratch_shapes=[pltpu.VMEM((TOTAL_ROWS, 128), BF), pltpu.SemaphoreType.DMA((2,))],
        ),
        out_shape=tuple(jax.ShapeDtypeStruct((9,) + s, F32) for s in shapes)
        + tuple(jax.ShapeDtypeStruct((1, outs), F32) for outs in OUTS),
        compiler_params=pltpu.CompilerParams(vmem_limit_bytes=32 * 2**20),
        name="unpack",
    )(core, mine, other)
    grads = list(results[:6])
    grads[0] = jnp.transpose(grads[0], (0, 2, 1))
    grads[1] = jnp.transpose(grads[1], (0, 2, 1))
    return grads, [bias.reshape(-1) for bias in results[6:]]


SWAP = [(0, 1), (1, 0)]
CHIPS = ("chan", "xy")


def chip_parts(own, sent, scalars):
    high = lax.reduce_precision(scalars, 8, 7)
    middle = lax.reduce_precision(scalars - high, 8, 7)
    low = scalars - high - middle
    note = jnp.stack([high, middle, low]).astype(BF)
    note = jnp.pad(note, ((0, NOTE - 3), (0, 128 - scalars.shape[0])))
    got_note = lax.ppermute(note, "core", SWAP)
    got = lax.ppermute(sent, "core", SWAP)
    return half_sum(own, got, note, got_note, lax.axis_size(CHIPS))

SLOT = 64
WIN = 80
PAY = 12 * COLS + 16 * WIN
HALF = 27 * COLS


def slanted(x, shift):
    shift = shift % 128
    if shift % 8:
        x = pltpu.roll(x, shift % 8, 1)
    return pltpu.roll(x, shift - shift % 8, 1, stride=1, stride_axis=0)


def two_rows(lane, parts):
    swap = [pltpu.roll(part, 64, 1) for part in parts]
    first = [jnp.where(lane < 64, parts[2 * h], swap[2 * h + 1]) for h in range(2)]
    second = [jnp.where(lane < 64, swap[2 * h], parts[2 * h + 1]) for h in range(2)]
    return jnp.concatenate(first, axis=1), jnp.concatenate(second, axis=1)


def diagonal(size, back):
    i = lax.broadcasted_iota(jnp.int32, (size, size), 0)
    j = lax.broadcasted_iota(jnp.int32, (size, size), 1)
    return jnp.where(i + j == size - 1 if back else i == j, 1.0, 0.0).astype(BF)


def pack_first_kernel(f1_ref, o_hbm, o_ref, sem):
    back = diagonal(256, True)

    def first(step, carry):
        for i in (3 * step, 3 * step + 1, 3 * step + 2):
            both = jnp.concatenate([f1_ref[i], f1_ref[i + 12]], axis=0)
            value = nt(back, both).astype(BF)
            for z in range(4):
                o_ref[z, pl.ds(pl.multiple_of(i * COLS, COLS), COLS), :] = value[192 - COLS * z : 256 - COLS * z]
        return carry
    lax.fori_loop(0, 4, first, 0)
    copy = pltpu.make_async_copy(o_ref, o_hbm.at[:, pl.ds(0, 12 * COLS), :], sem)
    copy.start()
    copy.wait()


def pack_first(f1):
    return pl.pallas_call(
        pack_first_kernel,
        out_shape=jax.ShapeDtypeStruct((4, PAY, 128), BF),
        in_specs=[pl.BlockSpec(memory_space=pltpu.VMEM)],
        out_specs=pl.BlockSpec(memory_space=pl.ANY),
        scratch_shapes=[pltpu.VMEM((4, 12 * COLS, 128), BF), pltpu.SemaphoreType.DMA],
        compiler_params=pltpu.CompilerParams(vmem_limit_bytes=32 * 2**20),
        name="pack_first",
    )(f1)


def pack_warped_kernel(f2_ref, above_ref, below_ref, first_hbm, o_hbm, o_ref, band, turn, sem):
    eye = diagonal(256, False)
    last = lax.broadcasted_iota(jnp.int32, (SLOT, 256), 1) == 255
    channel = lax.broadcasted_iota(jnp.int32, (SLOT, 256), 0) < CH // 4
    band[0:MD] = above_ref[...]
    band[MD : MD + ROWS] = f2_ref[...]
    band[MD + ROWS :] = below_ref[...]
    turn[...] = jnp.zeros(turn.shape, F32)

    def warped(t):
        upper = band[t].astype(F32)
        lower = band[t + 1].astype(F32)
        u = upper[49:50]
        v = upper[50:51]

        def across(x):
            return (1.0 - u) * x + u * jnp.where(last, 0.0, pltpu.roll(x, 255, 1))
        value = (1.0 - v) * across(upper) + v * across(lower)
        return jnp.where(channel, value, 0.0).astype(BF)

    def second(step, carry):
        for u in range(4):
            i = 4 * step + u
            both = jnp.concatenate([warped(i), warped(i + 16)], axis=0)
            turn[u, 8:264, :] = nt(eye, both)
            for z in range(4):
                start = pl.multiple_of(i * WIN, 16)
                o_ref[z, pl.ds(start, WIN), :] = turn[u, COLS * z + 4 : COLS * z + 4 + WIN, :].astype(BF)
        return carry
    lax.fori_loop(0, 4, second, 0)
    copy = pltpu.make_async_copy(o_ref, o_hbm.at[:, pl.ds(12 * COLS, 16 * WIN), :], sem)
    copy.start()
    copy.wait()


def pack_warped(f2, above, below, packed):
    vm = pl.BlockSpec(memory_space=pltpu.VMEM)
    hbm = pl.BlockSpec(memory_space=pl.ANY)
    return pl.pallas_call(
        pack_warped_kernel,
        out_shape=jax.ShapeDtypeStruct((4, PAY, 128), BF),
        in_specs=[vm, vm, vm, hbm],
        out_specs=hbm,
        input_output_aliases={3: 0},
        scratch_shapes=[
            pltpu.VMEM((4, 16 * WIN, 128), BF),
            pltpu.VMEM((33, SLOT, 256), BF),
            pltpu.VMEM((4, 288, 128), F32),
            pltpu.SemaphoreType.DMA,
        ],
        compiler_params=pltpu.CompilerParams(vmem_limit_bytes=32 * 2**20),
        name="pack_warped",
    )(f2, above, below, packed)


def flip_matrix():
    total = lax.broadcasted_iota(jnp.int32, (COLS, COLS), 0) + lax.broadcasted_iota(jnp.int32, (COLS, COLS), 1)
    return jnp.where(total == COLS - 1, 1.0, 0.0).astype(BF)


def read_features(rx_ref, lane, first_rows, warped_rows):
    def first(step, carry):
        for i in (3 * step, 3 * step + 1, 3 * step + 2):
            at = pl.ds(pl.multiple_of(i * COLS, COLS), COLS)
            one, two = two_rows(lane[:COLS], [rx_ref[q, at, :].astype(F32) for q in range(4)])
            first_rows(i, one.astype(BF))
            first_rows(i + 12, two.astype(BF))
        return carry
    lax.fori_loop(0, 4, first, 0)

    def second(step, carry):
        for i in (4 * step, 4 * step + 1, 4 * step + 2, 4 * step + 3):
            at = pl.ds(pl.multiple_of(12 * COLS + i * WIN, 16), WIN)
            one, two = two_rows(lane[:WIN], [rx_ref[q, at, :].astype(F32) for q in range(4)])
            warped_rows(i, one.astype(BF))
            warped_rows(i + 16, two.astype(BF))
        return carry
    lax.fori_loop(0, 4, second, 0)


def flip_four():
    i = lax.broadcasted_iota(jnp.int32, (4 * COLS, 4 * COLS), 0)
    j = lax.broadcasted_iota(jnp.int32, (4 * COLS, 4 * COLS), 1)
    here = ((i & (COLS - 1)) + (j & (COLS - 1)) == COLS - 1) & ((i & -COLS) == (j & -COLS))
    return jnp.where(here, 1.0, 0.0).astype(BF)


def cost_kernel(rx_ref, ex_ref, h0_ref, h1_ref, fs, ws, ms, vs, rs):
    lane = lax.broadcasted_iota(jnp.int32, (128, 128), 1)

    def put_first(i, value):
        fs[i] = value

    def put_warped(i, value):
        ws[i, 0:WIN] = value
    read_features(rx_ref, lane, put_first, put_warped)
    lane = lane[:COLS]
    flip = flip_four()

    for half, out in ((0, h0_ref), (1, h1_ref)):
        def group(g, carry, half=half, out=out):
            i = 12 * half + 4 * g
            ms[...] = nt(fs[pl.ds(i, 4)].reshape(4 * COLS, 256), ws[pl.ds(i, 12)].reshape(12 * 128, 256))
            for r in range(4):
                rows = slice(COLS * r, COLS * r + COLS)

                def band(dy, t, here, value, r=r, rows=rows):
                    block = slanted(ms[rows, 128 * (r + dy) : 128 * (r + dy) + 128], t - 63)
                    return jnp.where(here, block * (1.0 / CH**0.5), value)
                for h in range(2):
                    value = fs[i + r, :, 128 * h : 128 * h + 128].astype(F32)
                    for s in range(2):
                        at = 64 * s + 47
                        value = band(2 * h + s, at + 8, (lane >= at + 8) & (lane < at + 17), value)
                        value = band(4 + 2 * h + s, at, (lane >= at + 2) & (lane < at + 8), value)
                    vs[rows, 128 * h : 128 * h + 128] = value.astype(BF)
                value = jnp.zeros((COLS, 128), F32)
                for a in range(4):
                    here = (lane == 2 * a) | (lane == 2 * a + 1) | (lane == 2 * a + 8)
                    value = band(4 + a, 2 * a, here, value)
                vs[rows, 256:384] = band(8, 16, (lane >= 16) & (lane < 25), value).astype(BF)
            turned = nn(flip, vs[...])
            for h in range(2):
                at = pl.multiple_of(768 * h + 4 * g * COLS, 4 * COLS)
                out[pl.ds(at, 4 * COLS), :] = turned[:, 128 * h : 128 * h + 128].astype(BF)
            rs[pl.ds(i, 4)] = turned[:, 256:384].reshape(4, COLS, 128) + ex_ref[pl.ds(i, 4)].astype(F32)
            return carry
        lax.fori_loop(0, 3, group, 0)
    for half, out in ((0, h0_ref), (1, h1_ref)):
        for b in range(3):
            total = rs[12 * half + b]
            for a in range(1, 4):
                total = total + pltpu.roll(rs[12 * half + 3 * a + b], 32 * a, 1)
            out[1536 + COLS * b : 1536 + COLS * b + COLS, :] = total.astype(BF)


def cost_volume(rx, extra):
    vm = pl.BlockSpec(memory_space=pltpu.VMEM)
    return pl.pallas_call(
        cost_kernel,
        out_shape=(jax.ShapeDtypeStruct((HALF, 128), BF),) * 2,
        in_specs=[vm] * 2,
        out_specs=(vm, vm),
        scratch_shapes=[
            pltpu.VMEM((ROWS, COLS, 256), BF),
            pltpu.VMEM((ROWS + 8, 128, 256), BF),
            pltpu.VMEM((4 * COLS, 12 * 128), F32),
            pltpu.VMEM((4 * COLS, 384), BF),
            pltpu.VMEM((ROWS, COLS, 128), F32),
        ],
        compiler_params=pltpu.CompilerParams(vmem_limit_bytes=32 * 2**20),
        name="cost_volume",
    )(rx, extra)


def cost_back_kernel(
    place_ref, rx_ref, sh_hbm, w_hbm, wr_ref, o0, o1, o2, o3, plane_ref,
    o_ref, dr_ref, dm_ref, part, fs, ws, bs, gs, gw, sh, w_ref, sems
):
    loads = [pltpu.make_async_copy(sh_hbm, sh, sems.at[0]), pltpu.make_async_copy(w_hbm, w_ref, sems.at[1])]
    for load in loads:
        load.start()
    lane = lax.broadcasted_iota(jnp.int32, (128, 128), 1)
    zero = jnp.zeros((8, COLS, 256), BF)
    fs[0:8] = zero
    fs[32:40] = zero
    flip = flip_matrix()

    def put_first(i, value):
        fs[i + 8] = nn(flip, value).astype(BF)

    def put_warped(i, value):
        ws[i, 0:WIN] = value
        ws[i, WIN:] = jnp.zeros((128 - WIN, 256), BF)
    read_features(rx_ref, lane, put_first, put_warped)

    for load in loads:
        load.wait()

    def back_rest(i, carry):
        p = pl.multiple_of(i * 8 * PITCH, 8 * PITCH)
        total = None
        for dy in range(3):
            term = nn(sh[1, pl.ds(p + PITCH * (2 - dy), 8 * PITCH), :], wr_ref[dy])
            total = term if total is None else total + term
        part[...] = total
        for r in range(8):
            value = part[PITCH * r : PITCH * (r + 1), :]
            value = (
                pltpu.roll(value, PITCH - 1, 0)
                + pltpu.roll(value, 96, 1)
                + pltpu.roll(pltpu.roll(value, 1, 0), 64, 1)
            )
            dr_ref[pl.ds(pl.multiple_of(p + PITCH * r, PITCH), PITCH), :] = value
            turned = jnp.transpose(value)
            for n in range(4):
                plane_ref[n, pl.ds(8 * i + r, 1), :] = turned[9 + 2 * n : 10 + 2 * n, LEFT : LEFT + COLS]
        return carry
    lax.fori_loop(0, ROWS // 8, back_rest, 0)

    def back_main(i, carry):
        p = pl.multiple_of(i * 8 * PITCH, 8 * PITCH)
        total = None
        for dy in range(3):
            at = p + PITCH * (2 - dy)
            for dx in range(3):
                term = nn(sh[2 - dx, pl.ds(at, 8 * PITCH), :], w_ref[3 * dy + dx])
                total = term if total is None else total + term
        dm_ref[pl.ds(p, 8 * PITCH), :] = total.astype(BF)
        return carry
    lax.fori_loop(0, ROWS // 8, back_main, 0)

    def clear(i, carry):
        bs[i] = jnp.zeros((15, COLS, 128), BF)
        bs[i + 32] = jnp.zeros((15, COLS, 128), BF)
        return carry
    lax.fori_loop(0, 8, clear, 0)
    lane = lane[:COLS]
    ahead = lane - lax.broadcasted_iota(jnp.int32, (COLS, 128), 0)

    def row(i):
        at = pl.ds(pl.multiple_of(i * PITCH + LEFT, 16), COLS)
        halves = [pltpu.roll(dm_ref[at, 128 * h : 128 * h + 128].astype(F32), 1, 1) for h in range(2)]
        rest = dr_ref[at, :].astype(BF).astype(F32)

        def band(source, t, first, last, far=None):
            shift = (-t) % 128
            extra = shift % 8
            block = pltpu.roll(source, shift - extra, 1, stride=1, stride_axis=0)
            offset = (ahead + extra) & 127
            here = (offset >= first) & (offset <= last)
            if far is not None:
                here = here | (offset == far)
            block = jnp.where(here, block, 0.0)
            return pltpu.roll(block, extra, 1) if extra else block
        bs[i + 8, 0:3] = jnp.zeros((3, COLS, 128), BF)
        bs[i + 8, 12:15] = jnp.zeros((3, COLS, 128), BF)
        for dy in range(4):
            bs[i + 8, dy + 3] = band(halves[dy // 2], 64 * (dy % 2) + 56, 0, 8).astype(BF)
        for a in range(4):
            value = band(halves[a // 2], 64 * (a % 2) + 48, 2, 7) + band(rest, 2 * a, 0, 1, 8)
            bs[i + 8, a + 7] = value.astype(BF)
        bs[i + 8, 11] = band(rest, 16, 0, 8).astype(BF)
    def three_rows(step, carry):
        for u in range(3):
            row(3 * step + u)
        return carry
    lax.fori_loop(0, ROWS // 3, three_rows, 0)

    def to_first(g, carry):
        i = 4 * g
        left = jnp.concatenate(
            [jnp.concatenate([bs[i + 8 + r, t - r + 3] for t in range(12)], axis=1) for r in range(4)], axis=0
        )
        total = nn(left, ws[pl.ds(i, 12)].reshape(12 * 128, 256)) * (1.0 / CH**0.5)
        for r in range(4):
            at = pl.ds(pl.multiple_of((i + r) * PITCH + LEFT, 16), COLS)
            gs[i + r] = total[COLS * r : COLS * r + COLS] + dm_ref[at, :].astype(F32)
        return carry
    lax.fori_loop(0, ROWS // 4, to_first, 0)

    def to_warped(g, carry):
        t = 4 * g
        left = jnp.concatenate(
            [jnp.concatenate([bs[t + m, 11 - m + n] for n in range(4)], axis=1) for m in range(12)], axis=0
        )
        right = fs[pl.ds(t, 12)].reshape(12 * COLS, 256)
        total = lax.dot_general(left, right, (((0,), (0,)), ((), ())), preferred_element_type=F32)
        gw[pl.ds(t, 4)] = (total * (1.0 / CH**0.5)).reshape(4, 128, 256)
        return carry
    lax.fori_loop(0, 8, to_warped, 0)

    def put(start, size, one, two):
        for z in range(4):
            h, odd = divmod(z, 2)
            a = one[:, 128 * h : 128 * h + 128]
            b = two[:, 128 * h : 128 * h + 128]
            if odd:
                a = pltpu.roll(a, 64, 1)
            else:
                b = pltpu.roll(b, 64, 1)
            low = lax.broadcasted_iota(jnp.int32, (size, 128), 1) < 64
            o_ref[(z - place_ref[0]) & 3, pl.ds(start, size), :] = jnp.where(low, a, b).astype(BF)

    def send_first(step, carry):
        for i in (3 * step, 3 * step + 1, 3 * step + 2):
            put(pl.multiple_of(i * COLS, COLS), COLS, gs[i], gs[i + 12])
        return carry
    lax.fori_loop(0, 4, send_first, 0)

    def send_warped(step, carry):
        for i in (4 * step, 4 * step + 1, 4 * step + 2, 4 * step + 3):
            put(pl.multiple_of(12 * COLS + i * WIN, 16), WIN, gw[i, 0:WIN], gw[i + 16, 0:WIN])
        return carry
    lax.fori_loop(0, 4, send_warped, 0)
    copies = [pltpu.make_async_copy(o_ref.at[s], out, sems.at[s]) for s, out in enumerate((o0, o1, o2, o3))]
    for copy in copies:
        copy.start()
    for copy in copies:
        copy.wait()


def cost_back(place, rx, slopes, weight, weight_rest):
    vm = pl.BlockSpec(memory_space=pltpu.VMEM)
    hbm = pl.BlockSpec(memory_space=pl.ANY)
    size = ROWS * PITCH
    return pl.pallas_call(
        cost_back_kernel,
        out_shape=(jax.ShapeDtypeStruct((PAY, 128), BF),) * 4 + (jax.ShapeDtypeStruct((4, ROWS, COLS), F32),),
        in_specs=[pl.BlockSpec(memory_space=pltpu.SMEM), vm, hbm, hbm, vm],
        out_specs=(hbm,) * 4 + (vm,),
        scratch_shapes=[
            pltpu.VMEM((4, PAY, 128), BF),
            pltpu.VMEM((size, 128), F32),
            pltpu.VMEM((size, 256), BF),
            pltpu.VMEM((8 * PITCH, 128), F32),
            pltpu.VMEM((ROWS + 16, COLS, 256), BF),
            pltpu.VMEM((ROWS + 8, 128, 256), BF),
            pltpu.VMEM((ROWS + 16, 15, COLS, 128), BF),
            pltpu.VMEM((ROWS, COLS, 256), F32),
            pltpu.VMEM((ROWS + 8, 128, 256), F32),
            pltpu.VMEM((3, (ROWS + 2) * PITCH, 512), BF),
            pltpu.VMEM((9, 512, 256), BF),
            pltpu.SemaphoreType.DMA((4,)),
        ],
        compiler_params=pltpu.CompilerParams(vmem_limit_bytes=VMEM_MB * 2**20),
        name="cost_back",
    )(place, rx, slopes, weight, weight_rest)


def turn_kernel(place_ref, r0, r1, r2, r3, g1_ref, gw_ref, up_ref, down_ref, turn, both):
    eye = jnp.where(
        lax.broadcasted_iota(jnp.int32, (128, 128), 0) == lax.broadcasted_iota(jnp.int32, (128, 128), 1), 1.0, 0.0
    ).astype(BF)
    sources = [
        (ref, pl.multiple_of(((place_ref[0] - s) & 3) * COLS, COLS)) for s, ref in enumerate((r0, r1, r2, r3))
    ]

    def first(i, carry):
        at = pl.ds(pl.multiple_of(i * COLS, COLS), COLS)
        for ref, column in sources:
            both[pl.ds(column, COLS), :] = ref[at, :]
        value = nt(eye, both[...])
        g1_ref[i] = value[0:SLOT]
        g1_ref[i + 12] = value[SLOT:]
        return carry
    lax.fori_loop(0, 12, first, 0)

    def second(i, carry):
        at = pl.ds(pl.multiple_of(12 * COLS + i * WIN, 16), WIN)
        turn[...] = jnp.zeros(turn.shape, F32)
        for ref, column in sources:
            rows = pl.ds(pl.multiple_of(column + 8, 8), WIN)
            turn[rows, :] = turn[rows, :] + ref[at, :].astype(F32)
        value = jnp.transpose(turn[12:268, :])
        gw_ref[i] = value[0:SLOT]
        gw_ref[i + 16] = value[SLOT:]
        return carry
    lax.fori_loop(0, 16, second, 0)
    up_ref[...] = gw_ref[0:4].astype(BF)
    down_ref[...] = gw_ref[27:32].astype(BF)


def turn(place, parts):
    vm = pl.BlockSpec(memory_space=pltpu.VMEM)
    return pl.pallas_call(
        turn_kernel,
        out_shape=(
            jax.ShapeDtypeStruct((ROWS, SLOT, 256), F32),
            jax.ShapeDtypeStruct((ROWS + 8, SLOT, 256), F32),
            jax.ShapeDtypeStruct((4, SLOT, 256), BF),
            jax.ShapeDtypeStruct((5, SLOT, 256), BF),
        ),
        in_specs=[pl.BlockSpec(memory_space=pltpu.SMEM)] + [vm] * 4,
        out_specs=(vm,) * 4,
        scratch_shapes=[pltpu.VMEM((288, 128), F32), pltpu.VMEM((256, 128), BF)],
        compiler_params=pltpu.CompilerParams(vmem_limit_bytes=32 * 2**20),
        name="turn",
    )(place, *parts)


def warp_back_kernel(gw_ref, from_above, from_below, f2_ref, above_ref, below_ref, g2_ref, gf_ref, full, band):
    first = lax.broadcasted_iota(jnp.int32, (SLOT, 256), 1) == 0
    last = lax.broadcasted_iota(jnp.int32, (SLOT, 256), 1) == 255
    channel = lax.broadcasted_iota(jnp.int32, (SLOT, 256), 0) < CH // 4
    band[0] = above_ref[3]
    band[1 : ROWS + 1] = f2_ref[...]
    band[ROWS + 1] = below_ref[0]
    full[...] = gw_ref[3:28]
    full[0:5] = full[0:5] + from_above[...].astype(F32)
    full[21:25] = full[21:25] + from_below[...].astype(F32)

    def spread(u, x):
        part = u * x
        return (x - part) + jnp.where(first, 0.0, pltpu.roll(part, 1, 1))

    def row(r, carry):
        upper = band[r + 1].astype(F32)
        lower = band[r + 2].astype(F32)
        before = band[r].astype(F32)
        u, v = upper[49:50], upper[50:51]
        grad = full[r + 1]
        g2_ref[r] = spread(u, (1.0 - v) * grad) + spread(before[49:50], before[50:51] * full[r])
        upper_next = jnp.where(last, 0.0, pltpu.roll(upper, 255, 1))
        lower_next = jnp.where(last, 0.0, pltpu.roll(lower, 255, 1))
        to_u = (1.0 - v) * (upper_next - upper) + v * (lower_next - lower)
        to_v = ((1.0 - u) * lower + u * lower_next) - ((1.0 - u) * upper + u * upper_next)
        along = jnp.sum(jnp.where(channel, grad * to_u, 0.0), axis=0, keepdims=True)
        down = jnp.sum(jnp.where(channel, grad * to_v, 0.0), axis=0, keepdims=True)
        gf_ref[r] = jnp.concatenate([along, down, jnp.zeros((6, 256), F32)], axis=0)
        return carry
    lax.fori_loop(0, ROWS, row, 0)


def warp_back(gw, from_above, from_below, f2, above, below):
    vm = pl.BlockSpec(memory_space=pltpu.VMEM)
    return pl.pallas_call(
        warp_back_kernel,
        out_shape=(
            jax.ShapeDtypeStruct((ROWS, SLOT, 256), F32),
            jax.ShapeDtypeStruct((ROWS, 8, 256), F32),
        ),
        in_specs=[vm] * 6,
        out_specs=(vm, vm),
        scratch_shapes=[pltpu.VMEM((ROWS + 1, SLOT, 256), F32), pltpu.VMEM((ROWS + 2, SLOT, 256), BF)],
        compiler_params=pltpu.CompilerParams(vmem_limit_bytes=32 * 2**20),
        name="warp_back",
    )(gw, from_above, from_below, f2, above, below)
WIDE, REST = lane_maps()
GATHER = gather_map()
PLANES = plane_map()

PIX = ("xy", "core")


def ring(axis, steps):
    count = lax.axis_size(axis)
    return [(i, i + steps) for i in range(max(0, -steps), min(count, count - steps))]


def around(value, step):
    return lax.ppermute(value, "chan", [(i, (i + step) % 4) for i in range(4)])


def local(
    feat_one, feat_two, up_flow, up_feat, target_flow, valid_mask,
    conv_one, conv_two, conv_three, conv_four, conv_five, flow_head,
    bias_one, bias_two, bias_three, bias_four, bias_five, bias_head,
):
    convs = [conv_one, conv_two, conv_three, conv_four, conv_five, flow_head]
    biases = [bias_one, bias_two, bias_three, bias_four, bias_five, bias_head]
    channels = feat_one.shape[0]
    place = lax.axis_index("chan")
    f2 = jnp.concatenate([feat_two, up_flow, jnp.zeros((SLOT - channels - 2, ROWS, 256), BF)], axis=0)
    f2 = jnp.transpose(f2, (1, 0, 2))
    above = lax.ppermute(f2[ROWS - MD :], PIX, ring(PIX, 1))
    below = lax.ppermute(f2[: MD + 1], PIX, ring(PIX, -1))
    f1 = jnp.transpose(jnp.pad(feat_one, ((0, SLOT - channels), (0, 0), (0, 0))), (1, 0, 2))
    packed = pack_warped(f2, above, below, pack_first(f1))
    packed, biases = lax.optimization_barrier((packed, biases))
    features = lax.all_to_all(packed, "chan", split_axis=0, concat_axis=0, tiled=True)
    features, *weights = lax.optimization_barrier((features, *arrange(convs, biases)))

    flow_cols = lax.dynamic_slice_in_dim(up_flow, place * COLS, COLS, 2)
    high = target_flow.astype(BF)
    low = (target_flow - high.astype(F32)).astype(BF)
    one = jnp.ones((2, ROWS, COLS), BF)
    planes = jnp.concatenate([flow_cols, up_feat, one, valid_mask.astype(BF)[None], high, low], axis=0)
    extra = lax.dot_general(
        planes, jnp.asarray(PLANES, BF), (((0,), (0,)), ((), ())), preferred_element_type=F32
    ).astype(BF)
    upper, lower = cost_volume(features, extra)
    top = lax.ppermute(lower, PIX, ring(PIX, 1))
    bottom = lax.ppermute(upper, PIX, ring(PIX, -1))
    tiles = [tile.reshape(27, COLS, 128) for tile in (top, upper, lower, bottom)]
    left = lax.ppermute(
        jnp.concatenate([tile[:, COLS - LEFT :] for tile in tiles], axis=0), "chan", ring("chan", 1)
    )
    right = lax.ppermute(
        jnp.concatenate([tile[:, :LEFT] for tile in tiles], axis=0), "chan", ring("chan", -1)
    )
    acts, slopes, main, rest, flow_out, sums = decode(
        top, upper, lower, bottom, left, right, *weights
    )
    core = lax.axis_index("core").astype(jnp.int32)[None]
    own, sent = wgrad(core, slopes, main, rest, acts, jnp.asarray(GATHER, BF))
    parts = chip_parts(own, sent, jnp.sum(sums[:, :, 96], axis=1))
    parts, slopes = lax.optimization_barrier((parts, slopes))
    parts = lax.all_to_all(parts, CHIPS, split_axis=0, concat_axis=0, tiled=True)
    here = place.astype(jnp.int32)[None]
    *payload, small = cost_back(here, features, slopes, weights[0], weights[2])
    returned = [payload[0]] + [around(payload[step], step) for step in range(1, 4)]
    parts, _ = lax.optimization_barrier((parts, payload[0]))
    spread, notes = spread_total(parts)
    spread, *returned = lax.optimization_barrier((spread, *returned))
    mine = lax.all_to_all(spread, CHIPS, split_axis=0, concat_axis=0, tiled=True).reshape(HALF_ROWS, 128)
    grad_one, partial, to_above, to_below = turn(here, returned)
    from_above = lax.ppermute(to_below, PIX, ring(PIX, 1))
    from_below = lax.ppermute(to_above, PIX, ring(PIX, -1))
    grad_two, grad_flow = warp_back(partial, from_above, from_below, f2, above, below)
    grad_feat_one = jnp.transpose(grad_one[:, :channels], (1, 0, 2))
    grad_feat_two = jnp.transpose(grad_two[:, :channels], (1, 0, 2))
    flow_parts = jnp.transpose(grad_flow[:, :2], (1, 0, 2))
    total = lax.dynamic_slice_in_dim(flow_parts, place * COLS, COLS, 2)
    flow_parts = flow_parts.astype(BF)
    for step in range(1, 4):
        sent = lax.dynamic_slice_in_dim(flow_parts, lax.rem(place + step, 4) * COLS, COLS, 2)
        total = total + lax.ppermute(sent, "chan", [(i, (i + step) % 4) for i in range(4)]).astype(F32)

    grad_up_flow = total + small[:2]
    mine, *outputs = lax.optimization_barrier(
        (mine, flow_out, grad_feat_one, grad_feat_two, grad_up_flow, small[2:])
    )
    flow_out, grad_feat_one, grad_feat_two, grad_up_flow, grad_up_feat = outputs
    weight_grads, bias_grads = unpack(core, mine, lax.ppermute(mine, "core", SWAP))
    scalars = jnp.sum(notes[:, :3], axis=0)
    return (flow_out, scalars, grad_feat_one, grad_feat_two, grad_up_flow, grad_up_feat, *weight_grads, *bias_grads)


def solution(mesh):
    chan, pix = mesh.devices.shape
    cores = jax.sharding.Mesh(mesh.devices.reshape(chan, pix // 2, 2), ("chan", "xy", "core"))
    return jax.shard_map(
        local,
        mesh=cores,
        in_specs=(
            P("chan", PIX, None),
            P("chan", PIX, None),
            P(None, PIX, None),
            P(None, PIX, "chan"),
            P(None, PIX, "chan"),
            P(PIX, "chan"),
        )
        + (P(),) * 12,
        out_specs=(
            P(None, PIX, "chan"),
            P(),
            P("chan", PIX, None),
            P("chan", PIX, None),
            P(None, PIX, "chan"),
            P(None, PIX, "chan"),
        )
        + (P(),) * 12,
        check_vma=False,
    )
```
